32 devices in a mesh: dp: 8 (over y, x, core), mp: 4 (over z).
Axes of the slice: x: 2, y: 2, z: 4, core: 2. Of those that a mesh axis runs over, the one named last changes fastest.
Arguments:
- tokens: bfloat16 [16, 1024, 1024], P('dp'), may hold values from -6 to 6
- memory: bfloat16 [16, 1024, 1024], P('dp'), may hold values from -6 to 6
- target_lengths: int32 [16], P('dp'), may hold values from 128 to 1024, as said below
- source_lengths: int32 [16], P('dp'), may hold values from 128 to 1024, as said below
- cotangent: bfloat16 [16, 1024, 1024], P('dp'), may hold values from -6 to 6
- norm_gain: bfloat16 [3, 1024], replicated, may hold values from 0.5 to 1.5
- norm_bias: bfloat16 [3, 1024], replicated, may hold values from -1 to 1
- self_in: bfloat16 [3, 1024, 1024], P(None, None, 'mp'), may hold values from -0.1875 to 0.1875
- self_in_bias: bfloat16 [2, 1024], P(None, 'mp'), may hold values from -1 to 1
- self_out: bfloat16 [1024, 1024], P('mp'), may hold values from -1.5 to 1.5
- cross_query: bfloat16 [1024, 1024], P(None, 'mp'), may hold values from -0.1875 to 0.1875
- cross_kv: bfloat16 [2, 1024, 1024], P(None, None, 'mp'), may hold values from -0.1875 to 0.1875
- cross_bias: bfloat16 [2, 1024], P(None, 'mp'), may hold values from -1 to 1
- cross_out: bfloat16 [1024, 1024], P('mp'), may hold values from -1.5 to 1.5
- out_bias: bfloat16 [3, 1024], replicated, may hold values from -1 to 1
- ffn_up: bfloat16 [1024, 4096], P(None, 'mp'), may hold values from -0.1875 to 0.1875
- ffn_up_bias: bfloat16 [4096], P('mp'), may hold values from -1 to 1
- ffn_down: bfloat16 [4096, 1024], P('mp'), may hold values from -0.09375 to 0.09375
Outputs:
- output: bfloat16 [16, 1024, 1024], P('dp')
- tokens_grad: float32 [16, 1024, 1024], P('dp')
- memory_grad: float32 [16, 1024, 1024], P('dp')
- norm_gain_grad: float32 [3, 1024], replicated
- norm_bias_grad: float32 [3, 1024], replicated
- self_in_grad: float32 [3, 1024, 1024], P(None, None, 'mp')
- self_in_bias_grad: float32 [2, 1024], P(None, 'mp')
- self_out_grad: float32 [1024, 1024], P('mp')
- cross_query_grad: float32 [1024, 1024], P(None, 'mp')
- cross_kv_grad: float32 [2, 1024, 1024], P(None, None, 'mp')
- cross_bias_grad: float32 [2, 1024], P(None, 'mp')
- cross_out_grad: float32 [1024, 1024], P('mp')
- out_bias_grad: float32 [3, 1024], replicated
- ffn_up_grad: float32 [1024, 4096], P(None, 'mp')
- ffn_up_bias_grad: float32 [4096], P('mp')
- ffn_down_grad: float32 [4096, 1024], P('mp')
The draws below stay inside these ranges and needn't reach their ends.
Inputs may be any that keep to these rules, and one draw needn't show every extreme that they name: `target_lengths`: one row has exactly 1024. `source_lengths`: one row has exactly 1024.
All inputs are finite; a program needn't handle non-finite values.
Results may differ from the reference program's by a relative error of at most 0.024.
Values may be sent and summed in bfloat16 or wider, within the bound.
No kernel may reach another device: no remote copies, remote signals or barrier semaphores. Data moves between devices by JAX's collectives and lax.ppermute only.
A program may use at most 320 MiB of HBM per device.

```python
import jax
import jax.numpy as jnp
from jax import lax

D = 1024
HEAD_DIM = 64
FF = 4096
TLEN = 1024
SLEN = 1024
ROWS = 16


def ragged(key, count, longest):
    lengths = jax.random.randint(jax.random.fold_in(key, 1), (count,), longest // 8, longest + 1)
    chosen = jax.random.randint(jax.random.fold_in(key, 2), (), 0, count)
    return jnp.where(jnp.arange(count) == chosen, longest, lengths).astype(jnp.int32)


def draw_target_lengths(key, part):
    key = jax.random.fold_in(key, 11)
    return ragged(key, ROWS, TLEN)


def draw_source_lengths(key, part):
    key = jax.random.fold_in(key, 23)
    return ragged(key, ROWS, SLEN)


def block_scale(stream_key, shape, split, least, top_value):
    level = 1.0
    for dim, parts in split:
        steps = jax.random.uniform(jax.random.fold_in(jax.random.fold_in(stream_key, 6), dim), (parts,), jnp.float32, least / len(split), top_value / len(split))
        level = level * jnp.repeat(jnp.exp(steps), shape[dim] // parts).reshape((-1,) + (1,) * (len(shape) - 1 - dim))
    return level


def normal_values(own_key, dims, deviation, reach, cuts=(), kind=jnp.bfloat16):
    loudness = block_scale(own_key, dims, cuts, -0.22, 0.18) if cuts else 1.0
    values = jax.random.normal(own_key, dims, jnp.float32) * deviation * loudness
    return jnp.minimum(jnp.maximum(values, -reach), reach).astype(kind)


def setup_inputs(seed: int = 0) -> dict:
    arg_keys = jax.random.split(jax.random.key(seed), 19)
    return {
        "tokens": normal_values(arg_keys[0], (ROWS, TLEN, D), 1.0, 6.0, ((0, 8),)),
        "memory": normal_values(arg_keys[1], (ROWS, SLEN, D), 1.0, 6.0, ((0, 8),)),
        "target_lengths": draw_target_lengths(jax.random.fold_in(arg_keys[18], 71), 0),
        "source_lengths": draw_source_lengths(jax.random.fold_in(arg_keys[18], 71), 0),
        "cotangent": normal_values(arg_keys[4], (ROWS, TLEN, D), 1.0, 6.0, ((0, 8),)),
        "norm_gain": jnp.clip(1.0 + 0.1 * jax.random.normal(arg_keys[5], (3, D), jnp.float32), 0.5, 1.5).astype(jnp.bfloat16),
        "norm_bias": normal_values(arg_keys[6], (3, D), 0.2, 1.0),
        "self_in": normal_values(arg_keys[7], (3, D, D), D ** -0.5, 0.1875, ((2, 4),)),
        "self_in_bias": normal_values(arg_keys[8], (2, D), 0.2, 1.0, ((1, 4),)),
        "self_out": normal_values(arg_keys[9], (D, D), (D // 64) ** -0.5, 1.5, ((0, 4),)),
        "cross_query": normal_values(arg_keys[10], (D, D), D ** -0.5, 0.1875, ((1, 4),)),
        "cross_kv": normal_values(arg_keys[11], (2, D, D), D ** -0.5, 0.1875, ((2, 4),)),
        "cross_bias": normal_values(arg_keys[12], (2, D), 0.2, 1.0, ((1, 4),)),
        "cross_out": normal_values(arg_keys[13], (D, D), (D // 64) ** -0.5, 1.5, ((0, 4),)),
        "out_bias": normal_values(arg_keys[14], (3, D), 0.2, 1.0),
        "ffn_up": normal_values(arg_keys[15], (D, FF), D ** -0.5, 0.1875, ((1, 4),)),
        "ffn_up_bias": normal_values(arg_keys[16], (FF,), 0.2, 1.0, ((0, 4),)),
        "ffn_down": normal_values(arg_keys[17], (FF, D), FF ** -0.5, 0.09375, ((0, 4),)),
    }


highest = lax.Precision.HIGHEST
neg_fill = -1000000000.0
eps_norm = 1e-05

@jax.custom_vjp
def low(v):
    return lax.optimization_barrier(v.astype(jnp.bfloat16)).astype(jnp.float32)

@jax.custom_vjp
def low_back(v):
    return v

def low_keep(v):
    return (low(v), None)

def low_pass(kept, grad):
    return (grad,)

def back_keep(v):
    return (v, None)

def back_low(kept, grad):
    return (low(grad),)
low.defvjp(low_keep, low_pass)
low_back.defvjp(back_keep, back_low)

def matmul(left, right):
    return jnp.dot(left, right, precision=highest)

def norm_layer(values, gain, shift):
    centre = lax.optimization_barrier(jnp.mean(values, axis=-1, keepdims=True))
    offset = values - centre
    spread = lax.optimization_barrier(jnp.mean(offset * offset, axis=-1, keepdims=True))
    return offset * lax.rsqrt(spread + eps_norm) * gain + shift

def attend(query, keys, values, allowed):
    query_heads = query.reshape(query.shape[0], -1, HEAD_DIM)
    key_heads = keys.reshape(keys.shape[0], -1, HEAD_DIM)
    value_heads = values.reshape(values.shape[0], -1, HEAD_DIM)
    scores = jnp.einsum('qhe,khe->hqk', query_heads, key_heads, precision=highest) * HEAD_DIM ** (-0.5)
    scores = jnp.where(allowed[None], low_back(scores), neg_fill)
    probs = low(jax.nn.softmax(scores, axis=-1))
    mixed = jnp.einsum('hqk,khe->qhe', probs, value_heads, precision=highest)
    return low_back(low(mixed.reshape(mixed.shape[0], -1)))

def layer(params, tokens_row, memory_row, target_len, source_len):
    norm_gain, norm_bias, self_in, self_in_bias, self_out, cross_query, cross_kv, cross_bias, cross_out, out_bias, ffn_up, ffn_up_bias, ffn_down = params
    places = jnp.arange(TLEN, dtype=jnp.int32)
    source_places = jnp.arange(SLEN, dtype=jnp.int32)
    causal = (places[None, :] <= places[:, None]) & (places[None, :] < target_len)
    crossing = jnp.broadcast_to(source_places[None, :] < source_len, (TLEN, SLEN))
    normed = low(norm_layer(tokens_row, norm_gain[0], norm_bias[0]))
    query = low_back(low(matmul(normed, self_in[0]) + self_in_bias[0]))
    keys = low_back(low(matmul(normed, self_in[1])))
    values = low_back(low(matmul(normed, self_in[2]) + self_in_bias[1]))
    mixed = attend(query, keys, values, causal)
    first = tokens_row + low_back(matmul(mixed, self_out) + out_bias[0])
    normed = low(norm_layer(first, norm_gain[1], norm_bias[1]))
    query = low_back(low(matmul(normed, cross_query) + cross_bias[0]))
    keys = low_back(low(matmul(memory_row, cross_kv[0])))
    values = low_back(low(matmul(memory_row, cross_kv[1]) + cross_bias[1]))
    mixed = attend(query, keys, values, crossing)
    second = first + low_back(matmul(mixed, cross_out) + out_bias[1])
    normed = low(norm_layer(second, norm_gain[2], norm_bias[2]))
    hidden_pre = low_back(matmul(normed, ffn_up) + ffn_up_bias)
    hidden = low(jax.nn.gelu(hidden_pre, approximate=True))
    return second + low_back(matmul(hidden, ffn_down) + out_bias[2])

def reference(tokens, memory, target_lengths, source_lengths, cotangent, norm_gain, norm_bias, self_in, self_in_bias, self_out, cross_query, cross_kv, cross_bias, cross_out, out_bias, ffn_up, ffn_up_bias, ffn_down):
    params = (norm_gain.astype(jnp.float32), norm_bias.astype(jnp.float32), self_in.astype(jnp.float32), self_in_bias.astype(jnp.float32), self_out.astype(jnp.float32), cross_query.astype(jnp.float32), cross_kv.astype(jnp.float32), cross_bias.astype(jnp.float32), cross_out.astype(jnp.float32), out_bias.astype(jnp.float32), ffn_up.astype(jnp.float32), ffn_up_bias.astype(jnp.float32), ffn_down.astype(jnp.float32))

    def row_step(totals, row):
        tokens_row, memory_row, target_len, source_len, cot_row = row

        def apply(params_in, tokens_in, memory_in):
            return layer(params_in, tokens_in, memory_in, target_len, source_len)
        result, pullback = jax.vjp(apply, params, tokens_row.astype(jnp.float32), memory_row.astype(jnp.float32))
        grads, tokens_grad, memory_grad = pullback(cot_row.astype(jnp.float32))
        totals = jax.tree.map(jnp.add, totals, grads)
        return (totals, (result.astype(jnp.bfloat16), tokens_grad, memory_grad))
    zeros = jax.tree.map(jnp.zeros_like, params)
    totals, (output, tokens_grad, memory_grad) = lax.scan(row_step, zeros, (tokens, memory, target_lengths, source_lengths, cotangent))
    return (output, tokens_grad, memory_grad, totals[0], totals[1], totals[2], totals[3], totals[4], totals[5], totals[6], totals[7], totals[8], totals[9], totals[10], totals[11], totals[12])
```

```python
import functools

import jax
import jax.numpy as jnp
from jax import lax
from jax.experimental import pallas as pl
from jax.experimental.pallas import tpu as pltpu
from jax.sharding import PartitionSpec as P

neg_fill = -1000000000.0
open_cap = 3e38
eps_norm = 1e-05
PAIR = 128
HALF = 64
QUERY_SCALE = 0.125
f32 = jnp.float32
bf16 = jnp.bfloat16


def low(value):
    return value.astype(bf16)


def nn(left, right):
    return lax.dot_general(left, right, (((1,), (0,)), ((), ())), preferred_element_type=f32)


def nt(left, right):
    return lax.dot_general(left, right, (((1,), (1,)), ((), ())), preferred_element_type=f32)


def tn(left, right):
    return lax.dot_general(left, right, (((0,), (0,)), ((), ())), preferred_element_type=f32)


def after(value, *others):
    return lax.optimization_barrier((value,) + others)[0]


def norm_stats(values):
    centre = jnp.mean(values, axis=-1, keepdims=True)
    offset = values - centre
    spread = jnp.mean(offset * offset, axis=-1, keepdims=True)
    scale = lax.rsqrt(spread + eps_norm)
    return offset * scale, scale


def norm_forward(values, gain, shift):
    hat, scale = norm_stats(values)
    return low(hat * gain + shift)


def norm_backward(values, gain, grad):
    hat, scale = norm_stats(values)
    scaled = grad * gain
    mean_one = jnp.mean(scaled, axis=-1, keepdims=True)
    mean_two = jnp.mean(scaled * hat, axis=-1, keepdims=True)
    back = scale * (scaled - mean_one - hat * mean_two)
    return back, jnp.sum(grad * hat, axis=0), jnp.sum(grad, axis=0)


def head_halves(both):
    lane = lax.broadcasted_iota(jnp.int32, both.shape, 1)
    zero = jnp.zeros_like(both)
    return jnp.where(lane < HALF, both, zero), jnp.where(lane < HALF, zero, both)


def fill_caps(info, cap_ref, block, causal):
    length = cap_ref.shape[0]
    for t in range(2):
        keys = lax.broadcasted_iota(jnp.int32, (length, block), 0)
        allowed = keys < info[0]
        if causal:
            places = lax.broadcasted_iota(jnp.int32, (length, block), 1) + info[1 + t] * block
            allowed = allowed & (keys <= places)
        cap_ref[:, t * block : (t + 1) * block] = jnp.where(allowed, open_cap, neg_fill)


def forward_kernel(info, q_ref, k_ref, v_ref, o_ref, lse_ref, cap_ref, s_ref, *, block, causal, chunk):
    length = k_ref.shape[0]

    @pl.when(pl.program_id(0) == 0)
    def _():
        fill_caps(info, cap_ref, block, causal)

    for t in (1, 0):
        rows = slice(t * block, (t + 1) * block)
        span = length // 2 if (causal and t == 0) else length
        queries = jnp.concatenate(head_halves(q_ref[rows, :] * bf16(QUERY_SCALE)), axis=0)
        most = jnp.full((8, 2 * block), -open_cap, f32)
        for c in range(0, span, chunk):
            keys = slice(c, c + chunk)
            cap = cap_ref[keys, rows]
            scores = jnp.minimum(nt(k_ref[keys, :], queries), jnp.concatenate([cap, cap], axis=1))
            s_ref[t, keys, :] = scores
            most = jnp.maximum(most, jnp.max(scores.reshape(chunk // 8, 8, 2 * block), axis=0))
        most = jnp.max(most, axis=0, keepdims=True)
        total = jnp.zeros((8, 2 * block), f32)
        mixed = jnp.zeros((PAIR, 2 * block), f32)
        for c in range(0, span, chunk):
            keys = slice(c, c + chunk)
            weights = jnp.exp(s_ref[t, keys, :] - most)
            total = total + jnp.sum(weights.reshape(chunk // 8, 8, 2 * block), axis=0)
            mixed = mixed + tn(v_ref[keys, :], low(weights))
        total = jnp.sum(total, axis=0, keepdims=True)
        mixed = mixed / total
        sub = lax.broadcasted_iota(jnp.int32, (PAIR, block), 0)
        o_ref[rows, :] = low(jnp.where(sub < HALF, mixed[:, :block], mixed[:, block:]).T)
        lse = most + jnp.log(total)
        lse_ref[0, 0:1, rows] = lse[:, :block]
        lse_ref[0, 1:2, rows] = lse[:, block:]


def backward_kernel(
    info, q_ref, k_ref, v_ref, o_ref, g_ref, lse_ref, dq_ref, dk_ref, dv_ref, cap_ref, dk_acc, dv_acc,
    *, block, causal, chunk
):
    length = k_ref.shape[0]

    @pl.when(pl.program_id(0) == 0)
    def _():
        fill_caps(info, cap_ref, block, causal)

    for t in (1, 0):
        rows = slice(t * block, (t + 1) * block)
        span = length // 2 if (causal and t == 0) else length
        grads = g_ref[rows, :]
        prod = (grads.astype(f32) * o_ref[rows, :].astype(f32)).T
        centre = jnp.concatenate(
            [jnp.sum(prod[:HALF], axis=0, keepdims=True), jnp.sum(prod[HALF:], axis=0, keepdims=True)], axis=1
        )
        lse = jnp.concatenate([lse_ref[0, 0:1, rows], lse_ref[0, 1:2, rows]], axis=1)
        queries = jnp.concatenate(head_halves(q_ref[rows, :] * bf16(QUERY_SCALE)), axis=0)
        grads = jnp.concatenate(head_halves(grads), axis=0)
        dq = jnp.zeros((PAIR, 2 * block), f32)
        for c in range(0, span, chunk):
            keys = slice(c, c + chunk)
            k, v = k_ref[keys, :], v_ref[keys, :]
            cap = cap_ref[keys, rows]
            scores = jnp.minimum(nt(k, queries), jnp.concatenate([cap, cap], axis=1))
            probs = jnp.exp(scores - lse)
            grad_scores = low(probs * (nt(v, grads) - centre))
            dv = nn(low(probs), grads)
            dk = nn(grad_scores, queries)
            dq = dq + tn(k, grad_scores)
            if t == 1:
                dk_acc[keys, :] = dk
                dv_acc[keys, :] = dv
            else:
                dk_acc[keys, :] += dk
                dv_acc[keys, :] += dv
        sub = lax.broadcasted_iota(jnp.int32, (PAIR, block), 0)
        dq = jnp.where(sub < HALF, dq[:, :block], dq[:, block:]) * QUERY_SCALE
        dq_ref[rows, :] = low(dq.T)
    dk_ref[...] = low(dk_acc[...])
    dv_ref[...] = low(dv_acc[...])


def attention_specs(queries, length):
    one = pl.BlockSpec((queries, PAIR), lambda i, *_: (0, i))
    key = pl.BlockSpec((length, PAIR), lambda i, *_: (0, i))
    lse = pl.BlockSpec((1, 8, queries), lambda i, *_: (i, 0, 0))
    return one, key, lse


def attend_forward(info, query, keys, values, causal):
    queries, width = query.shape
    length = keys.shape[0]
    one, key, lse = attention_specs(queries, length)
    pairs = width // PAIR
    return pl.pallas_call(
        functools.partial(forward_kernel, block=queries // 2, causal=causal, chunk=min(256, length // 2)),
        out_shape=(
            jax.ShapeDtypeStruct((queries, width), bf16),
            jax.ShapeDtypeStruct((pairs, 8, queries), f32),
        ),
        grid_spec=pltpu.PrefetchScalarGridSpec(
            num_scalar_prefetch=1,
            grid=(pairs,),
            in_specs=[one, key, key],
            out_specs=[one, lse],
            scratch_shapes=[pltpu.VMEM((length, queries), f32), pltpu.VMEM((2, length, queries), f32)],
        ),
        compiler_params=pltpu.CompilerParams(vmem_limit_bytes=40 << 20),
        cost_estimate=pl.CostEstimate(
            flops=12 * queries * length * width, bytes_accessed=4 * (queries + length) * width, transcendentals=0
        ),
    )(info, query, keys, values)


def attend_backward(info, query, keys, values, mixed, grad, lse_rows, causal):
    queries, width = query.shape
    length = keys.shape[0]
    one, key, lse = attention_specs(queries, length)
    return pl.pallas_call(
        functools.partial(backward_kernel, block=queries // 2, causal=causal, chunk=min(256, length // 2)),
        out_shape=(
            jax.ShapeDtypeStruct((queries, width), bf16),
            jax.ShapeDtypeStruct((length, width), bf16),
            jax.ShapeDtypeStruct((length, width), bf16),
        ),
        grid_spec=pltpu.PrefetchScalarGridSpec(
            num_scalar_prefetch=1,
            grid=(width // PAIR,),
            in_specs=[one, key, key, one, one, lse],
            out_specs=[one, key, key],
            scratch_shapes=[
                pltpu.VMEM((length, queries), f32),
                pltpu.VMEM((length, PAIR), f32),
                pltpu.VMEM((length, PAIR), f32),
            ],
        ),
        compiler_params=pltpu.CompilerParams(vmem_limit_bytes=40 << 20),
        cost_estimate=pl.CostEstimate(
            flops=20 * queries * length * width, bytes_accessed=4 * (queries + length) * width, transcendentals=0
        ),
    )(info, query, keys, values, mixed, grad, lse_rows)


def place_kernel(where, *refs, count, pieces):
    out_ref = refs[-1]
    step = pl.program_id(0)
    for k in range(count):

        @pl.when(step // pieces == k)
        def _(k=k):
            out_ref[...] = refs[k][...].astype(out_ref.dtype)


def place(where, slots, kind):
    count, pieces = len(slots), where.shape[0] // len(slots)
    rows, width = slots[0].shape
    block = rows // pieces
    return pl.pallas_call(
        functools.partial(place_kernel, count=count, pieces=pieces),
        out_shape=jax.ShapeDtypeStruct((rows * count, width), kind),
        grid_spec=pltpu.PrefetchScalarGridSpec(
            num_scalar_prefetch=1,
            grid=(count * pieces,),
            in_specs=[
                pl.BlockSpec(
                    (block, width),
                    lambda i, where, k=k: (jnp.clip(i - k * pieces, 0, pieces - 1), 0),
                )
                for k in range(count)
            ],
            out_specs=pl.BlockSpec((block, width), lambda i, where: (where[i], 0)),
        ),
        compiler_params=pltpu.CompilerParams(vmem_limit_bytes=40 << 20),
        cost_estimate=pl.CostEstimate(flops=0, bytes_accessed=6 * rows * count * width, transcendentals=0),
    )(where, *slots)


def build(dp_size, mp_size):
    ring = [(i, (i + 1) % mp_size) for i in range(mp_size)]
    back_ring = [(i, (i - 1) % mp_size) for i in range(mp_size)]
    dp_bits = dp_size.bit_length() - 1

    def flip(axis, size, bit):
        return lambda value: lax.ppermute(value, axis, [(i, i ^ (1 << bit)) for i in range(size)])

    def gather_slots(share):
        slots = [share]
        for _ in range(mp_size - 1):
            slots.append(lax.ppermute(slots[-1], "mp", ring))
        return slots

    def reduce_slots(slots):
        total = slots[mp_size - 1]
        for k in range(mp_size - 2, -1, -1):
            total = lax.ppermute(total, "mp", back_ring) + slots[k]
        return total

    def shards(
        tokens,
        memory,
        target_lengths,
        source_lengths,
        cotangent,
        norm_gain,
        norm_bias,
        self_in,
        self_in_bias,
        self_out,
        cross_query,
        cross_kv,
        cross_bias,
        cross_out,
        out_bias,
        ffn_up,
        ffn_up_bias,
        ffn_down,
    ):
        rows, length, width = tokens.shape
        source = memory.shape[1]
        d = lax.axis_index("dp")
        z = lax.axis_index("mp")
        group = mp_size // rows
        row = z // group
        part = z % group
        block = length // (2 * group)
        share = width // dp_size
        own_starts = (part * block, (2 * group - 1 - part) * block)

        def own(values):
            return jnp.concatenate([lax.dynamic_slice_in_dim(values, s, block, 0) for s in own_starts])

        def take_row(values):
            return lax.dynamic_index_in_dim(values, row, 0, keepdims=False)

        def rows_of(weight):
            return lax.dynamic_slice_in_dim(weight, d * share, share, 0)

        def cols_of(weight):
            return lax.dynamic_slice_in_dim(weight, d * share, share, 1).T

        def with_bias(piece, bias):
            extra = jnp.zeros((16, piece.shape[1]), bf16)
            if bias is not None:
                extra = lax.dynamic_update_slice(extra, bias[None], (0, 0))
            return jnp.concatenate([piece, extra])

        def group_slots(pieces, *held):
            cat = jnp.concatenate([with_bias(p, b) for p, b in pieces], axis=1)
            if held:
                cat = after(cat, *held)
            return gather_slots(cat)

        def gather_group(slots, wides, *held):
            starts = [0]
            for w in wides:
                starts.append(starts[-1] + w)
            both = jnp.concatenate(
                [s[:, a:b] for a, b in zip(starts[:-1], starts[1:]) for s in slots], axis=1
            )
            part_to_send = both[:share]
            if held:
                part_to_send = after(part_to_send, *held)
            full = lax.all_gather(part_to_send, "dp", axis=0, tiled=True)
            bias = both[share].astype(f32)
            found = []
            for a, b in zip(starts[:-1], starts[1:]):
                cols = slice(a * mp_size, b * mp_size)
                found.append((full[:, cols], bias[cols]))
            return found

        per = width // mp_size
        hid = ffn_up.shape[1]
        slots_a = group_slots(
            [
                (rows_of(self_in[0]), self_in_bias[0]),
                (rows_of(self_in[1]), None),
                (rows_of(self_in[2]), self_in_bias[1]),
            ]
        )
        slots_b = group_slots(
            [
                (cols_of(self_out), None),
                (rows_of(cross_query), cross_bias[0]),
                (rows_of(cross_kv[0]), None),
                (rows_of(cross_kv[1]), cross_bias[1]),
            ],
            slots_a[-1],
        )
        slots_c = group_slots(
            [(cols_of(cross_out), None), (rows_of(ffn_up), ffn_up_bias), (cols_of(ffn_down), None)],
            slots_b[-1],
        )
        (w_q1, b_q1), (w_k1, _), (w_v1, b_v1) = gather_group(slots_a, [per, per, per])
        (w_o1, _), (w_q2, b_q2), (w_k2, _), (w_v2, b_v2) = gather_group(slots_b, [per, per, per, per])
        (w_o2, _), (w_up, b_up), (w_down, _) = gather_group(slots_c, [per, hid, hid])
        gains, shifts = norm_gain.astype(f32), norm_bias.astype(f32)
        biases = out_bias.astype(f32)

        ends = jnp.stack([part, 2 * group - 1 - part]).astype(jnp.int32)
        target_info = jnp.concatenate([target_lengths[row][None], ends])
        source_info = jnp.concatenate([source_lengths[row][None], ends])
        full_row = take_row(tokens).astype(f32)
        mem_row = take_row(memory)
        resid = own(full_row)
        grad_out_low = own(take_row(cotangent))
        grad_out = grad_out_low.astype(f32)
        h1_row = norm_forward(full_row, gains[0], shifts[0])
        h1 = own(h1_row)
        q1 = low(nn(h1, w_q1) + b_q1)
        k1 = low(nn(h1_row, w_k1))
        v1 = low(nn(h1_row, w_v1) + b_v1)
        o1, lse1 = attend_forward(target_info, q1, k1, v1, True)
        first = resid + nt(o1, w_o1) + biases[0]
        h2 = norm_forward(first, gains[1], shifts[1])
        q2 = low(nn(h2, w_q2) + b_q2)
        k2 = low(nn(mem_row, w_k2))
        v2 = low(nn(mem_row, w_v2) + b_v2)
        o2, lse2 = attend_forward(source_info, q2, k2, v2, False)
        second = first + nt(o2, w_o2) + biases[1]
        h3 = norm_forward(second, gains[2], shifts[2])
        pre = nn(h3, w_up) + b_up
        hidden, pull_gelu = jax.vjp(lambda u: jax.nn.gelu(u, approximate=True), pre)
        hidden = low(hidden)
        final = low(second + nt(hidden, w_down) + biases[2])

        def slot_places():
            found = []
            for k in range(mp_size):
                other = lax.rem(z - k + mp_size, mp_size)
                base = (other // group) * (2 * group)
                found += [base + other % group, base + 2 * group - 1 - other % group]
            return jnp.stack(found).astype(jnp.int32)

        causal_places = slot_places()
        memory_places = jnp.stack([lax.rem(z - k + mp_size, mp_size) for k in range(mp_size)]).astype(jnp.int32)

        bias_three = jnp.sum(grad_out, axis=0)
        grad_down = low(tn(grad_out_low, hidden))
        grad_pre = low(pull_gelu(nn(grad_out_low, w_down))[0])
        grad_up = low(tn(h3, grad_pre))
        up_bias_grad = jnp.sum(grad_pre.astype(f32), axis=0)
        back, gain_three, shift_three = norm_backward(second, gains[2], nt(grad_pre, w_up))
        grad_second = grad_out + back
        e2 = low(grad_second)
        output_slots = gather_slots(final)

        def scatter(grad):
            return lax.psum_scatter(grad, "dp", scatter_dimension=0, tiled=True)

        down_share = scatter(grad_down)
        up_share = scatter(grad_up)

        def bit_of(b):
            return lax.rem(lax.shift_right_logical(d, b), 2)

        def halves_of(act):
            wide = act.reshape(act.shape[0], dp_size // 2, 2, share)
            core = bit_of(0)
            send = lax.dynamic_index_in_dim(wide, 1 - core, 2, keepdims=False)
            keep = lax.dynamic_index_in_dim(wide, core, 2, keepdims=False)
            return send.reshape(act.shape[0], -1), keep.reshape(act.shape[0], -1)

        def halving_sum(pairs):
            split = [(halves_of(act), grad) for act, grad in pairs]
            sent = jnp.concatenate([low(tn(send, grad)) for (send, _), grad in split], axis=1)
            got = flip("dp", dp_size, 0)(sent)
            kept = jnp.concatenate([tn(keep, grad) for (_, keep), grad in split], axis=1)
            kept = low(kept + got.astype(f32))
            cols = kept.shape[1]
            bits = list(range(1, dp_bits))
            sides = []
            for order, side in ((bits, slice(0, cols // 2)), (bits[::-1], slice(cols // 2, cols))):
                value = kept[:, side].reshape((2,) * len(bits) + (share, cols // 2))
                left = bits[::-1]
                for b in order:
                    axis = left.index(b)
                    bit = bit_of(b)
                    send = lax.dynamic_index_in_dim(value, 1 - bit, axis, keepdims=False)
                    keep = lax.dynamic_index_in_dim(value, bit, axis, keepdims=False)
                    value = keep + flip("dp", dp_size, b)(send)
                    left = [x for x in left if x != b]
                sides.append(value)
            return jnp.concatenate(sides, axis=1)

        def slots_of(shares):
            return [
                jnp.concatenate(
                    [s[:, k * (s.shape[1] // mp_size) : (k + 1) * (s.shape[1] // mp_size)] for s in shares], axis=1
                )
                for k in range(mp_size)
            ]

        def gather_grads(total):
            return lax.all_gather(total, "dp", axis=0, tiled=True)

        bias_two = jnp.sum(e2.astype(f32), axis=0)
        do2 = low(nn(e2, w_o2))
        dq2, dk2, dv2 = attend_backward(source_info, q2, k2, v2, o2, do2, lse2, False)
        memory_part = low(nt(dk2, w_k2) + nt(dv2, w_v2))
        back, gain_two, shift_two = norm_backward(first, gains[1], nt(dq2, w_q2))
        grad_first = grad_second + back
        e1 = low(grad_first)

        pair_perm = [(i, (i // group) * group + (i % group - 1) % group) for i in range(mp_size)]

        def row_sum(piece_of):
            total = piece_of(lax.rem(part + 1, group))
            for k in range(group - 2, -1, -1):
                total = lax.ppermute(total, "mp", pair_perm).astype(f32)
                total = total + piece_of(lax.rem(part - k + group, group)).astype(f32)
                if k:
                    total = low(total)
            return total

        def memory_piece(p):
            return lax.dynamic_slice_in_dim(memory_part, p * (source // group), source // group, 0)

        memory_slots = gather_slots(low(row_sum(memory_piece)))
        cross_share = halving_sum([(h2, dq2), (mem_row, dk2), (mem_row, dv2), (e2, o2)])

        bias_one = jnp.sum(e1.astype(f32), axis=0)
        do1 = low(nn(e1, w_o1))
        output = place(causal_places, output_slots, bf16).reshape(tokens.shape)
        do1 = after(do1, output)
        dq1, dk1, dv1 = attend_backward(target_info, q1, k1, v1, o1, do1, lse1, True)
        kv_part = low(nt(dk1, w_k1) + nt(dv1, w_v1))

        def causal_piece(p):
            return jnp.concatenate(
                [
                    lax.dynamic_slice_in_dim(kv_part, s, block, 0)
                    for s in (p * block, (2 * group - 1 - p) * block)
                ]
            )

        ffn_total = reduce_slots(slots_of([down_share, up_share]))
        ffn_full = gather_grads(ffn_total)
        cross_total = reduce_slots(slots_of([cross_share[:, i * width : (i + 1) * width] for i in range(4)]))
        cross_full = gather_grads(cross_total)

        grad_h1 = nt(dq1, w_q1) + row_sum(causal_piece)
        back, gain_one, shift_one = norm_backward(resid, gains[0], grad_h1)
        tokens_own = low(grad_first + back)
        tokens_slots = gather_slots(tokens_own)

        self_share = halving_sum([(h1, dq1), (h1_row, dk1), (h1_row, dv1), (e1, o1)])
        self_total = reduce_slots(slots_of([self_share[:, i * width : (i + 1) * width] for i in range(4)]))
        self_full = gather_grads(self_total)

        memory_grad = place(memory_places, memory_slots, f32).reshape(memory.shape)
        tokens_grad = place(causal_places, tokens_slots, f32).reshape(tokens.shape)

        def by_slot(vector):
            return vector.reshape(mp_size, -1)

        def total_of(values):
            return jnp.sum(values.astype(f32), axis=0)

        slot_sums = jnp.concatenate(
            [
                by_slot(total_of(dq1)),
                by_slot(total_of(dv1)),
                by_slot(total_of(dq2)),
                by_slot(total_of(dv2)),
                by_slot(up_bias_grad),
            ],
            axis=1,
        )
        flipped = slot_sums[::-1]
        twice = jnp.concatenate([flipped, flipped])
        in_order = lax.dynamic_slice_in_dim(twice, mp_size - 1 - z, mp_size, 0)
        whole = jnp.stack(
            [gain_one, gain_two, gain_three, shift_one, shift_two, shift_three, bias_one, bias_two, bias_three]
        )
        small = jnp.concatenate([in_order.reshape(-1, PAIR), whole.reshape(-1, PAIR)])
        for b in range(dp_bits):
            small = small + flip("dp", dp_size, b)(small)
        for b in range(mp_size.bit_length() - 1):
            small = small + flip("mp", mp_size, b)(small)
        small = small.reshape(-1)
        slot_part = small[: in_order.size].reshape(in_order.shape)
        mine = lax.dynamic_index_in_dim(slot_part, z, 0, keepdims=False)
        whole = small[in_order.size :].reshape(9, width)

        def cut(full, i):
            return full[:, i * per : (i + 1) * per].astype(f32)

        return (
            output,
            tokens_grad,
            memory_grad,
            whole[0:3],
            whole[3:6],
            jnp.stack([cut(self_full, 0), cut(self_full, 1), cut(self_full, 2)]),
            jnp.stack([mine[:per], mine[per : 2 * per]]),
            cut(self_full, 3).T,
            cut(cross_full, 0),
            jnp.stack([cut(cross_full, 1), cut(cross_full, 2)]),
            jnp.stack([mine[2 * per : 3 * per], mine[3 * per : 4 * per]]),
            cut(cross_full, 3).T,
            whole[6:9],
            ffn_full[:, hid:].astype(f32),
            mine[4 * per :],
            ffn_full[:, :hid].astype(f32).T,
        )

    return shards


def solution(mesh):
    placed = (
        P("dp", None, None),
        P("dp", None, None),
        P("dp"),
        P("dp"),
        P("dp", None, None),
        P(),
        P(),
        P(None, None, "mp"),
        P(None, "mp"),
        P("mp", None),
        P(None, "mp"),
        P(None, None, "mp"),
        P(None, "mp"),
        P("mp", None),
        P(),
        P(None, "mp"),
        P("mp"),
        P("mp", None),
    )
    return jax.shard_map(
        build(mesh.shape["dp"], mesh.shape["mp"]),
        mesh=mesh,
        in_specs=placed,
        out_specs=(
            P("dp", None, None),
            P("dp", None, None),
            P("dp", None, None),
            P(),
            P(),
            P(None, None, "mp"),
            P(None, "mp"),
            P("mp", None),
            P(None, "mp"),
            P(None, None, "mp"),
            P(None, "mp"),
            P("mp", None),
            P(),
            P(None, "mp"),
            P("mp"),
            P("mp", None),
        ),
        check_vma=False,
    )
```

```python
import functools

import jax
import jax.numpy as jnp
from jax import lax
from jax.experimental import pallas as pl
from jax.experimental.pallas import tpu as pltpu
from jax.sharding import PartitionSpec as P

neg_fill = -1000000000.0
open_cap = 3e38
eps_norm = 1e-05
PAIR = 128
HALF = 64
QUERY_SCALE = 0.125
ROOT = 0.7978845608028654
CUBE = 0.044715
f32 = jnp.float32
bf16 = jnp.bfloat16
ROW, FIRST, SECOND, TARGET, SOURCE, PLANE, CORE = range(7)


def low(value):
    return value.astype(bf16)


def nn(left, right):
    return lax.dot_general(left, right, (((1,), (0,)), ((), ())), preferred_element_type=f32)


def nt(left, right):
    return lax.dot_general(left, right, (((1,), (1,)), ((), ())), preferred_element_type=f32)


def tn(left, right):
    return lax.dot_general(left, right, (((0,), (0,)), ((), ())), preferred_element_type=f32)


def after(value, *others):
    return lax.optimization_barrier((value,) + others)[0]


def wall(*values):
    return lax.optimization_barrier(values)


def call(kernel, info, grid, ins, outs, scratch=(), micros=1.0):
    return pl.pallas_call(
        kernel,
        out_shape=tuple(jax.ShapeDtypeStruct(s, t) for s, t, _, _ in outs),
        grid_spec=pltpu.PrefetchScalarGridSpec(
            num_scalar_prefetch=1,
            grid=grid,
            in_specs=[pl.BlockSpec(b, m) for _, b, m in ins],
            out_specs=tuple(pl.BlockSpec(b, m) for _, _, b, m in outs),
            scratch_shapes=list(scratch),
        ),
        compiler_params=pltpu.CompilerParams(vmem_limit_bytes=52 << 20),
        cost_estimate=pl.CostEstimate(flops=int(micros * 1e7), bytes_accessed=1 << 10, transcendentals=0),
    )(info, *(a for a, _, _ in ins))


def rows_of_eight(values):
    return jnp.sum(values.reshape(values.shape[0] // 8, 8, values.shape[1]), axis=0)


def norm_stats(values):
    centre = jnp.mean(values, axis=-1, keepdims=True)
    offset = values - centre
    spread = jnp.mean(offset * offset, axis=-1, keepdims=True)
    scale = lax.rsqrt(spread + eps_norm)
    return offset * scale, scale


def norm_back(values, gain, grad):
    hat, scale = norm_stats(values)
    scaled = grad * gain
    mean_one = jnp.mean(scaled, axis=-1, keepdims=True)
    mean_two = jnp.mean(scaled * hat, axis=-1, keepdims=True)
    return scale * (scaled - mean_one - hat * mean_two), grad * hat


def head_halves(both):
    lane = lax.broadcasted_iota(jnp.int32, both.shape, 1)
    zero = jnp.zeros_like(both)
    return jnp.where(lane < HALF, both, zero), jnp.where(lane < HALF, zero, both)


def fill_caps(info, cap_ref, block, causal):
    length = cap_ref.shape[0]
    for t in range(2):
        keys = lax.broadcasted_iota(jnp.int32, (length, block), 0)
        allowed = keys < info[TARGET if causal else SOURCE]
        if causal:
            places = lax.broadcasted_iota(jnp.int32, (length, block), 1) + info[FIRST + t] * block
            allowed = allowed & (keys <= places)
        cap_ref[:, t * block : (t + 1) * block] = jnp.where(allowed, open_cap, neg_fill)


def forward_kernel(info, q_ref, k_ref, v_ref, o_ref, lse_ref, cap_ref, s_ref, *, block, causal, chunk):
    length = k_ref.shape[0]

    @pl.when(pl.program_id(0) == 0)
    def _():
        fill_caps(info, cap_ref, block, causal)

    for t in (1, 0):
        rows = slice(t * block, (t + 1) * block)
        span = length // 2 if (causal and t == 0) else length
        queries = jnp.concatenate(head_halves(q_ref[rows, :] * bf16(QUERY_SCALE)), axis=0)
        most = jnp.full((8, 2 * block), -open_cap, f32)
        for c in range(0, span, chunk):
            keys = slice(c, c + chunk)
            cap = cap_ref[keys, rows]
            scores = jnp.minimum(nt(k_ref[keys, :], queries), jnp.concatenate([cap, cap], axis=1))
            s_ref[t, keys, :] = scores
            most = jnp.maximum(most, jnp.max(scores.reshape(chunk // 8, 8, 2 * block), axis=0))
        most = jnp.max(most, axis=0, keepdims=True)
        total = jnp.zeros((8, 2 * block), f32)
        mixed = jnp.zeros((PAIR, 2 * block), f32)
        for c in range(0, span, chunk):
            keys = slice(c, c + chunk)
            weights = jnp.exp(s_ref[t, keys, :] - most)
            total = total + rows_of_eight(weights)
            mixed = mixed + tn(v_ref[keys, :], low(weights))
        total = jnp.sum(total, axis=0, keepdims=True)
        mixed = mixed / total
        sub = lax.broadcasted_iota(jnp.int32, (PAIR, block), 0)
        o_ref[rows, :] = low(jnp.where(sub < HALF, mixed[:, :block], mixed[:, block:]).T)
        lse = most + jnp.log(total)
        lse_ref[0, 0:1, rows] = lse[:, :block]
        lse_ref[0, 1:2, rows] = lse[:, block:]


def backward_kernel(
    info, q_ref, k_ref, v_ref, o_ref, g_ref, lse_ref, dq_ref, dk_ref, dv_ref, qs_ref, vs_ref, cap_ref, dk_acc, dv_acc,
    *, block, causal, chunk
):
    length = k_ref.shape[0]

    @pl.when(pl.program_id(0) == 0)
    def _():
        fill_caps(info, cap_ref, block, causal)

    q_sums = jnp.zeros((8, PAIR), f32)
    for t in (1, 0):
        rows = slice(t * block, (t + 1) * block)
        span = length // 2 if (causal and t == 0) else length
        grads = g_ref[rows, :]
        prod = (grads.astype(f32) * o_ref[rows, :].astype(f32)).T
        centre = jnp.concatenate(
            [jnp.sum(prod[:HALF], axis=0, keepdims=True), jnp.sum(prod[HALF:], axis=0, keepdims=True)], axis=1
        )
        lse = jnp.concatenate([lse_ref[0, 0:1, rows], lse_ref[0, 1:2, rows]], axis=1)
        queries = jnp.concatenate(head_halves(q_ref[rows, :] * bf16(QUERY_SCALE)), axis=0)
        grads = jnp.concatenate(head_halves(grads), axis=0)
        dq = jnp.zeros((PAIR, 2 * block), f32)
        for c in range(0, span, chunk):
            keys = slice(c, c + chunk)
            k, v = k_ref[keys, :], v_ref[keys, :]
            cap = cap_ref[keys, rows]
            scores = jnp.minimum(nt(k, queries), jnp.concatenate([cap, cap], axis=1))
            probs = jnp.exp(scores - lse)
            grad_scores = low(probs * (nt(v, grads) - centre))
            dv = nn(low(probs), grads)
            dk = nn(grad_scores, queries)
            dq = dq + tn(k, grad_scores)
            if t == 1:
                dk_acc[keys, :] = dk
                dv_acc[keys, :] = dv
            else:
                dk_acc[keys, :] += dk
                dv_acc[keys, :] += dv
        sub = lax.broadcasted_iota(jnp.int32, (PAIR, block), 0)
        dq = jnp.where(sub < HALF, dq[:, :block], dq[:, block:]) * QUERY_SCALE
        dq = low(dq.T)
        dq_ref[rows, :] = dq
        q_sums = q_sums + rows_of_eight(dq.astype(f32))
    dk_ref[...] = low(dk_acc[...])
    dv = low(dv_acc[...])
    dv_ref[...] = dv
    qs_ref[...] = q_sums
    vs_ref[...] = rows_of_eight(dv.astype(f32))


def attend_forward(info, query, keys, values, causal):
    queries, width = query.shape
    length = keys.shape[0]
    here = lambda i, _: (0, i)
    return call(
        functools.partial(forward_kernel, block=queries // 2, causal=causal, chunk=min(256, length // 2)),
        info,
        (width // PAIR,),
        [(query, (queries, PAIR), here), (keys, (length, PAIR), here), (values, (length, PAIR), here)],
        [
            ((queries, width), bf16, (queries, PAIR), here),
            ((width // PAIR, 8, queries), f32, (1, 8, queries), lambda i, _: (i, 0, 0)),
        ],
        [pltpu.VMEM((length, queries), f32), pltpu.VMEM((2, length, queries), f32)],
        micros=16,
    )


def attend_backward(info, query, keys, values, mixed, grad, lse_rows, causal):
    queries, width = query.shape
    length = keys.shape[0]
    here = lambda i, _: (0, i)
    one, key = (queries, PAIR), (length, PAIR)
    return call(
        functools.partial(backward_kernel, block=queries // 2, causal=causal, chunk=min(256, length // 2)),
        info,
        (width // PAIR,),
        [
            (query, one, here),
            (keys, key, here),
            (values, key, here),
            (mixed, one, here),
            (grad, one, here),
            (lse_rows, (1, 8, queries), lambda i, _: (i, 0, 0)),
        ],
        [
            ((queries, width), bf16, one, here),
            ((length, width), bf16, key, here),
            ((length, width), bf16, key, here),
            ((8, width), f32, (8, PAIR), here),
            ((8, width), f32, (8, PAIR), here),
        ],
        [pltpu.VMEM((length, queries), f32), pltpu.VMEM((length, PAIR), f32), pltpu.VMEM((length, PAIR), f32)],
        micros=24,
    )


def order_kernel(info, same_ref, other_ref, out_ref, *, part_of):
    mine = lax.rem(part_of(pl.program_id(0)), 2) == info[CORE]

    @pl.when(mine)
    def _():
        out_ref[...] = same_ref[...].astype(out_ref.dtype)

    @pl.when(jnp.logical_not(mine))
    def _():
        out_ref[...] = other_ref[...].astype(out_ref.dtype)


def order_rows(info, found, got, rows, group, pieces, kind):
    half, width = got.shape
    steps = group * pieces
    block = half // (rows * steps // 2)

    def part_of(i):
        b = lax.rem(i, steps)
        return jnp.where(b >= group, steps - 1 - b, b)

    def source(i):
        late = (lax.rem(i, steps) >= group).astype(jnp.int32)
        return (lax.div(i, steps) * (group // 2) + lax.div(part_of(i), 2)) * pieces + late

    return call(
        functools.partial(order_kernel, part_of=part_of),
        info,
        (rows * steps,),
        [
            (found, (block, width), lambda i, info: (source(i) + info[CORE] * (half // block), 0)),
            (got, (block, width), lambda i, _: (source(i), 0)),
        ],
        [((2 * half, width), kind, (block, width), lambda i, _: (i, 0))],
        micros=4,
    )[0]


def entry_kernel(info, x_ref, gain_ref, shift_ref, h_ref, *, which):
    hat, _ = norm_stats(x_ref[...].astype(f32))
    one = slice(which, which + 1)
    h_ref[...] = low(hat * gain_ref[one, :].astype(f32) + shift_ref[one, :].astype(f32))


def entry_norm(info, tokens, gains, shifts):
    _, length, width = tokens.shape
    tile = min(256, length)
    whole = lambda i, _: (0, 0)
    return call(
        functools.partial(entry_kernel, which=0),
        info,
        (length // tile,),
        [
            (tokens, (None, tile, width), lambda i, info: (info[ROW], i, 0)),
            (gains, gains.shape, whole),
            (shifts, shifts.shape, whole),
        ],
        [((length, width), bf16, (tile, width), lambda i, _: (i, 0))],
        micros=3,
    )[0]


def weight_ins(weight, slots):
    own, lead, rest, place = weight
    depth = rest.shape[0]
    wide = own.shape[1] * own.shape[2] // depth
    return [
        (own, (None,) + own.shape[1:], lambda *_: (lead, 0, 0)),
        (rest, (depth, (slots - 1) * wide), lambda *_: (0, place)),
    ]


def project_kernel(info, x_ref, own_ref, rest_ref, *others, flipped):
    x = x_ref[...]
    mine = nt(x, own_ref[...]) if flipped else nn(x, own_ref[...])
    wide = mine.shape[1]
    rest = nn(x, rest_ref[...])
    out_ref = others[-1]
    if len(others) > 1:
        mine = mine + others[0][:, :wide]
        rest = rest + others[0][:, wide:]
    out_ref[:, :wide] = low(mine)
    out_ref[:, wide:] = low(rest)


def project(info, x, place_of, tiles, weight, bias, slots, flipped=False):
    count, tile = tiles
    depth = x.shape[2]
    ins = [(x, (None, tile, depth), lambda i, info: place_of(i, info) + (0,))] + weight_ins(weight, slots)
    own = weight[0]
    width = slots * (own.shape[1] * own.shape[2] // depth)
    if bias is not None:
        ins.append((bias, bias.shape, lambda i, _: (0, 0)))
    return call(
        functools.partial(project_kernel, flipped=flipped),
        info,
        (count,),
        ins,
        [((count * tile, width), bf16, (tile, width), lambda i, _: (i, 0))],
        micros=2.5 * count * tile / 1024,
    )[0]


def mix_kernel(info, x_ref, own_ref, rest_ref, resid_ref, bias_ref, gain_ref, shift_ref, sum_ref, h_ref, *, which):
    wide = own_ref.shape[0]
    found = nn(x_ref[:, :wide], own_ref[...]) + nt(x_ref[:, wide:], rest_ref[...])
    found = resid_ref[...].astype(f32) + found + bias_ref[which : which + 1, :].astype(f32)
    sum_ref[...] = found
    hat, _ = norm_stats(found)
    one = slice(which + 1, which + 2)
    h_ref[...] = low(hat * gain_ref[one, :].astype(f32) + shift_ref[one, :].astype(f32))


def mix(info, x, weight, resid, resid_place, biases, gains, shifts, which, slots):
    rows, width = x.shape
    block = rows // 2
    whole = lambda i, _: (0, 0)
    here = lambda i, _: (i, 0)
    depth = resid.shape[2]
    return call(
        functools.partial(mix_kernel, which=which),
        info,
        (2,),
        [(x, (block, width), here)]
        + weight_ins(weight, slots)
        + [
            (resid, (None, block, depth), lambda i, info: resid_place(i, info) + (0,)),
            (biases, biases.shape, whole),
            (gains, gains.shape, whole),
            (shifts, shifts.shape, whole),
        ],
        [((rows, depth), f32, (block, depth), here), ((rows, depth), bf16, (block, depth), here)],
        micros=4,
    )


def back_dots(pairs):
    total = None
    for x_ref, own_ref, rest_ref in pairs:
        wide = own_ref.shape[1]
        found = nt(x_ref[:, :wide], own_ref[...]) + nt(x_ref[:, wide:], rest_ref[...])
        total = found if total is None else total + found
    return total


def back_kernel(info, *refs, count):
    pairs = [refs[3 * j : 3 * j + 3] for j in range(count)]
    refs[-1][...] = low(back_dots(pairs))


def back(info, terms, slots):
    rows, width = terms[0][0].shape
    depth = terms[0][1][2].shape[0]
    tile = min(256, rows)
    ins = []
    for x, weight in terms:
        ins += [(x, (tile, width), lambda i, _: (i, 0))] + weight_ins(weight, slots)
    return call(
        functools.partial(back_kernel, count=len(terms)),
        info,
        (rows // tile,),
        ins,
        [((rows, depth), bf16, (tile, depth), lambda i, _: (i, 0))],
        micros=5,
    )[0]


def back_norm_kernel(info, *refs, extras, which, keep):
    x_ref, own_ref, rest_ref = refs[:3]
    extra = refs[3 : 3 + extras]
    v_ref, add_ref, gain_ref = refs[3 + extras : 6 + extras]
    outs = refs[6 + extras :]
    grad = back_dots([(x_ref, own_ref, rest_ref)])
    for e in extra:
        grad = grad + e[...].astype(f32)
    found, to_gain = norm_back(v_ref[...].astype(f32), gain_ref[which : which + 1, :].astype(f32), grad)
    found = add_ref[...] + found
    low_found = low(found)
    if keep:
        outs[0][...] = found
    outs[-2][...] = low_found
    sums = jnp.concatenate([rows_of_eight(to_gain), rows_of_eight(grad), rows_of_eight(low_found.astype(f32))])

    @pl.when(pl.program_id(0) == 0)
    def _():
        outs[-1][...] = sums

    @pl.when(pl.program_id(0) > 0)
    def _():
        outs[-1][...] += sums


def back_norm(info, x, weight, extras, values, values_place, add, gains, which, slots, keep):
    rows, width = x.shape
    block = rows // 2
    depth = add.shape[1]
    here = lambda i, _: (i, 0)
    whole = lambda i, _: (0, 0)
    one = (block, depth)
    outs = [((rows, depth), bf16, one, here), ((24, depth), f32, (24, depth), whole)]
    if keep:
        outs = [((rows, depth), f32, one, here)] + outs
    return call(
        functools.partial(back_norm_kernel, extras=len(extras), which=which, keep=keep),
        info,
        (2,),
        [(x, (block, width), here)]
        + weight_ins(weight, slots)
        + [(e, one, here) for e in extras]
        + [
            (values, (None, block, depth), lambda i, info: values_place(i, info) + (0,)),
            (add, one, here),
            (gains, gains.shape, whole),
        ],
        outs,
        micros=4,
    )


def feed_kernel(
    info, h_ref, c0_ref, c1_ref, second_ref, upo_ref, downo_ref, upr_ref, downr_ref, ub_ref, bias_ref, gain_ref,
    a_ref, du_ref, us_ref, final_ref, g_ref, e_ref, sums_ref, out_acc, dh_acc, *, own_tiles
):
    i = pl.program_id(0)
    block = c0_ref.shape[0]
    cots = (c0_ref, c1_ref)
    which = 2

    def tile(own):
        sums = None
        for t in range(2):
            rows = slice(t * block, (t + 1) * block)
            up = upo_ref[...] if own else upr_ref[...]
            pre = nn(h_ref[rows, :], up) + ub_ref[...]
            square = pre * pre
            curve = jnp.tanh(ROOT * (pre + CUBE * square * pre))
            act = low(0.5 * pre * (1.0 + curve))
            slope = 0.5 * (1.0 + curve) + 0.5 * pre * (1.0 - curve * curve) * (ROOT * (1.0 + 3.0 * CUBE * square))
            a_ref[rows, :] = act
            if own:
                grad = nt(cots[t][...], downo_ref[...])
                out = nn(act, downo_ref[...])
            else:
                grad = nn(cots[t][...], downr_ref[...])
                out = nt(act, downr_ref[...])
            du = low(slope * grad)
            du_ref[rows, :] = du
            part = rows_of_eight(du.astype(f32))
            sums = part if sums is None else sums + part
            dh = nt(du, up)
            first = i == 0
            if own:

                @pl.when(first)
                def _():
                    out_acc[rows, :] = out
                    dh_acc[rows, :] = dh

                @pl.when(jnp.logical_not(first))
                def _():
                    out_acc[rows, :] += out
                    dh_acc[rows, :] += dh
            else:
                out_acc[rows, :] += out
                dh_acc[rows, :] += dh
        us_ref[...] = sums

    @pl.when(i < own_tiles)
    def _():
        tile(True)

    @pl.when(i >= own_tiles)
    def _():
        tile(False)

    @pl.when(i == pl.num_programs(0) - 1)
    def _():
        sums = None
        gain = gain_ref[which : which + 1, :].astype(f32)
        for t in range(2):
            rows = slice(t * block, (t + 1) * block)
            second = second_ref[rows, :]
            final_ref[rows, :] = low(second + out_acc[rows, :] + bias_ref[which : which + 1, :].astype(f32))
            cot = cots[t][...].astype(f32)
            grad = dh_acc[rows, :]
            found, to_gain = norm_back(second, gain, grad)
            found = cot + found
            g_ref[rows, :] = found
            rounded = low(found)
            e_ref[rows, :] = rounded
            part = jnp.concatenate(
                [
                    rows_of_eight(to_gain),
                    rows_of_eight(grad),
                    rows_of_eight(rounded.astype(f32)),
                    rows_of_eight(cot),
                ]
            )
            sums = part if sums is None else sums + part
        sums_ref[...] = sums


def feed_forward(info, h, cotangent, second, up, down, up_bias, biases, gains, slots):
    rows, depth = h.shape
    block = rows // 2
    up_own, _, up_rest, up_place = up
    down_own, _, down_rest, down_place = down
    hidden = up_own.shape[2]
    tile = min(512, hidden)
    own_tiles = hidden // tile
    total = slots * own_tiles
    rest_tiles = (slots - 1) * own_tiles
    own_at = lambda i: jnp.minimum(i, own_tiles - 1)
    rest_at = lambda i: jnp.maximum(i - own_tiles, 0)
    whole = lambda i, _: (0, 0)
    full = (rows, depth)
    return call(
        functools.partial(feed_kernel, own_tiles=own_tiles),
        info,
        (total,),
        [
            (h, full, whole),
            (cotangent, (None, block, depth), lambda i, _: (0, 0, 0)),
            (cotangent, (None, block, depth), lambda i, _: (0, 1, 0)),
            (second, full, whole),
            (up_own, (None, depth, tile), lambda i, _: (0, 0, own_at(i))),
            (down_own, (None, tile, depth), lambda i, _: (0, own_at(i), 0)),
            (up_rest, (depth, tile), lambda i, _: (0, up_place * rest_tiles + rest_at(i))),
            (down_rest, (depth, tile), lambda i, _: (0, down_place * rest_tiles + rest_at(i))),
            (up_bias, (1, tile), lambda i, _: (0, i)),
            (biases, biases.shape, whole),
            (gains, gains.shape, whole),
        ],
        [
            ((rows, total * tile), bf16, (rows, tile), lambda i, _: (0, i)),
            ((rows, total * tile), bf16, (rows, tile), lambda i, _: (0, i)),
            ((8, total * tile), f32, (8, tile), lambda i, _: (0, i)),
            (full, bf16, full, whole),
            (full, f32, full, whole),
            (full, bf16, full, whole),
            ((32, depth), f32, (32, depth), whole),
        ],
        [pltpu.VMEM(full, f32), pltpu.VMEM(full, f32)],
        micros=32,
    )


def grad_kernel(info, *refs, plan, share, plane, mine):
    acts = refs[: sum(len(pieces) for pieces, _ in plan)]
    refs = refs[len(acts) :]
    grads = refs[: len(plan)]
    refs = refs[len(plan) :]
    got_ref = None
    if mine:
        got_ref, refs = refs[0], refs[1:]
    outs, turned = refs[: plane if mine else 1], refs[-len(plan) :]
    core = info[CORE] if mine else 1 - info[CORE]

    @pl.when(pl.program_id(0) == 0)
    def _():
        at = 0
        for t, (pieces, _) in enumerate(plan):
            start = 0
            for length in pieces:
                for r in range(plane):
                    if share % PAIR == 0:
                        block = 2 * jnp.bitwise_xor(info[PLANE], r) + core
                        cols = acts[at][:, pl.ds(pl.multiple_of(block * share, share), share)]
                    else:
                        cols = acts[at][:, r * share : (r + 1) * share]
                    turned[t][r * share : (r + 1) * share, start : start + length] = cols.T
                start += length
                at += 1

    first = 0
    for t, (_, wide) in enumerate(plan):
        cols = slice(first, first + wide)
        found = nn(turned[t][...], grads[t][...])
        if mine:
            found = low(found + got_ref[:, cols].astype(f32))
            for r in range(plane):
                outs[r][:, cols] = found[r * share : (r + 1) * share, :]
        else:
            outs[0][:, cols] = low(found)
        first += wide


def weight_grads(info, tensors, d, dp_size, slots, got=None):
    depth = tensors[0][0][0][0].shape[2]
    share, plane = depth // dp_size, dp_size // 2
    core = lax.rem(d, 2) if got is not None else 1 - lax.rem(d, 2)
    plan = [(tuple(rows for _, rows, _ in pieces), grad.shape[1] // slots) for pieces, grad in tensors]
    ins = []
    for pieces, _ in tensors:
        for array, rows, place in pieces:
            if share % PAIR == 0:
                ins.append((array, (None, rows, depth), lambda i, info, place=place: place(info) + (0,)))
            else:
                wide = array.reshape(array.shape[:2] + (plane, 2, share))
                wide = lax.dynamic_index_in_dim(wide, core, 3, keepdims=False)
                order = [jnp.bitwise_xor(d // 2, r) for r in range(plane)]
                wide = jnp.concatenate([lax.dynamic_index_in_dim(wide, b, 2) for b in order], axis=2)
                wide = wide.reshape(array.shape[:2] + (depth // 2,))
                ins.append((wide, (None, rows, depth // 2), lambda i, info, place=place: place(info) + (0,)))
    for (_, grad), (_, wide) in zip(tensors, plan):
        ins.append((grad, (grad.shape[0], wide), lambda i, _: (0, i)))
    half = depth // 2
    tile = sum(wide for _, wide in plan)
    if got is not None:
        ins.append((got, (half, tile), lambda i, _: (0, i)))
        outs = [((share, slots * tile), bf16, (share, tile), lambda i, _: (0, i))] * plane
    else:
        outs = [((half, slots * tile), bf16, (half, tile), lambda i, _: (0, i))]
    return call(
        functools.partial(grad_kernel, plan=plan, share=share, plane=plane, mine=got is not None),
        info,
        (slots,),
        ins,
        outs,
        [pltpu.VMEM((half, g.shape[0]), bf16) for _, g in tensors],
        micros=8,
    )


def finish_kernel(info, in_ref, out_ref, *, turn):
    value = in_ref[...].astype(f32)
    out_ref[...] = value.T if turn else value


def finish(info, full, places, wide, turn=False):
    depth = full.shape[0]
    first = places[0]
    if turn:
        tile, cut = min(256, depth), min(512, wide)
        return call(
            functools.partial(finish_kernel, turn=True),
            info,
            (depth // tile, wide // cut),
            [(full, (tile, cut), lambda i, j, _: (i, first * (wide // cut) + j))],
            [((wide, depth), f32, (cut, tile), lambda i, j, _: (j, i))],
            micros=3,
        )[0]
    tile = min(512, depth)
    return call(
        functools.partial(finish_kernel, turn=False),
        info,
        (len(places), depth // tile),
        [(full, (tile, wide), lambda i, j, _: (j, first + i))],
        [((len(places), depth, wide), f32, (None, tile, wide), lambda i, j, _: (i, j, 0))],
        micros=3,
    )[0]


def finish_pair_kernel(info, in_ref, q_ref, kv_ref, o_ref, s_ref, so_ref):
    wide = q_ref.shape[1]

    def cols(t):
        return in_ref[:, t * wide : (t + 1) * wide].astype(f32)

    q_ref[...] = cols(0)
    for t in range(2):
        kv_ref[t] = cols(1 + t)
    o_ref[...] = cols(3).T
    for t in range(3):
        s_ref[t] = cols(4 + t)
    so_ref[...] = cols(7).T


def finish_pair(info, full):
    depth = full.shape[0]
    wide = full.shape[1] // 8
    tile = min(256, depth)
    return call(
        finish_pair_kernel,
        info,
        (depth // tile,),
        [(full, (tile, 8 * wide), lambda i, _: (i, 0))],
        [
            ((depth, wide), f32, (tile, wide), lambda i, _: (i, 0)),
            ((2, depth, wide), f32, (2, tile, wide), lambda i, _: (0, i, 0)),
            ((wide, depth), f32, (wide, tile), lambda i, _: (0, i)),
            ((3, depth, wide), f32, (3, tile, wide), lambda i, _: (0, i, 0)),
            ((wide, depth), f32, (wide, tile), lambda i, _: (0, i)),
        ],
        micros=4,
    )


def build(dp_size, mp_size):
    ring = [(i, (i + 1) % mp_size) for i in range(mp_size)]
    dp_bits = dp_size.bit_length() - 1
    plane = dp_size // 2

    def flip(axis, size, bits):
        return lambda value: lax.ppermute(value, axis, [(i, i ^ bits) for i in range(size)])

    def shards(
        tokens,
        memory,
        target_lengths,
        source_lengths,
        cotangent,
        norm_gain,
        norm_bias,
        self_in,
        self_in_bias,
        self_out,
        cross_query,
        cross_kv,
        cross_bias,
        cross_out,
        out_bias,
        ffn_up,
        ffn_up_bias,
        ffn_down,
    ):
        rows, length, width = tokens.shape
        source = memory.shape[1]
        d = lax.axis_index("dp")
        z = lax.axis_index("mp")
        group = mp_size // rows
        core = lax.rem(d, 2)
        chips = group // 2
        chip_row = z // chips
        part = (z % chips) * 2 + core
        held = chip_row // rows == core
        row = lax.rem(chip_row, rows)
        block = length // (2 * group)
        share = width // dp_size
        per = width // mp_size
        hid = ffn_up.shape[1]
        swap = flip("dp", dp_size, 1)

        def across(mine, theirs):
            return jnp.where(held, mine, swap(theirs))

        def take_row(values):
            return lax.dynamic_index_in_dim(values, row, 0, keepdims=False)

        def blocks_of(values, p):
            return jnp.concatenate(
                [
                    lax.dynamic_slice_in_dim(values, s * block, block, 0)
                    for s in (p, 2 * group - 1 - p)
                ]
            )

        own_place = lambda i, info: (info[ROW], info[FIRST + i])
        own_h_place = lambda i, info: (0, info[FIRST + i])
        flat_place = lambda i, info: (0, i)
        row_place = lambda i, info: (info[ROW], i)

        def rows_of(weight):
            return lax.dynamic_slice_in_dim(weight, d * share, share, 0)

        def cols_of(weight):
            return lax.dynamic_slice_in_dim(weight, d * share, share, 1).T

        def with_bias(piece, bias):
            extra = jnp.zeros((16, piece.shape[1]), bf16)
            if bias is not None:
                extra = lax.dynamic_update_slice(extra, bias[None], (0, 0))
            return jnp.concatenate([piece, extra])

        def side_by_side(pieces):
            return jnp.concatenate([with_bias(p, b) for p, b in pieces], axis=1)

        def pass_on(value):
            return lax.ppermute(value, "mp", ring)

        def gather_rest(found, wides, *held):
            starts = [0]
            for w in wides:
                starts.append(starts[-1] + w)
            both = jnp.concatenate([s[:, a:b] for a, b in zip(starts[:-1], starts[1:]) for s in found], axis=1)
            ours = both[:share]
            if held:
                ours = after(ours, *held)
            return lax.all_gather(ours, "dp", axis=0, tiled=True), both[share : share + 1].astype(f32)

        def bias_of(own, biases, t, wide):
            far = (mp_size - 1) * wide
            return jnp.concatenate([own.astype(f32)[None], biases[:, t * far : (t + 1) * far]], axis=1)

        found_a = [
            pass_on(
                side_by_side(
                    [
                        (rows_of(self_in[0]), self_in_bias[0]),
                        (rows_of(self_in[1]), None),
                        (rows_of(self_in[2]), self_in_bias[1]),
                    ]
                )
            )
        ]
        lengths = jnp.stack([target_lengths[row], source_lengths[row]])
        lengths = across(lengths, lengths)
        tokens_row = take_row(tokens)
        tokens_row = across(tokens_row, tokens_row)[None]
        info = jnp.stack(
            [0 * part, part, 2 * group - 1 - part, lengths[0], lengths[1], d // 2, core]
        ).astype(jnp.int32)
        found_a[0], tokens_row, info = wall(found_a[0], tokens_row, info)
        for _ in range(mp_size - 2):
            found_a.append(pass_on(found_a[-1]))
        h1_row = entry_norm(info, tokens_row, norm_gain, norm_bias)
        memory_row = take_row(memory)
        memory_row = across(memory_row, memory_row)[None]
        cot_row = take_row(cotangent)
        cot_own = across(blocks_of(cot_row, part), blocks_of(cot_row, jnp.bitwise_xor(part, 1)))[None]
        found_a[-1], h1_row, memory_row, cot_own = wall(found_a[-1], h1_row, memory_row, cot_own)
        found_b = [
            after(
                side_by_side(
                    [
                        (cols_of(self_out), None),
                        (rows_of(cross_query), cross_bias[0]),
                        (rows_of(cross_kv[0]), None),
                        (rows_of(cross_kv[1]), cross_bias[1]),
                    ]
                ),
                found_a[-1],
            )
        ]
        for _ in range(mp_size - 1):
            found_b.append(pass_on(found_b[-1]))
        found_b = found_b[1:]
        rest_a, bias_a = gather_rest(found_a, [per] * 3)
        rest_b, bias_b = gather_rest(found_b, [per] * 4)
        w_q1, w_k1, w_v1 = [(self_in, t, rest_a, t) for t in range(3)]
        w_o1 = (self_out[None], 0, rest_b, 0)
        w_q2 = (cross_query[None], 0, rest_b, 1)
        w_k2, w_v2 = (cross_kv, 0, rest_b, 2), (cross_kv, 1, rest_b, 3)

        last_share = after(
            side_by_side(
                [(rows_of(ffn_up), ffn_up_bias), (cols_of(ffn_down), None), (cols_of(cross_out), None)]
            ),
            found_b[-1],
        )
        found_c = [pass_on(last_share)]
        far = min(256, length)
        h1_flat = h1_row[None]
        k1 = project(info, h1_flat, flat_place, (length // far, far), w_k1, None, mp_size)
        v1 = project(
            info, h1_flat, flat_place, (length // far, far), w_v1, bias_of(self_in_bias[1], bias_a, 2, per), mp_size
        )
        found_c[0], k1, v1 = wall(found_c[0], k1, v1)
        for _ in range(mp_size - 3):
            found_c.append(pass_on(found_c[-1]))
        q1 = project(info, h1_flat, own_h_place, (2, block), w_q1, bias_of(self_in_bias[0], bias_a, 0, per), mp_size)
        found_c[-1], q1 = wall(found_c[-1], q1)
        found_c.append(pass_on(found_c[-1]))
        rest_c, bias_c = gather_rest(found_c, [hid, hid, per])
        w_up, w_down = (ffn_up[None], 0, rest_c, 0), (ffn_down[None], 0, rest_c, 1)
        w_o2 = (cross_out[None], 0, rest_c, 2 * hid // per)
        o1, lse1 = attend_forward(info, q1, k1, v1, True)
        first, h2 = mix(info, o1, w_o1, tokens_row, own_place, out_bias, norm_gain, norm_bias, 0, mp_size)
        q2 = project(info, h2[None], flat_place, (2, block), w_q2, bias_of(cross_bias[0], bias_b, 1, per), mp_size)
        k2 = project(info, memory_row, row_place, (source // far, far), w_k2, None, mp_size)
        v2 = project(
            info, memory_row, row_place, (source // far, far), w_v2, bias_of(cross_bias[1], bias_b, 3, per), mp_size
        )
        o2, lse2 = attend_forward(info, q2, k2, v2, False)
        second, h3 = mix(info, o2, w_o2, first[None], flat_place, out_bias, norm_gain, norm_bias, 1, mp_size)
        hidden, grad_pre, up_sums, final, g2, e2, sums_three = feed_forward(
            info, h3, cot_own, second, w_up, w_down, bias_of(ffn_up_bias, bias_c, 0, hid), out_bias, norm_gain, mp_size
        )

        def to_plane(piece, r):
            return flip("dp", dp_size, 2 * r)(piece)

        def slots_of(total):
            wide = total[0].shape[1] // mp_size
            slots = []
            for k in range(mp_size):
                cols = slice(k * wide, (k + 1) * wide)
                slots.append(low(sum(t[:, cols].astype(f32) for t in total)))
            return slots

        def to_owners(slots):
            return [
                lax.ppermute(slots[k], "mp", [(i, (i - k) % mp_size) for i in range(mp_size)])
                for k in range(1, mp_size)
            ]

        def add_up(values):
            return low(sum(v.astype(f32) for v in values))

        def gather_grads(total):
            return lax.all_gather(total, "dp", axis=0, tiled=True)

        def gather_rows(mine):
            return lax.all_gather(mine, "mp", axis=0, tiled=True)

        def for_other(found):
            half = found.shape[0] // 2
            return swap(lax.dynamic_slice_in_dim(found, (1 - core) * half, half, 0))

        def own_blocks(array, lead):
            return [
                (array, block, lambda info, t=t: ((info[ROW] if lead else 0), info[FIRST + t])) for t in range(2)
            ]

        def all_rows(array, lead=False):
            return [(array, array.shape[1], lambda info: ((info[ROW] if lead else 0), 0))]

        def core_send(tensors):
            return weight_grads(info, tensors, d, dp_size, mp_size)[0]

        def to_core(sent):
            return flip("dp", dp_size, 1)(sent)

        def core_keep(tensors, got):
            return weight_grads(info, tensors, d, dp_size, mp_size, got)

        row_perm = [(i, (i // chips) * chips + (i % chips - 1) % chips) for i in range(mp_size)]

        def row_sum(piece_of):
            got = [swap(piece_of(2 * c + 1 - core)) for c in range(chips)]
            if chips == 1:
                return got[0], piece_of(part)
            pieces = jnp.stack([add_up([got[c], piece_of(2 * c + core)]) for c in range(chips)])
            place = z % chips
            total = lax.dynamic_index_in_dim(pieces, lax.rem(place + 1, chips), 0, keepdims=False)
            for k in range(chips - 2, -1, -1):
                total = lax.ppermute(total, "mp", row_perm)
                here = lax.dynamic_index_in_dim(pieces, lax.rem(place - k + chips, chips), 0, keepdims=False)
                if k:
                    total = add_up([total, here])
            return total, here

        def all_planes(kept):
            return [kept[0]] + [to_plane(kept[r], r) for r in range(1, plane)]

        output_found = gather_rows(final)
        ffn_tensors = [(all_rows(h3[None]), grad_pre), (all_rows(cot_own), hidden)]
        ffn_sent = core_send(ffn_tensors)
        e2, ffn_sent = wall(e2, ffn_sent)

        ffn_got = to_core(ffn_sent)
        do2 = project(info, e2[None], flat_place, (2, block), w_o2, None, mp_size, flipped=True)
        dq2, dk2, dv2, sum_q2, sum_v2 = attend_backward(info, q2, k2, v2, o2, do2, lse2, False)
        memory_part = back(info, [(dk2, w_k2), (dv2, w_v2)], mp_size)

        def memory_piece(p):
            return lax.dynamic_slice_in_dim(memory_part, p * (source // group), source // group, 0)

        ffn_got, memory_part, dq2 = wall(ffn_got, memory_part, dq2)
        memory_got, memory_here = row_sum(memory_piece)
        ffn_kept = core_keep(ffn_tensors, ffn_got)
        memory_got, dq2, *ffn_kept = wall(memory_got, dq2, *ffn_kept)
        memory_own = add_up([memory_got, memory_here])
        memory_found = gather_rows(memory_own)
        memory_own, dq2 = wall(memory_own, dq2)

        late = plane - 1
        ffn_total = [ffn_kept[0]] + [to_plane(ffn_kept[r], r) for r in range(1, late)]
        g1, e1, sums_two = back_norm(
            info, dq2, w_q2, [], first[None], flat_place, g2, norm_gain, 1, mp_size, True
        )
        do1 = project(info, e1[None], flat_place, (2, block), w_o1, None, mp_size, flipped=True)
        dq1, dk1, dv1, sum_q1, sum_v1 = attend_backward(info, q1, k1, v1, o1, do1, lse1, True)
        kv_part = back(info, [(dk1, w_k1), (dv1, w_v1)], mp_size)
        cross_tensors = [
            (all_rows(h2[None]), dq2),
            (all_rows(memory_row), dk2),
            (all_rows(memory_row), dv2),
            (all_rows(e2[None]), o2),
        ]
        cross_sent = core_send(cross_tensors)
        kv_part, cross_sent, last_kept, *ffn_total = wall(kv_part, cross_sent, ffn_kept[late], *ffn_total)

        def causal_piece(p):
            return blocks_of(kv_part, p)

        ffn_total = ffn_total + [to_plane(last_kept, late)]
        got, here = row_sum(causal_piece)
        cross_got = to_core(cross_sent)
        self_tensors = [
            (own_blocks(h1_flat, False), dq1),
            (all_rows(h1_flat), dk1),
            (all_rows(h1_flat), dv1),
            (all_rows(e1[None]), o1),
        ]
        self_sent = core_send(self_tensors)
        output_got = for_other(output_found)
        got, cross_got, self_sent, output_got = wall(got, cross_got, self_sent, output_got)
        tokens_own, sums_one = back_norm(
            info, dq1, w_q1, [got, here], tokens_row, own_place, g1, norm_gain, 0, mp_size, False
        )
        tokens_found = gather_rows(tokens_own)
        tokens_own, self_sent, cross_got = wall(tokens_own, self_sent, cross_got)
        self_got = to_core(self_sent)
        cross_kept = core_keep(cross_tensors, cross_got)
        output = order_rows(info, output_found, output_got, rows, group, 2, bf16).reshape(tokens.shape)
        self_got, output, *kept = wall(self_got, output, *cross_kept)
        cross_total = all_planes(kept)
        self_kept = core_keep(self_tensors, self_got)
        *self_kept, ffn_total[0], ffn_total[late] = wall(*self_kept, ffn_total[0], ffn_total[late])
        ffn_slots = slots_of(ffn_total)
        self_kept[0], *ffn_slots = wall(self_kept[0], *ffn_slots)
        self_total = all_planes(self_kept)
        ffn_total = [ffn_slots[0]] + to_owners(ffn_slots)
        memory_got = for_other(memory_found)
        memory_got, *cross_total = wall(memory_got, *cross_total)
        cross_slots = slots_of(cross_total)
        cross_total = [cross_slots[0]] + to_owners(cross_slots)
        memory_grad = order_rows(info, memory_found, memory_got, rows, group, 1, f32).reshape(memory.shape)
        memory_grad, *kept = wall(memory_grad, *self_total, *ffn_total)
        self_slots = slots_of(kept[:plane])
        self_total = [self_slots[0]] + to_owners(self_slots)
        ffn_full = gather_grads(add_up(kept[plane:]))
        up_grad, down_grad = finish(info, ffn_full, [0], hid)[0], finish(info, ffn_full, [1], hid, True)
        tokens_got = for_other(tokens_found)
        tokens_grad = order_rows(info, tokens_found, tokens_got, rows, group, 2, f32).reshape(tokens.shape)
        tokens_grad, up_grad, down_grad, *kept = wall(tokens_grad, up_grad, down_grad, *cross_total, *self_total)
        joint = jnp.concatenate([add_up(kept[:mp_size]), add_up(kept[mp_size:])], axis=1)
        joint_full = gather_grads(joint)

        def by_slot(sums):
            return jnp.sum(sums, axis=0).reshape(mp_size, -1)

        slot_sums = jnp.concatenate([by_slot(s) for s in (sum_q1, sum_v1, sum_q2, sum_v2, up_sums)], axis=1)
        flipped = slot_sums[::-1]
        twice = jnp.concatenate([flipped, flipped])
        in_order = lax.dynamic_slice_in_dim(twice, mp_size - 1 - z, mp_size, 0)
        whole = [
            jnp.sum(sums.reshape(-1, 8, width), axis=1) for sums in (sums_one, sums_two, sums_three)
        ]
        whole = jnp.concatenate(
            [w[0:1] for w in whole] + [w[1:2] for w in whole] + [whole[1][2:3], whole[2][2:3], whole[2][3:4]]
        )
        small = jnp.concatenate([in_order.reshape(-1, PAIR), whole.reshape(-1, PAIR)])
        for b in range(dp_bits):
            small = small + flip("dp", dp_size, 1 << b)(small)
        for b in range(mp_size.bit_length() - 1):
            small = small + flip("mp", mp_size, 1 << b)(small)
        small = small.reshape(-1)
        slot_part = small[: in_order.size].reshape(in_order.shape)
        mine = lax.dynamic_index_in_dim(slot_part, z, 0, keepdims=False)
        whole = small[in_order.size :].reshape(9, width)
        cross_q, cross_both, cross_o, self_three, self_o = finish_pair(info, joint_full)
        return (
            output,
            tokens_grad,
            memory_grad,
            whole[0:3],
            whole[3:6],
            self_three,
            jnp.stack([mine[:per], mine[per : 2 * per]]),
            self_o,
            cross_q,
            cross_both,
            jnp.stack([mine[2 * per : 3 * per], mine[3 * per : 4 * per]]),
            cross_o,
            whole[6:9],
            up_grad,
            mine[4 * per :],
            down_grad,
        )

    return shards


def solution(mesh):
    placed = (
        P("dp", None, None),
        P("dp", None, None),
        P("dp"),
        P("dp"),
        P("dp", None, None),
        P(),
        P(),
        P(None, None, "mp"),
        P(None, "mp"),
        P("mp", None),
        P(None, "mp"),
        P(None, None, "mp"),
        P(None, "mp"),
        P("mp", None),
        P(),
        P(None, "mp"),
        P("mp"),
        P("mp", None),
    )
    return jax.shard_map(
        build(mesh.shape["dp"], mesh.shape["mp"]),
        mesh=mesh,
        in_specs=placed,
        out_specs=(
            P("dp", None, None),
            P("dp", None, None),
            P("dp", None, None),
            P(),
            P(),
            P(None, None, "mp"),
            P(None, "mp"),
            P("mp", None),
            P(None, "mp"),
            P(None, None, "mp"),
            P(None, "mp"),
            P("mp", None),
            P(),
            P(None, "mp"),
            P("mp"),
            P("mp", None),
        ),
        check_vma=False,
    )
```

```python
import functools

import jax
import jax.numpy as jnp
from jax import lax
from jax.experimental import pallas as pl
from jax.experimental.pallas import tpu as pltpu
from jax.sharding import PartitionSpec as P

neg_fill = -1000000000.0
open_cap = 3e38
eps_norm = 1e-05
PAIR = 128
HALF = 64
QUERY_SCALE = 0.125
ROOT = 0.7978845608028654
CUBE = 0.044715
f32 = jnp.float32
bf16 = jnp.bfloat16
ROW, FIRST, SECOND, TARGET, SOURCE, PLANE, CORE = range(7)


def low(value):
    return value.astype(bf16)


def nn(left, right):
    return lax.dot_general(left, right, (((1,), (0,)), ((), ())), preferred_element_type=f32)


def nt(left, right):
    return lax.dot_general(left, right, (((1,), (1,)), ((), ())), preferred_element_type=f32)


def tn(left, right):
    return lax.dot_general(left, right, (((0,), (0,)), ((), ())), preferred_element_type=f32)


def after(value, *others):
    return lax.optimization_barrier((value,) + others)[0]


def wall(*values):
    return lax.optimization_barrier(values)


def call(kernel, info, grid, ins, outs, scratch=(), micros=1.0):
    return pl.pallas_call(
        kernel,
        out_shape=tuple(jax.ShapeDtypeStruct(s, t) for s, t, _, _ in outs),
        grid_spec=pltpu.PrefetchScalarGridSpec(
            num_scalar_prefetch=1,
            grid=grid,
            in_specs=[pl.BlockSpec(b, m) for _, b, m in ins],
            out_specs=tuple(pl.BlockSpec(b, m) for _, _, b, m in outs),
            scratch_shapes=list(scratch),
        ),
        compiler_params=pltpu.CompilerParams(vmem_limit_bytes=52 << 20),
        cost_estimate=pl.CostEstimate(flops=int(micros * 1e7), bytes_accessed=1 << 10, transcendentals=0),
    )(info, *(a for a, _, _ in ins))


def rows_of_eight(values):
    return jnp.sum(values.reshape(values.shape[0] // 8, 8, values.shape[1]), axis=0)


def norm_stats(values):
    centre = jnp.mean(values, axis=-1, keepdims=True)
    offset = values - centre
    spread = jnp.mean(offset * offset, axis=-1, keepdims=True)
    scale = lax.rsqrt(spread + eps_norm)
    return offset * scale, scale


def norm_back(values, gain, grad):
    hat, scale = norm_stats(values)
    scaled = grad * gain
    mean_one = jnp.mean(scaled, axis=-1, keepdims=True)
    mean_two = jnp.mean(scaled * hat, axis=-1, keepdims=True)
    return scale * (scaled - mean_one - hat * mean_two), grad * hat


def head_halves(both):
    lane = lax.broadcasted_iota(jnp.int32, both.shape, 1)
    zero = jnp.zeros_like(both)
    return jnp.where(lane < HALF, both, zero), jnp.where(lane < HALF, zero, both)


def fill_caps(info, cap_ref, block, causal):
    length = cap_ref.shape[0]
    for t in range(2):
        keys = lax.broadcasted_iota(jnp.int32, (length, block), 0)
        allowed = keys < info[TARGET if causal else SOURCE]
        if causal:
            places = lax.broadcasted_iota(jnp.int32, (length, block), 1) + info[FIRST + t] * block
            allowed = allowed & (keys <= places)
        cap_ref[:, t * block : (t + 1) * block] = jnp.where(allowed, open_cap, neg_fill)


def forward_kernel(info, q_ref, k_ref, v_ref, o_ref, lse_ref, cap_ref, s_ref, *, block, causal, chunk):
    length = k_ref.shape[0]

    @pl.when(pl.program_id(0) == 0)
    def _():
        fill_caps(info, cap_ref, block, causal)

    for t in (1, 0):
        rows = slice(t * block, (t + 1) * block)
        span = length // 2 if (causal and t == 0) else length
        queries = jnp.concatenate(head_halves(q_ref[rows, :] * bf16(QUERY_SCALE)), axis=0)
        most = jnp.full((8, 2 * block), -open_cap, f32)
        for c in range(0, span, chunk):
            keys = slice(c, c + chunk)
            cap = cap_ref[keys, rows]
            scores = jnp.minimum(nt(k_ref[keys, :], queries), jnp.concatenate([cap, cap], axis=1))
            s_ref[t, keys, :] = scores
            most = jnp.maximum(most, jnp.max(scores.reshape(chunk // 8, 8, 2 * block), axis=0))
        most = jnp.max(most, axis=0, keepdims=True)
        total = jnp.zeros((8, 2 * block), f32)
        mixed = jnp.zeros((PAIR, 2 * block), f32)
        for c in range(0, span, chunk):
            keys = slice(c, c + chunk)
            weights = jnp.exp(s_ref[t, keys, :] - most)
            total = total + rows_of_eight(weights)
            mixed = mixed + tn(v_ref[keys, :], low(weights))
        total = jnp.sum(total, axis=0, keepdims=True)
        mixed = mixed / total
        sub = lax.broadcasted_iota(jnp.int32, (PAIR, block), 0)
        o_ref[rows, :] = low(jnp.where(sub < HALF, mixed[:, :block], mixed[:, block:]).T)
        lse = most + jnp.log(total)
        lse_ref[0, 0:1, rows] = lse[:, :block]
        lse_ref[0, 1:2, rows] = lse[:, block:]


def backward_kernel(
    info, q_ref, k_ref, v_ref, o_ref, g_ref, lse_ref, dq_ref, dk_ref, dv_ref, qs_ref, vs_ref, cap_ref, dk_acc, dv_acc,
    *, block, causal, chunk
):
    length = k_ref.shape[0]

    @pl.when(pl.program_id(0) == 0)
    def _():
        fill_caps(info, cap_ref, block, causal)

    q_sums = jnp.zeros((8, PAIR), f32)
    for t in (1, 0):
        rows = slice(t * block, (t + 1) * block)
        span = length // 2 if (causal and t == 0) else length
        grads = g_ref[rows, :]
        prod = (grads.astype(f32) * o_ref[rows, :].astype(f32)).T
        centre = jnp.concatenate(
            [jnp.sum(prod[:HALF], axis=0, keepdims=True), jnp.sum(prod[HALF:], axis=0, keepdims=True)], axis=1
        )
        lse = jnp.concatenate([lse_ref[0, 0:1, rows], lse_ref[0, 1:2, rows]], axis=1)
        queries = jnp.concatenate(head_halves(q_ref[rows, :] * bf16(QUERY_SCALE)), axis=0)
        grads = jnp.concatenate(head_halves(grads), axis=0)
        dq = jnp.zeros((PAIR, 2 * block), f32)
        for c in range(0, span, chunk):
            keys = slice(c, c + chunk)
            k, v = k_ref[keys, :], v_ref[keys, :]
            cap = cap_ref[keys, rows]
            scores = jnp.minimum(nt(k, queries), jnp.concatenate([cap, cap], axis=1))
            probs = jnp.exp(scores - lse)
            grad_scores = low(probs * (nt(v, grads) - centre))
            dv = nn(low(probs), grads)
            dk = nn(grad_scores, queries)
            dq = dq + tn(k, grad_scores)
            if t == 1:
                dk_acc[keys, :] = dk
                dv_acc[keys, :] = dv
            else:
                dk_acc[keys, :] += dk
                dv_acc[keys, :] += dv
        sub = lax.broadcasted_iota(jnp.int32, (PAIR, block), 0)
        dq = jnp.where(sub < HALF, dq[:, :block], dq[:, block:]) * QUERY_SCALE
        dq = low(dq.T)
        dq_ref[rows, :] = dq
        q_sums = q_sums + rows_of_eight(dq.astype(f32))
    dk_ref[...] = low(dk_acc[...])
    dv = low(dv_acc[...])
    dv_ref[...] = dv
    qs_ref[...] = q_sums
    vs_ref[...] = rows_of_eight(dv.astype(f32))


def attend_forward(info, query, keys, values, causal):
    queries, width = query.shape
    length = keys.shape[0]
    here = lambda i, _: (0, i)
    return call(
        functools.partial(forward_kernel, block=queries // 2, causal=causal, chunk=min(256, length // 2)),
        info,
        (width // PAIR,),
        [(query, (queries, PAIR), here), (keys, (length, PAIR), here), (values, (length, PAIR), here)],
        [
            ((queries, width), bf16, (queries, PAIR), here),
            ((width // PAIR, 8, queries), f32, (1, 8, queries), lambda i, _: (i, 0, 0)),
        ],
        [pltpu.VMEM((length, queries), f32), pltpu.VMEM((2, length, queries), f32)],
        micros=16,
    )


def attend_backward(info, query, keys, values, mixed, grad, lse_rows, causal):
    queries, width = query.shape
    length = keys.shape[0]
    here = lambda i, _: (0, i)
    one, key = (queries, PAIR), (length, PAIR)
    return call(
        functools.partial(backward_kernel, block=queries // 2, causal=causal, chunk=min(256, length // 2)),
        info,
        (width // PAIR,),
        [
            (query, one, here),
            (keys, key, here),
            (values, key, here),
            (mixed, one, here),
            (grad, one, here),
            (lse_rows, (1, 8, queries), lambda i, _: (i, 0, 0)),
        ],
        [
            ((queries, width), bf16, one, here),
            ((length, width), bf16, key, here),
            ((length, width), bf16, key, here),
            ((8, width), f32, (8, PAIR), here),
            ((8, width), f32, (8, PAIR), here),
        ],
        [pltpu.VMEM((length, queries), f32), pltpu.VMEM((length, PAIR), f32), pltpu.VMEM((length, PAIR), f32)],
        micros=24,
    )


def order_kernel(info, same_ref, other_ref, out_ref, *, part_of):
    mine = lax.rem(part_of(pl.program_id(0)), 2) == info[CORE]

    @pl.when(mine)
    def _():
        out_ref[...] = same_ref[...].astype(out_ref.dtype)

    @pl.when(jnp.logical_not(mine))
    def _():
        out_ref[...] = other_ref[...].astype(out_ref.dtype)


def order_rows(info, found, got, rows, group, pieces, kind):
    half, width = got.shape
    steps = group * pieces
    block = half // (rows * steps // 2)

    def part_of(i):
        b = lax.rem(i, steps)
        return jnp.where(b >= group, steps - 1 - b, b)

    def source(i):
        late = (lax.rem(i, steps) >= group).astype(jnp.int32)
        return (lax.div(i, steps) * (group // 2) + lax.div(part_of(i), 2)) * pieces + late

    return call(
        functools.partial(order_kernel, part_of=part_of),
        info,
        (rows * steps,),
        [
            (found, (block, width), lambda i, info: (source(i) + info[CORE] * (half // block), 0)),
            (got, (block, width), lambda i, _: (source(i), 0)),
        ],
        [((2 * half, width), kind, (block, width), lambda i, _: (i, 0))],
        micros=4,
    )[0]


def entry_kernel(info, x_ref, gain_ref, shift_ref, h_ref, *, which):
    hat, _ = norm_stats(x_ref[...].astype(f32))
    one = slice(which, which + 1)
    h_ref[...] = low(hat * gain_ref[one, :].astype(f32) + shift_ref[one, :].astype(f32))


def entry_norm(info, tokens, gains, shifts):
    _, length, width = tokens.shape
    tile = min(256, length)
    whole = lambda i, _: (0, 0)
    return call(
        functools.partial(entry_kernel, which=0),
        info,
        (length // tile,),
        [
            (tokens, (None, tile, width), lambda i, info: (info[ROW], i, 0)),
            (gains, gains.shape, whole),
            (shifts, shifts.shape, whole),
        ],
        [((length, width), bf16, (tile, width), lambda i, _: (i, 0))],
        micros=3,
    )[0]


def weight_ins(weight, slots):
    own, lead, rest, place = weight
    depth = rest.shape[0]
    wide = own.shape[1] * own.shape[2] // depth
    return [
        (own, (None,) + own.shape[1:], lambda *_: (lead, 0, 0)),
        (rest, (depth, (slots - 1) * wide), lambda *_: (0, place)),
    ]


def project_kernel(info, x_ref, own_ref, rest_ref, *others, flipped):
    x = x_ref[...]
    mine = nt(x, own_ref[...]) if flipped else nn(x, own_ref[...])
    wide = mine.shape[1]
    rest = nn(x, rest_ref[...])
    out_ref = others[-1]
    if len(others) > 1:
        mine = mine + others[0][:, :wide]
        rest = rest + others[0][:, wide:]
    out_ref[:, :wide] = low(mine)
    out_ref[:, wide:] = low(rest)


def project(info, x, place_of, tiles, weight, bias, slots, flipped=False):
    count, tile = tiles
    depth = x.shape[2]
    ins = [(x, (None, tile, depth), lambda i, info: place_of(i, info) + (0,))] + weight_ins(weight, slots)
    own = weight[0]
    width = slots * (own.shape[1] * own.shape[2] // depth)
    if bias is not None:
        ins.append((bias, bias.shape, lambda i, _: (0, 0)))
    return call(
        functools.partial(project_kernel, flipped=flipped),
        info,
        (count,),
        ins,
        [((count * tile, width), bf16, (tile, width), lambda i, _: (i, 0))],
        micros=2.5 * count * tile / 1024,
    )[0]


def mix_kernel(info, x_ref, own_ref, rest_ref, resid_ref, bias_ref, gain_ref, shift_ref, sum_ref, h_ref, *, which):
    wide = own_ref.shape[0]
    found = nn(x_ref[:, :wide], own_ref[...]) + nt(x_ref[:, wide:], rest_ref[...])
    found = resid_ref[...].astype(f32) + found + bias_ref[which : which + 1, :].astype(f32)
    sum_ref[...] = found
    hat, _ = norm_stats(found)
    one = slice(which + 1, which + 2)
    h_ref[...] = low(hat * gain_ref[one, :].astype(f32) + shift_ref[one, :].astype(f32))


def mix(info, x, weight, resid, resid_place, biases, gains, shifts, which, slots):
    rows, width = x.shape
    block = rows // 2
    whole = lambda i, _: (0, 0)
    here = lambda i, _: (i, 0)
    depth = resid.shape[2]
    return call(
        functools.partial(mix_kernel, which=which),
        info,
        (2,),
        [(x, (block, width), here)]
        + weight_ins(weight, slots)
        + [
            (resid, (None, block, depth), lambda i, info: resid_place(i, info) + (0,)),
            (biases, biases.shape, whole),
            (gains, gains.shape, whole),
            (shifts, shifts.shape, whole),
        ],
        [((rows, depth), f32, (block, depth), here), ((rows, depth), bf16, (block, depth), here)],
        micros=4,
    )


def back_dots(pairs):
    total = None
    for x_ref, own_ref, rest_ref in pairs:
        wide = own_ref.shape[1]
        found = nt(x_ref[:, :wide], own_ref[...]) + nt(x_ref[:, wide:], rest_ref[...])
        total = found if total is None else total + found
    return total


def back_kernel(info, *refs, count):
    pairs = [refs[3 * j : 3 * j + 3] for j in range(count)]
    refs[-1][...] = low(back_dots(pairs))


def back(info, terms, slots):
    rows, width = terms[0][0].shape
    depth = terms[0][1][2].shape[0]
    tile = min(256, rows)
    ins = []
    for x, weight in terms:
        ins += [(x, (tile, width), lambda i, _: (i, 0))] + weight_ins(weight, slots)
    return call(
        functools.partial(back_kernel, count=len(terms)),
        info,
        (rows // tile,),
        ins,
        [((rows, depth), bf16, (tile, depth), lambda i, _: (i, 0))],
        micros=5,
    )[0]


def back_norm_kernel(info, *refs, extras, which, keep):
    x_ref, own_ref, rest_ref = refs[:3]
    extra = refs[3 : 3 + extras]
    v_ref, add_ref, gain_ref = refs[3 + extras : 6 + extras]
    outs = refs[6 + extras :]
    grad = back_dots([(x_ref, own_ref, rest_ref)])
    for e in extra:
        grad = grad + e[...].astype(f32)
    found, to_gain = norm_back(v_ref[...].astype(f32), gain_ref[which : which + 1, :].astype(f32), grad)
    found = add_ref[...] + found
    low_found = low(found)
    if keep:
        outs[0][...] = found
    outs[-2][...] = low_found
    sums = jnp.concatenate([rows_of_eight(to_gain), rows_of_eight(grad), rows_of_eight(low_found.astype(f32))])

    @pl.when(pl.program_id(0) == 0)
    def _():
        outs[-1][...] = sums

    @pl.when(pl.program_id(0) > 0)
    def _():
        outs[-1][...] += sums


def back_norm(info, x, weight, extras, values, values_place, add, gains, which, slots, keep):
    rows, width = x.shape
    block = rows // 2
    depth = add.shape[1]
    here = lambda i, _: (i, 0)
    whole = lambda i, _: (0, 0)
    one = (block, depth)
    outs = [((rows, depth), bf16, one, here), ((24, depth), f32, (24, depth), whole)]
    if keep:
        outs = [((rows, depth), f32, one, here)] + outs
    return call(
        functools.partial(back_norm_kernel, extras=len(extras), which=which, keep=keep),
        info,
        (2,),
        [(x, (block, width), here)]
        + weight_ins(weight, slots)
        + [(e, one, here) for e in extras]
        + [
            (values, (None, block, depth), lambda i, info: values_place(i, info) + (0,)),
            (add, one, here),
            (gains, gains.shape, whole),
        ],
        outs,
        micros=4,
    )


def feed_kernel(
    info, h_ref, c0_ref, c1_ref, second_ref, upo_ref, downo_ref, upr_ref, downr_ref, ub_ref, bias_ref, gain_ref,
    a_ref, du_ref, us_ref, final_ref, g_ref, e_ref, sums_ref, out_acc, dh_acc, *, own_tiles
):
    i = pl.program_id(0)
    block = c0_ref.shape[0]
    cots = (c0_ref, c1_ref)
    which = 2

    def tile(own):
        sums = None
        for t in range(2):
            rows = slice(t * block, (t + 1) * block)
            up = upo_ref[...] if own else upr_ref[...]
            pre = nn(h_ref[rows, :], up) + ub_ref[...]
            square = pre * pre
            curve = jnp.tanh(ROOT * (pre + CUBE * square * pre))
            act = low(0.5 * pre * (1.0 + curve))
            slope = 0.5 * (1.0 + curve) + 0.5 * pre * (1.0 - curve * curve) * (ROOT * (1.0 + 3.0 * CUBE * square))
            a_ref[rows, :] = act
            if own:
                grad = nt(cots[t][...], downo_ref[...])
                out = nn(act, downo_ref[...])
            else:
                grad = nn(cots[t][...], downr_ref[...])
                out = nt(act, downr_ref[...])
            du = low(slope * grad)
            du_ref[rows, :] = du
            part = rows_of_eight(du.astype(f32))
            sums = part if sums is None else sums + part
            dh = nt(du, up)
            first = i == 0
            if own:

                @pl.when(first)
                def _():
                    out_acc[rows, :] = out
                    dh_acc[rows, :] = dh

                @pl.when(jnp.logical_not(first))
                def _():
                    out_acc[rows, :] += out
                    dh_acc[rows, :] += dh
            else:
                out_acc[rows, :] += out
                dh_acc[rows, :] += dh
        us_ref[...] = sums

    @pl.when(i < own_tiles)
    def _():
        tile(True)

    @pl.when(i >= own_tiles)
    def _():
        tile(False)

    @pl.when(i == pl.num_programs(0) - 1)
    def _():
        sums = None
        gain = gain_ref[which : which + 1, :].astype(f32)
        for t in range(2):
            rows = slice(t * block, (t + 1) * block)
            second = second_ref[rows, :]
            final_ref[rows, :] = low(second + out_acc[rows, :] + bias_ref[which : which + 1, :].astype(f32))
            cot = cots[t][...].astype(f32)
            grad = dh_acc[rows, :]
            found, to_gain = norm_back(second, gain, grad)
            found = cot + found
            g_ref[rows, :] = found
            rounded = low(found)
            e_ref[rows, :] = rounded
            part = jnp.concatenate(
                [
                    rows_of_eight(to_gain),
                    rows_of_eight(grad),
                    rows_of_eight(rounded.astype(f32)),
                    rows_of_eight(cot),
                ]
            )
            sums = part if sums is None else sums + part
        sums_ref[...] = sums


def feed_forward(info, h, cotangent, second, up, down, up_bias, biases, gains, slots):
    rows, depth = h.shape
    block = rows // 2
    up_own, _, up_rest, up_place = up
    down_own, _, down_rest, down_place = down
    hidden = up_own.shape[2]
    tile = min(512, hidden)
    own_tiles = hidden // tile
    total = slots * own_tiles
    rest_tiles = (slots - 1) * own_tiles
    own_at = lambda i: jnp.minimum(i, own_tiles - 1)
    rest_at = lambda i: jnp.maximum(i - own_tiles, 0)
    whole = lambda i, _: (0, 0)
    full = (rows, depth)
    return call(
        functools.partial(feed_kernel, own_tiles=own_tiles),
        info,
        (total,),
        [
            (h, full, whole),
            (cotangent, (None, block, depth), lambda i, _: (0, 0, 0)),
            (cotangent, (None, block, depth), lambda i, _: (0, 1, 0)),
            (second, full, whole),
            (up_own, (None, depth, tile), lambda i, _: (0, 0, own_at(i))),
            (down_own, (None, tile, depth), lambda i, _: (0, own_at(i), 0)),
            (up_rest, (depth, tile), lambda i, _: (0, up_place * rest_tiles + rest_at(i))),
            (down_rest, (depth, tile), lambda i, _: (0, down_place * rest_tiles + rest_at(i))),
            (up_bias, (1, tile), lambda i, _: (0, i)),
            (biases, biases.shape, whole),
            (gains, gains.shape, whole),
        ],
        [
            ((rows, total * tile), bf16, (rows, tile), lambda i, _: (0, i)),
            ((rows, total * tile), bf16, (rows, tile), lambda i, _: (0, i)),
            ((8, total * tile), f32, (8, tile), lambda i, _: (0, i)),
            (full, bf16, full, whole),
            (full, f32, full, whole),
            (full, bf16, full, whole),
            ((32, depth), f32, (32, depth), whole),
        ],
        [pltpu.VMEM(full, f32), pltpu.VMEM(full, f32)],
        micros=32,
    )


def grad_kernel(info, *refs, plan, share, plane, mine):
    acts = refs[: sum(len(pieces) for pieces, _ in plan)]
    refs = refs[len(acts) :]
    grads = refs[: len(plan)]
    refs = refs[len(plan) :]
    got_ref = None
    if mine:
        got_ref, refs = refs[0], refs[1:]
    outs, turned = refs[: plane if mine else 1], refs[-len(plan) :]
    core = info[CORE] if mine else 1 - info[CORE]

    @pl.when(pl.program_id(0) == 0)
    def _():
        at = 0
        for t, (pieces, _) in enumerate(plan):
            start = 0
            for length in pieces:
                for r in range(plane):
                    if share % PAIR == 0:
                        block = 2 * jnp.bitwise_xor(info[PLANE], r) + core
                        cols = acts[at][:, pl.ds(pl.multiple_of(block * share, share), share)]
                    else:
                        cols = acts[at][:, r * share : (r + 1) * share]
                    turned[t][r * share : (r + 1) * share, start : start + length] = cols.T
                start += length
                at += 1

    first = 0
    for t, (_, wide) in enumerate(plan):
        cols = slice(first, first + wide)
        found = nn(turned[t][...], grads[t][...])
        if mine:
            found = low(found + got_ref[:, cols].astype(f32))
            for r in range(plane):
                outs[r][:, cols] = found[r * share : (r + 1) * share, :]
        else:
            outs[0][:, cols] = low(found)
        first += wide


def weight_grads(info, tensors, d, dp_size, slots, got=None):
    depth = tensors[0][0][0][0].shape[2]
    share, plane = depth // dp_size, dp_size // 2
    core = lax.rem(d, 2) if got is not None else 1 - lax.rem(d, 2)
    plan = [(tuple(rows for _, rows, _ in pieces), grad.shape[1] // slots) for pieces, grad in tensors]
    ins = []
    for pieces, _ in tensors:
        for array, rows, place in pieces:
            if share % PAIR == 0:
                ins.append((array, (None, rows, depth), lambda i, info, place=place: place(info) + (0,)))
            else:
                wide = array.reshape(array.shape[:2] + (plane, 2, share))
                wide = lax.dynamic_index_in_dim(wide, core, 3, keepdims=False)
                order = [jnp.bitwise_xor(d // 2, r) for r in range(plane)]
                wide = jnp.concatenate([lax.dynamic_index_in_dim(wide, b, 2) for b in order], axis=2)
                wide = wide.reshape(array.shape[:2] + (depth // 2,))
                ins.append((wide, (None, rows, depth // 2), lambda i, info, place=place: place(info) + (0,)))
    for (_, grad), (_, wide) in zip(tensors, plan):
        ins.append((grad, (grad.shape[0], wide), lambda i, _: (0, i)))
    half = depth // 2
    tile = sum(wide for _, wide in plan)
    if got is not None:
        ins.append((got, (half, tile), lambda i, _: (0, i)))
        outs = [((share, slots * tile), bf16, (share, tile), lambda i, _: (0, i))] * plane
    else:
        outs = [((half, slots * tile), bf16, (half, tile), lambda i, _: (0, i))]
    return call(
        functools.partial(grad_kernel, plan=plan, share=share, plane=plane, mine=got is not None),
        info,
        (slots,),
        ins,
        outs,
        [pltpu.VMEM((half, g.shape[0]), bf16) for _, g in tensors],
        micros=8,
    )


def finish_kernel(info, in_ref, out_ref, *, turn):
    value = in_ref[...].astype(f32)
    out_ref[...] = value.T if turn else value


def finish(info, full, places, wide, turn=False):
    depth = full.shape[0]
    first = places[0]
    if turn:
        tile, cut = min(256, depth), min(512, wide)
        return call(
            functools.partial(finish_kernel, turn=True),
            info,
            (depth // tile, wide // cut),
            [(full, (tile, cut), lambda i, j, _: (i, first * (wide // cut) + j))],
            [((wide, depth), f32, (cut, tile), lambda i, j, _: (j, i))],
            micros=3,
        )[0]
    tile = min(512, depth)
    return call(
        functools.partial(finish_kernel, turn=False),
        info,
        (len(places), depth // tile),
        [(full, (tile, wide), lambda i, j, _: (j, first + i))],
        [((len(places), depth, wide), f32, (None, tile, wide), lambda i, j, _: (i, j, 0))],
        micros=3,
    )[0]


def finish_pair_kernel(info, in_ref, q_ref, kv_ref, o_ref, s_ref, so_ref):
    wide = q_ref.shape[1]

    def cols(t):
        return in_ref[:, t * wide : (t + 1) * wide].astype(f32)

    q_ref[...] = cols(0)
    for t in range(2):
        kv_ref[t] = cols(1 + t)
    o_ref[...] = cols(3).T
    for t in range(3):
        s_ref[t] = cols(4 + t)
    so_ref[...] = cols(7).T


def finish_pair(info, full):
    depth = full.shape[0]
    wide = full.shape[1] // 8
    tile = min(256, depth)
    return call(
        finish_pair_kernel,
        info,
        (depth // tile,),
        [(full, (tile, 8 * wide), lambda i, _: (i, 0))],
        [
            ((depth, wide), f32, (tile, wide), lambda i, _: (i, 0)),
            ((2, depth, wide), f32, (2, tile, wide), lambda i, _: (0, i, 0)),
            ((wide, depth), f32, (wide, tile), lambda i, _: (0, i)),
            ((3, depth, wide), f32, (3, tile, wide), lambda i, _: (0, i, 0)),
            ((wide, depth), f32, (wide, tile), lambda i, _: (0, i)),
        ],
        micros=4,
    )


def build(dp_size, mp_size):
    ring = [(i, (i + 1) % mp_size) for i in range(mp_size)]
    back_ring = [(i, (i - 1) % mp_size) for i in range(mp_size)]
    dp_bits = dp_size.bit_length() - 1
    plane = dp_size // 2

    def flip(axis, size, bits):
        return lambda value: lax.ppermute(value, axis, [(i, i ^ bits) for i in range(size)])

    def shards(
        tokens,
        memory,
        target_lengths,
        source_lengths,
        cotangent,
        norm_gain,
        norm_bias,
        self_in,
        self_in_bias,
        self_out,
        cross_query,
        cross_kv,
        cross_bias,
        cross_out,
        out_bias,
        ffn_up,
        ffn_up_bias,
        ffn_down,
    ):
        rows, length, width = tokens.shape
        source = memory.shape[1]
        d = lax.axis_index("dp")
        z = lax.axis_index("mp")
        group = mp_size // rows
        core = lax.rem(d, 2)
        chips = group // 2
        chip_row = z // chips
        part = (z % chips) * 2 + core
        held = chip_row // rows == core
        row = lax.rem(chip_row, rows)
        block = length // (2 * group)
        share = width // dp_size
        per = width // mp_size
        hid = ffn_up.shape[1]
        swap = flip("dp", dp_size, 1)

        def take_row(values):
            return lax.dynamic_index_in_dim(values, row, 0, keepdims=False)

        def blocks_of(values, p):
            return jnp.concatenate(
                [
                    lax.dynamic_slice_in_dim(values, s * block, block, 0)
                    for s in (p, 2 * group - 1 - p)
                ]
            )

        own_place = lambda i, info: (info[ROW], info[FIRST + i])
        own_h_place = lambda i, info: (0, info[FIRST + i])
        flat_place = lambda i, info: (0, i)
        row_place = lambda i, info: (info[ROW], i)

        def rows_of(weight):
            return lax.dynamic_slice_in_dim(weight, d * share, share, 0)

        def cols_of(weight):
            return lax.dynamic_slice_in_dim(weight, d * share, share, 1).T

        def with_bias(piece, bias):
            extra = jnp.zeros((16, piece.shape[1]), bf16)
            if bias is not None:
                extra = lax.dynamic_update_slice(extra, bias[None], (0, 0))
            return jnp.concatenate([piece, extra])

        def side_by_side(pieces):
            return jnp.concatenate([with_bias(p, b) for p, b in pieces], axis=1)

        def pass_on(value):
            return lax.ppermute(value, "mp", ring)

        def gather_rest(found, wides, *held):
            starts = [0]
            for w in wides:
                starts.append(starts[-1] + w)
            both = jnp.concatenate([s[:, a:b] for a, b in zip(starts[:-1], starts[1:]) for s in found], axis=1)
            ours = both[:share]
            if held:
                ours = after(ours, *held)
            return lax.all_gather(ours, "dp", axis=0, tiled=True), both[share : share + 1].astype(f32)

        def bias_of(own, biases, t, wide):
            far = (mp_size - 1) * wide
            return jnp.concatenate([own.astype(f32)[None], biases[:, t * far : (t + 1) * far]], axis=1)

        def row_of(mine, theirs, cut=lambda values: values):
            return jnp.where(held, cut(take_row(mine)), cut(take_row(theirs)))[None]

        lengths = jnp.stack([target_lengths, source_lengths])
        lengths = jnp.where(held, lengths, swap(lengths))
        lengths = lax.dynamic_index_in_dim(lengths, row, 1, keepdims=False)
        info = jnp.stack(
            [0 * part, part, 2 * group - 1 - part, lengths[0], lengths[1], d // 2, core]
        ).astype(jnp.int32)
        found_a = [
            pass_on(
                side_by_side(
                    [
                        (rows_of(self_in[0]), self_in_bias[0]),
                        (rows_of(self_in[1]), None),
                        (rows_of(self_in[2]), self_in_bias[1]),
                    ]
                )
            )
        ]
        for _ in range(mp_size - 3):
            found_a.append(pass_on(found_a[-1]))
        found_a[-1], tokens_got, info = wall(found_a[-1], swap(tokens), info)
        found_a.append(pass_on(found_a[-1]))
        tokens_row = row_of(tokens, tokens_got)
        share_b = side_by_side(
            [
                (cols_of(self_out), None),
                (rows_of(cross_query), cross_bias[0]),
                (rows_of(cross_kv[0]), None),
                (rows_of(cross_kv[1]), cross_bias[1]),
            ]
        )
        share_c = side_by_side(
            [(rows_of(ffn_up), ffn_up_bias), (cols_of(ffn_down), None), (cols_of(cross_out), None)]
        )
        found_a[-1], tokens_row, share_b, share_c = wall(found_a[-1], tokens_row, share_b, share_c)
        found_b = [pass_on(share_b)]
        h1_row = entry_norm(info, tokens_row, norm_gain, norm_bias)
        found_b[0], h1_row = wall(found_b[0], h1_row)
        for _ in range(mp_size - 3):
            found_b.append(pass_on(found_b[-1]))
        found_b[-1], memory_got = wall(found_b[-1], swap(memory))
        found_b.append(pass_on(found_b[-1]))
        memory_row = row_of(memory, memory_got)
        found_b[-1], memory_row = wall(found_b[-1], memory_row)
        rest_a, bias_a = gather_rest(found_a, [per] * 3)
        rest_b, bias_b = gather_rest(found_b, [per] * 4)
        w_q1, w_k1, w_v1 = [(self_in, t, rest_a, t) for t in range(3)]
        w_o1 = (self_out[None], 0, rest_b, 0)
        w_q2 = (cross_query[None], 0, rest_b, 1)
        w_k2, w_v2 = (cross_kv, 0, rest_b, 2), (cross_kv, 1, rest_b, 3)

        found_c = [pass_on(after(share_c, found_b[-1]))]
        for _ in range(mp_size - 3):
            found_c.append(pass_on(found_c[-1]))
        far = min(256, length)
        h1_flat = h1_row[None]
        k1 = project(info, h1_flat, flat_place, (length // far, far), w_k1, None, mp_size)
        found_c[-1], k1, h1_flat = wall(found_c[-1], k1, h1_flat)
        found_c.append(pass_on(found_c[-1]))
        v1 = project(
            info, h1_flat, flat_place, (length // far, far), w_v1, bias_of(self_in_bias[1], bias_a, 2, per), mp_size
        )
        q1 = project(info, h1_flat, own_h_place, (2, block), w_q1, bias_of(self_in_bias[0], bias_a, 0, per), mp_size)
        cot_own = row_of(cotangent, swap(cotangent), lambda values: blocks_of(values, part))
        found_c[-1], v1, q1 = wall(found_c[-1], v1, q1)
        rest_c, bias_c = gather_rest(found_c, [hid, hid, per])
        w_up, w_down = (ffn_up[None], 0, rest_c, 0), (ffn_down[None], 0, rest_c, 1)
        w_o2 = (cross_out[None], 0, rest_c, 2 * hid // per)
        o1, lse1 = attend_forward(info, q1, k1, v1, True)
        first, h2 = mix(info, o1, w_o1, tokens_row, own_place, out_bias, norm_gain, norm_bias, 0, mp_size)
        q2 = project(info, h2[None], flat_place, (2, block), w_q2, bias_of(cross_bias[0], bias_b, 1, per), mp_size)
        k2 = project(info, memory_row, row_place, (source // far, far), w_k2, None, mp_size)
        v2 = project(
            info, memory_row, row_place, (source // far, far), w_v2, bias_of(cross_bias[1], bias_b, 3, per), mp_size
        )
        o2, lse2 = attend_forward(info, q2, k2, v2, False)
        second, h3 = mix(info, o2, w_o2, first[None], flat_place, out_bias, norm_gain, norm_bias, 1, mp_size)
        hidden, grad_pre, up_sums, final, g2, e2, sums_three = feed_forward(
            info, h3, cot_own, second, w_up, w_down, bias_of(ffn_up_bias, bias_c, 0, hid), out_bias, norm_gain, mp_size
        )

        def to_plane(piece, r):
            return flip("dp", dp_size, 2 * r)(piece)

        def slots_of(total, count=mp_size):
            wide = total[0].shape[1] // count
            slots = []
            for k in range(count):
                cols = slice(k * wide, (k + 1) * wide)
                slots.append(low(sum(t[:, cols].astype(f32) for t in total)))
            return slots

        def to_owners(slots):
            return [
                lax.ppermute(slots[k], "mp", [(i, (i - k) % mp_size) for i in range(mp_size)])
                for k in range(1, mp_size)
            ]

        def add_up(values):
            return low(sum(v.astype(f32) for v in values))

        def gather_grads(total):
            return lax.all_gather(total, "dp", axis=0, tiled=True)

        def gather_rows(mine):
            return lax.all_gather(mine, "mp", axis=0, tiled=True)

        def for_other(found):
            half = found.shape[0] // 2
            return swap(lax.dynamic_slice_in_dim(found, (1 - core) * half, half, 0))

        def own_blocks(array, lead):
            return [
                (array, block, lambda info, t=t: ((info[ROW] if lead else 0), info[FIRST + t])) for t in range(2)
            ]

        def all_rows(array, lead=False):
            return [(array, array.shape[1], lambda info: ((info[ROW] if lead else 0), 0))]

        def core_send(tensors):
            return weight_grads(info, tensors, d, dp_size, mp_size)[0]

        def to_core(sent):
            return flip("dp", dp_size, 1)(sent)

        def core_keep(tensors, got):
            return weight_grads(info, tensors, d, dp_size, mp_size, got)

        row_perm = [(i, (i // chips) * chips + (i % chips - 1) % chips) for i in range(mp_size)]

        def row_sum(piece_of):
            got = [swap(piece_of(2 * c + 1 - core)) for c in range(chips)]
            if chips == 1:
                return got[0], piece_of(part)
            pieces = jnp.stack([add_up([got[c], piece_of(2 * c + core)]) for c in range(chips)])
            place = z % chips
            total = lax.dynamic_index_in_dim(pieces, lax.rem(place + 1, chips), 0, keepdims=False)
            for k in range(chips - 2, -1, -1):
                total = lax.ppermute(total, "mp", row_perm)
                here = lax.dynamic_index_in_dim(pieces, lax.rem(place - k + chips, chips), 0, keepdims=False)
                if k:
                    total = add_up([total, here])
            return total, here

        def all_planes(kept):
            return [kept[0]] + [to_plane(kept[r], r) for r in range(1, plane)]

        output_found = gather_rows(final)
        ffn_tensors = [(all_rows(h3[None]), grad_pre), (all_rows(cot_own), hidden)]
        ffn_sent = core_send(ffn_tensors)
        e2, ffn_sent = wall(e2, ffn_sent)

        ffn_got = to_core(ffn_sent)
        do2 = project(info, e2[None], flat_place, (2, block), w_o2, None, mp_size, flipped=True)
        dq2, dk2, dv2, sum_q2, sum_v2 = attend_backward(info, q2, k2, v2, o2, do2, lse2, False)
        memory_part = back(info, [(dk2, w_k2), (dv2, w_v2)], mp_size)

        def memory_piece(p):
            return lax.dynamic_slice_in_dim(memory_part, p * (source // group), source // group, 0)

        ffn_got, memory_part, dq2 = wall(ffn_got, memory_part, dq2)
        memory_got, memory_here = row_sum(memory_piece)
        ffn_kept = core_keep(ffn_tensors, ffn_got)
        memory_got, dq2, *ffn_kept = wall(memory_got, dq2, *ffn_kept)
        memory_own = add_up([memory_got, memory_here])
        memory_found = gather_rows(memory_own)
        memory_own, dq2 = wall(memory_own, dq2)

        late = plane - 1
        ffn_total = [ffn_kept[0]] + [to_plane(ffn_kept[r], r) for r in range(1, late)]
        g1, e1, sums_two = back_norm(
            info, dq2, w_q2, [], first[None], flat_place, g2, norm_gain, 1, mp_size, True
        )
        cross_tensors = [
            (all_rows(h2[None]), dq2),
            (all_rows(memory_row), dk2),
            (all_rows(memory_row), dv2),
            (all_rows(e2[None]), o2),
        ]
        cross_sent = core_send(cross_tensors)
        cross_got = to_core(cross_sent)
        e1 = after(e1, cross_sent)
        do1 = project(info, e1[None], flat_place, (2, block), w_o1, None, mp_size, flipped=True)
        dq1, dk1, dv1, sum_q1, sum_v1 = attend_backward(info, q1, k1, v1, o1, do1, lse1, True)
        kv_part = back(info, [(dk1, w_k1), (dv1, w_v1)], mp_size)
        wide = ffn_kept[late].shape[1] // 2
        last_one, last_two = ffn_kept[late][:, :wide], ffn_kept[late][:, wide:]
        kv_part, cross_got, last_one, last_two, *ffn_total = wall(kv_part, cross_got, last_one, last_two, *ffn_total)

        def causal_piece(p):
            return blocks_of(kv_part, p)

        last_two = to_plane(last_two, late)
        got, here = row_sum(causal_piece)
        cross_kept = core_keep(cross_tensors, cross_got)
        self_tensors = [
            (own_blocks(h1_flat, False), dq1),
            (all_rows(h1_flat), dk1),
            (all_rows(h1_flat), dv1),
            (all_rows(e1[None]), o1),
        ]
        self_sent = core_send(self_tensors)
        output_got = for_other(output_found)
        got, self_sent, output_got, last_one, last_two, *cross_kept = wall(
            got, self_sent, output_got, last_one, last_two, *cross_kept
        )
        last_one = to_plane(last_one, late)
        cross_total = all_planes(cross_kept)
        self_got = to_core(self_sent)
        tokens_own, sums_one = back_norm(
            info, dq1, w_q1, [got, here], tokens_row, own_place, g1, norm_gain, 0, mp_size, False
        )
        tokens_found = gather_rows(tokens_own)

        def by_slot(sums):
            return jnp.sum(sums, axis=0).reshape(mp_size, -1)

        slot_sums = jnp.concatenate([by_slot(s) for s in (sum_q1, sum_v1, sum_q2, sum_v2, up_sums)], axis=1)
        flipped = slot_sums[::-1]
        twice = jnp.concatenate([flipped, flipped])
        in_order = lax.dynamic_slice_in_dim(twice, mp_size - 1 - z, mp_size, 0)
        whole = [
            jnp.sum(sums.reshape(-1, 8, width), axis=1) for sums in (sums_one, sums_two, sums_three)
        ]
        whole = jnp.concatenate(
            [w[0:1] for w in whole] + [w[1:2] for w in whole] + [whole[1][2:3], whole[2][2:3], whole[2][3:4]]
        )
        small = jnp.concatenate([in_order.reshape(-1, PAIR), whole.reshape(-1, PAIR)])
        small_steps = [("dp", dp_size, 1 << b) for b in range(dp_bits)]
        small_steps += [("mp", mp_size, 1 << b) for b in range(mp_size.bit_length() - 1)]

        self_got, tokens_own = wall(self_got, tokens_own)
        self_kept = core_keep(self_tensors, self_got)
        last_one, *self_kept = wall(last_one, *self_kept)
        self_total = all_planes(self_kept)
        ffn_slots = slots_of([t[:, :wide] for t in ffn_total] + [last_one], mp_size // 2)
        ffn_slots += slots_of([t[:, wide:] for t in ffn_total] + [last_two], mp_size // 2)
        output = order_rows(info, output_found, output_got, rows, group, 2, bf16).reshape(tokens.shape)
        output, small, *ffn_slots = wall(output, small, *ffn_slots)

        def ring_start(slots):
            return lax.ppermute(slots[mp_size - 1], "mp", back_ring)

        def ring_next(slots, k, state):
            return lax.ppermute(add_up([slots[k], state]), "mp", back_ring)

        ffn_state = ring_start(ffn_slots)
        memory_got = for_other(memory_found)
        memory_got, small, ffn_state, *cross_total = wall(memory_got, small, ffn_state, *cross_total)
        for k in range(mp_size - 2, 1, -1):
            ffn_state = ring_next(ffn_slots, k, ffn_state)
        cross_slots = slots_of(cross_total)
        cross_state = ring_start(cross_slots)
        memory_grad = order_rows(info, memory_found, memory_got, rows, group, 1, f32).reshape(memory.shape)
        memory_grad, small, ffn_state, cross_state = wall(memory_grad, small, ffn_state, cross_state)
        ffn_state = ring_next(ffn_slots, 1, ffn_state)
        for k in range(mp_size - 2, 1, -1):
            cross_state = ring_next(cross_slots, k, cross_state)
        ffn_state, small, cross_state, *self_total = wall(ffn_state, small, cross_state, *self_total)
        ffn_full = gather_grads(add_up([ffn_slots[0], ffn_state]))
        cross_state = ring_next(cross_slots, 1, cross_state)
        self_slots = slots_of(self_total)
        self_total = [self_slots[0]] + to_owners(self_slots)
        tokens_got = for_other(tokens_found)
        tokens_grad = order_rows(info, tokens_found, tokens_got, rows, group, 2, f32).reshape(tokens.shape)
        tokens_grad, small, cross_state, *self_total = wall(tokens_grad, small, cross_state, *self_total)
        for step in small_steps:
            small = small + flip(*step)(small)
        joint = jnp.concatenate([add_up([cross_slots[0], cross_state]), add_up(self_total)], axis=1)
        joint_full = gather_grads(joint)
        up_grad, down_grad = finish(info, ffn_full, [0], hid)[0], finish(info, ffn_full, [1], hid, True)
        small = small.reshape(-1)
        slot_part = small[: in_order.size].reshape(in_order.shape)
        mine = lax.dynamic_index_in_dim(slot_part, z, 0, keepdims=False)
        whole = small[in_order.size :].reshape(9, width)
        cross_q, cross_both, cross_o, self_three, self_o = finish_pair(after(info, up_grad, down_grad), joint_full)
        return (
            output,
            tokens_grad,
            memory_grad,
            whole[0:3],
            whole[3:6],
            self_three,
            jnp.stack([mine[:per], mine[per : 2 * per]]),
            self_o,
            cross_q,
            cross_both,
            jnp.stack([mine[2 * per : 3 * per], mine[3 * per : 4 * per]]),
            cross_o,
            whole[6:9],
            up_grad,
            mine[4 * per :],
            down_grad,
        )

    return shards


def solution(mesh):
    placed = (
        P("dp", None, None),
        P("dp", None, None),
        P("dp"),
        P("dp"),
        P("dp", None, None),
        P(),
        P(),
        P(None, None, "mp"),
        P(None, "mp"),
        P("mp", None),
        P(None, "mp"),
        P(None, None, "mp"),
        P(None, "mp"),
        P("mp", None),
        P(),
        P(None, "mp"),
        P("mp"),
        P("mp", None),
    )
    return jax.shard_map(
        build(mesh.shape["dp"], mesh.shape["mp"]),
        mesh=mesh,
        in_specs=placed,
        out_specs=(
            P("dp", None, None),
            P("dp", None, None),
            P("dp", None, None),
            P(),
            P(),
            P(None, None, "mp"),
            P(None, "mp"),
            P("mp", None),
            P(None, "mp"),
            P(None, None, "mp"),
            P(None, "mp"),
            P("mp", None),
            P(),
            P(None, "mp"),
            P("mp"),
            P("mp", None),
        ),
        check_vma=False,
    )
```

```python
import functools

import jax
import jax.numpy as jnp
from jax import lax
from jax.experimental import pallas as pl
from jax.experimental.pallas import tpu as pltpu
from jax.sharding import PartitionSpec as P

neg_fill = -1000000000.0
open_cap = 3e38
eps_norm = 1e-05
PAIR = 128
HALF = 64
QUERY_SCALE = 0.125
ROOT = 0.7978845608028654
CUBE = 0.044715
f32 = jnp.float32
bf16 = jnp.bfloat16
ROW, FIRST, SECOND, TARGET, SOURCE, PLANE, CORE = range(7)


def low(value):
    return value.astype(bf16)


def nn(left, right):
    return lax.dot_general(left, right, (((1,), (0,)), ((), ())), preferred_element_type=f32)


def nt(left, right):
    return lax.dot_general(left, right, (((1,), (1,)), ((), ())), preferred_element_type=f32)


def tn(left, right):
    return lax.dot_general(left, right, (((0,), (0,)), ((), ())), preferred_element_type=f32)


def after(value, *others):
    return lax.optimization_barrier((value,) + others)[0]


def wall(*values):
    return lax.optimization_barrier(values)


def call(kernel, info, grid, ins, outs, scratch=(), micros=1.0):
    return pl.pallas_call(
        kernel,
        out_shape=tuple(jax.ShapeDtypeStruct(s, t) for s, t, _, _ in outs),
        grid_spec=pltpu.PrefetchScalarGridSpec(
            num_scalar_prefetch=1,
            grid=grid,
            in_specs=[pl.BlockSpec(b, m) for _, b, m in ins],
            out_specs=tuple(pl.BlockSpec(b, m) for _, _, b, m in outs),
            scratch_shapes=list(scratch),
        ),
        compiler_params=pltpu.CompilerParams(vmem_limit_bytes=52 << 20),
        cost_estimate=pl.CostEstimate(flops=int(micros * 1e7), bytes_accessed=1 << 10, transcendentals=0),
    )(info, *(a for a, _, _ in ins))


def rows_of_eight(values):
    return jnp.sum(values.reshape(values.shape[0] // 8, 8, values.shape[1]), axis=0)


def norm_stats(values):
    centre = jnp.mean(values, axis=-1, keepdims=True)
    offset = values - centre
    spread = jnp.mean(offset * offset, axis=-1, keepdims=True)
    scale = lax.rsqrt(spread + eps_norm)
    return offset * scale, scale


def norm_back(values, gain, grad):
    hat, scale = norm_stats(values)
    scaled = grad * gain
    mean_one = jnp.mean(scaled, axis=-1, keepdims=True)
    mean_two = jnp.mean(scaled * hat, axis=-1, keepdims=True)
    return scale * (scaled - mean_one - hat * mean_two), grad * hat


def head_halves(both):
    lane = lax.broadcasted_iota(jnp.int32, both.shape, 1)
    zero = jnp.zeros_like(both)
    return jnp.where(lane < HALF, both, zero), jnp.where(lane < HALF, zero, both)


def fill_caps(info, cap_ref, block, causal):
    length = cap_ref.shape[0]
    for t in range(2):
        keys = lax.broadcasted_iota(jnp.int32, (length, block), 0)
        allowed = keys < info[TARGET if causal else SOURCE]
        if causal:
            places = lax.broadcasted_iota(jnp.int32, (length, block), 1) + info[FIRST + t] * block
            allowed = allowed & (keys <= places)
        cap_ref[:, t * block : (t + 1) * block] = jnp.where(allowed, open_cap, neg_fill)


def forward_kernel(info, q_ref, k_ref, v_ref, o_ref, lse_ref, cap_ref, s_ref, *, block, causal, chunk):
    length = k_ref.shape[0]

    @pl.when(pl.program_id(0) == 0)
    def _():
        fill_caps(info, cap_ref, block, causal)

    for t in (1, 0):
        rows = slice(t * block, (t + 1) * block)
        span = length // 2 if (causal and t == 0) else length
        queries = jnp.concatenate(head_halves(q_ref[rows, :] * bf16(QUERY_SCALE)), axis=0)
        most = jnp.full((8, 2 * block), -open_cap, f32)
        for c in range(0, span, chunk):
            keys = slice(c, c + chunk)
            cap = cap_ref[keys, rows]
            scores = jnp.minimum(nt(k_ref[keys, :], queries), jnp.concatenate([cap, cap], axis=1))
            s_ref[t, keys, :] = scores
            most = jnp.maximum(most, jnp.max(scores.reshape(chunk // 8, 8, 2 * block), axis=0))
        most = jnp.max(most, axis=0, keepdims=True)
        total = jnp.zeros((8, 2 * block), f32)
        mixed = jnp.zeros((PAIR, 2 * block), f32)
        for c in range(0, span, chunk):
            keys = slice(c, c + chunk)
            weights = jnp.exp(s_ref[t, keys, :] - most)
            total = total + rows_of_eight(weights)
            mixed = mixed + tn(v_ref[keys, :], low(weights))
        total = jnp.sum(total, axis=0, keepdims=True)
        mixed = mixed / total
        sub = lax.broadcasted_iota(jnp.int32, (PAIR, block), 0)
        o_ref[rows, :] = low(jnp.where(sub < HALF, mixed[:, :block], mixed[:, block:]).T)
        lse = most + jnp.log(total)
        lse_ref[0, 0:1, rows] = lse[:, :block]
        lse_ref[0, 1:2, rows] = lse[:, block:]


def backward_kernel(
    info, q_ref, k_ref, v_ref, o_ref, g_ref, lse_ref, dq_ref, dk_ref, dv_ref, qs_ref, vs_ref, cap_ref, dk_acc, dv_acc,
    *, block, causal, chunk
):
    length = k_ref.shape[0]

    @pl.when(pl.program_id(0) == 0)
    def _():
        fill_caps(info, cap_ref, block, causal)

    q_sums = jnp.zeros((8, PAIR), f32)
    for t in (1, 0):
        rows = slice(t * block, (t + 1) * block)
        span = length // 2 if (causal and t == 0) else length
        grads = g_ref[rows, :]
        prod = (grads.astype(f32) * o_ref[rows, :].astype(f32)).T
        centre = jnp.concatenate(
            [jnp.sum(prod[:HALF], axis=0, keepdims=True), jnp.sum(prod[HALF:], axis=0, keepdims=True)], axis=1
        )
        lse = jnp.concatenate([lse_ref[0, 0:1, rows], lse_ref[0, 1:2, rows]], axis=1)
        queries = jnp.concatenate(head_halves(q_ref[rows, :] * bf16(QUERY_SCALE)), axis=0)
        grads = jnp.concatenate(head_halves(grads), axis=0)
        dq = jnp.zeros((PAIR, 2 * block), f32)
        for c in range(0, span, chunk):
            keys = slice(c, c + chunk)
            k, v = k_ref[keys, :], v_ref[keys, :]
            cap = cap_ref[keys, rows]
            scores = jnp.minimum(nt(k, queries), jnp.concatenate([cap, cap], axis=1))
            probs = jnp.exp(scores - lse)
            grad_scores = low(probs * (nt(v, grads) - centre))
            dv = nn(low(probs), grads)
            dk = nn(grad_scores, queries)
            dq = dq + tn(k, grad_scores)
            if t == 1:
                dk_acc[keys, :] = dk
                dv_acc[keys, :] = dv
            else:
                dk_acc[keys, :] += dk
                dv_acc[keys, :] += dv
        sub = lax.broadcasted_iota(jnp.int32, (PAIR, block), 0)
        dq = jnp.where(sub < HALF, dq[:, :block], dq[:, block:]) * QUERY_SCALE
        dq = low(dq.T)
        dq_ref[rows, :] = dq
        q_sums = q_sums + rows_of_eight(dq.astype(f32))
    dk_ref[...] = low(dk_acc[...])
    dv = low(dv_acc[...])
    dv_ref[...] = dv
    qs_ref[...] = q_sums
    vs_ref[...] = rows_of_eight(dv.astype(f32))


def attend_forward(info, query, keys, values, causal):
    queries, width = query.shape
    length = keys.shape[0]
    here = lambda i, _: (0, i)
    return call(
        functools.partial(forward_kernel, block=queries // 2, causal=causal, chunk=min(256, length // 2)),
        info,
        (width // PAIR,),
        [(query, (queries, PAIR), here), (keys, (length, PAIR), here), (values, (length, PAIR), here)],
        [
            ((queries, width), bf16, (queries, PAIR), here),
            ((width // PAIR, 8, queries), f32, (1, 8, queries), lambda i, _: (i, 0, 0)),
        ],
        [pltpu.VMEM((length, queries), f32), pltpu.VMEM((2, length, queries), f32)],
        micros=16,
    )


def attend_backward(info, query, keys, values, mixed, grad, lse_rows, causal):
    queries, width = query.shape
    length = keys.shape[0]
    here = lambda i, _: (0, i)
    one, key = (queries, PAIR), (length, PAIR)
    return call(
        functools.partial(backward_kernel, block=queries // 2, causal=causal, chunk=min(256, length // 2)),
        info,
        (width // PAIR,),
        [
            (query, one, here),
            (keys, key, here),
            (values, key, here),
            (mixed, one, here),
            (grad, one, here),
            (lse_rows, (1, 8, queries), lambda i, _: (i, 0, 0)),
        ],
        [
            ((queries, width), bf16, one, here),
            ((length, width), bf16, key, here),
            ((length, width), bf16, key, here),
            ((8, width), f32, (8, PAIR), here),
            ((8, width), f32, (8, PAIR), here),
        ],
        [pltpu.VMEM((length, queries), f32), pltpu.VMEM((length, PAIR), f32), pltpu.VMEM((length, PAIR), f32)],
        micros=24,
    )


def order_kernel(info, same_ref, other_ref, out_ref, *, part_of):
    mine = lax.rem(part_of(pl.program_id(0)), 2) == info[CORE]

    @pl.when(mine)
    def _():
        out_ref[...] = same_ref[...].astype(out_ref.dtype)

    @pl.when(jnp.logical_not(mine))
    def _():
        out_ref[...] = other_ref[...].astype(out_ref.dtype)


def order_rows(info, found, got, rows, group, pieces, kind):
    half, width = got.shape
    steps = group * pieces
    block = half // (rows * steps // 2)

    def part_of(i):
        b = lax.rem(i, steps)
        return jnp.where(b >= group, steps - 1 - b, b)

    def source(i):
        late = (lax.rem(i, steps) >= group).astype(jnp.int32)
        return (lax.div(i, steps) * (group // 2) + lax.div(part_of(i), 2)) * pieces + late

    return call(
        functools.partial(order_kernel, part_of=part_of),
        info,
        (rows * steps,),
        [
            (found, (block, width), lambda i, info: (source(i) + info[CORE] * (half // block), 0)),
            (got, (block, width), lambda i, _: (source(i), 0)),
        ],
        [((2 * half, width), kind, (block, width), lambda i, _: (i, 0))],
        micros=4,
    )[0]


def entry_kernel(info, x_ref, gain_ref, shift_ref, h_ref, *, which):
    hat, _ = norm_stats(x_ref[...].astype(f32))
    one = slice(which, which + 1)
    h_ref[...] = low(hat * gain_ref[one, :].astype(f32) + shift_ref[one, :].astype(f32))


def entry_norm(info, tokens, gains, shifts):
    _, length, width = tokens.shape
    tile = min(256, length)
    whole = lambda i, _: (0, 0)
    return call(
        functools.partial(entry_kernel, which=0),
        info,
        (length // tile,),
        [
            (tokens, (None, tile, width), lambda i, info: (info[ROW], i, 0)),
            (gains, gains.shape, whole),
            (shifts, shifts.shape, whole),
        ],
        [((length, width), bf16, (tile, width), lambda i, _: (i, 0))],
        micros=3,
    )[0]


def weight_ins(weight, slots):
    own, lead, rest, place = weight
    depth = rest.shape[0]
    wide = own.shape[1] * own.shape[2] // depth
    return [
        (own, (None,) + own.shape[1:], lambda *_: (lead, 0, 0)),
        (rest, (depth, (slots - 1) * wide), lambda *_: (0, place)),
    ]


def project_kernel(info, x_ref, own_ref, rest_ref, *others, flipped):
    x = x_ref[...]
    mine = nt(x, own_ref[...]) if flipped else nn(x, own_ref[...])
    wide = mine.shape[1]
    rest = nn(x, rest_ref[...])
    out_ref = others[-1]
    if len(others) > 1:
        mine = mine + others[0][:, :wide]
        rest = rest + others[0][:, wide:]
    out_ref[:, :wide] = low(mine)
    out_ref[:, wide:] = low(rest)


def project(info, x, place_of, tiles, weight, bias, slots, flipped=False):
    count, tile = tiles
    depth = x.shape[2]
    ins = [(x, (None, tile, depth), lambda i, info: place_of(i, info) + (0,))] + weight_ins(weight, slots)
    own = weight[0]
    width = slots * (own.shape[1] * own.shape[2] // depth)
    if bias is not None:
        ins.append((bias, bias.shape, lambda i, _: (0, 0)))
    return call(
        functools.partial(project_kernel, flipped=flipped),
        info,
        (count,),
        ins,
        [((count * tile, width), bf16, (tile, width), lambda i, _: (i, 0))],
        micros=2.5 * count * tile / 1024,
    )[0]


def mix_kernel(info, x_ref, own_ref, rest_ref, resid_ref, bias_ref, gain_ref, shift_ref, sum_ref, h_ref, *, which):
    wide = own_ref.shape[0]
    found = nn(x_ref[:, :wide], own_ref[...]) + nt(x_ref[:, wide:], rest_ref[...])
    found = resid_ref[...].astype(f32) + found + bias_ref[which : which + 1, :].astype(f32)
    sum_ref[...] = found
    hat, _ = norm_stats(found)
    one = slice(which + 1, which + 2)
    h_ref[...] = low(hat * gain_ref[one, :].astype(f32) + shift_ref[one, :].astype(f32))


def mix(info, x, weight, resid, resid_place, biases, gains, shifts, which, slots):
    rows, width = x.shape
    block = rows // 2
    whole = lambda i, _: (0, 0)
    here = lambda i, _: (i, 0)
    depth = resid.shape[2]
    return call(
        functools.partial(mix_kernel, which=which),
        info,
        (2,),
        [(x, (block, width), here)]
        + weight_ins(weight, slots)
        + [
            (resid, (None, block, depth), lambda i, info: resid_place(i, info) + (0,)),
            (biases, biases.shape, whole),
            (gains, gains.shape, whole),
            (shifts, shifts.shape, whole),
        ],
        [((rows, depth), f32, (block, depth), here), ((rows, depth), bf16, (block, depth), here)],
        micros=4,
    )


def back_dots(pairs):
    total = None
    for x_ref, own_ref, rest_ref in pairs:
        wide = own_ref.shape[1]
        found = nt(x_ref[:, :wide], own_ref[...]) + nt(x_ref[:, wide:], rest_ref[...])
        total = found if total is None else total + found
    return total


def back_kernel(info, *refs, count):
    pairs = [refs[3 * j : 3 * j + 3] for j in range(count)]
    refs[-1][...] = low(back_dots(pairs))


def back(info, terms, slots):
    rows, width = terms[0][0].shape
    depth = terms[0][1][2].shape[0]
    tile = min(256, rows)
    ins = []
    for x, weight in terms:
        ins += [(x, (tile, width), lambda i, _: (i, 0))] + weight_ins(weight, slots)
    return call(
        functools.partial(back_kernel, count=len(terms)),
        info,
        (rows // tile,),
        ins,
        [((rows, depth), bf16, (tile, depth), lambda i, _: (i, 0))],
        micros=5,
    )[0]


def back_norm_kernel(info, *refs, extras, which, keep):
    x_ref, own_ref, rest_ref = refs[:3]
    extra = refs[3 : 3 + extras]
    v_ref, add_ref, gain_ref = refs[3 + extras : 6 + extras]
    outs = refs[6 + extras :]
    grad = back_dots([(x_ref, own_ref, rest_ref)])
    for e in extra:
        grad = grad + e[...].astype(f32)
    found, to_gain = norm_back(v_ref[...].astype(f32), gain_ref[which : which + 1, :].astype(f32), grad)
    found = add_ref[...] + found
    low_found = low(found)
    if keep:
        outs[0][...] = found
    outs[-2][...] = low_found
    sums = jnp.concatenate([rows_of_eight(to_gain), rows_of_eight(grad), rows_of_eight(low_found.astype(f32))])

    @pl.when(pl.program_id(0) == 0)
    def _():
        outs[-1][...] = sums

    @pl.when(pl.program_id(0) > 0)
    def _():
        outs[-1][...] += sums


def back_norm(info, x, weight, extras, values, values_place, add, gains, which, slots, keep):
    rows, width = x.shape
    block = rows // 2
    depth = add.shape[1]
    here = lambda i, _: (i, 0)
    whole = lambda i, _: (0, 0)
    one = (block, depth)
    outs = [((rows, depth), bf16, one, here), ((24, depth), f32, (24, depth), whole)]
    if keep:
        outs = [((rows, depth), f32, one, here)] + outs
    return call(
        functools.partial(back_norm_kernel, extras=len(extras), which=which, keep=keep),
        info,
        (2,),
        [(x, (block, width), here)]
        + weight_ins(weight, slots)
        + [(e, one, here) for e in extras]
        + [
            (values, (None, block, depth), lambda i, info: values_place(i, info) + (0,)),
            (add, one, here),
            (gains, gains.shape, whole),
        ],
        outs,
        micros=4,
    )


def feed_kernel(
    info, h_ref, c0_ref, c1_ref, second_ref, upo_ref, downo_ref, upr_ref, downr_ref, ub_ref, bias_ref, gain_ref,
    a_ref, du_ref, us_ref, final_ref, g_ref, e_ref, sums_ref, out_acc, dh_acc, *, own_tiles
):
    i = pl.program_id(0)
    block = c0_ref.shape[0]
    cots = (c0_ref, c1_ref)
    which = 2

    def tile(own):
        sums = None
        for t in range(2):
            rows = slice(t * block, (t + 1) * block)
            up = upo_ref[...] if own else upr_ref[...]
            pre = nn(h_ref[rows, :], up) + ub_ref[...]
            square = pre * pre
            curve = jnp.tanh(ROOT * (pre + CUBE * square * pre))
            act = low(0.5 * pre * (1.0 + curve))
            slope = 0.5 * (1.0 + curve) + 0.5 * pre * (1.0 - curve * curve) * (ROOT * (1.0 + 3.0 * CUBE * square))
            a_ref[rows, :] = act
            if own:
                grad = nt(cots[t][...], downo_ref[...])
                out = nn(act, downo_ref[...])
            else:
                grad = nn(cots[t][...], downr_ref[...])
                out = nt(act, downr_ref[...])
            du = low(slope * grad)
            du_ref[rows, :] = du
            part = rows_of_eight(du.astype(f32))
            sums = part if sums is None else sums + part
            dh = nt(du, up)
            first = i == 0
            if own:

                @pl.when(first)
                def _():
                    out_acc[rows, :] = out
                    dh_acc[rows, :] = dh

                @pl.when(jnp.logical_not(first))
                def _():
                    out_acc[rows, :] += out
                    dh_acc[rows, :] += dh
            else:
                out_acc[rows, :] += out
                dh_acc[rows, :] += dh
        us_ref[...] = sums

    @pl.when(i < own_tiles)
    def _():
        tile(True)

    @pl.when(i >= own_tiles)
    def _():
        tile(False)

    @pl.when(i == pl.num_programs(0) - 1)
    def _():
        sums = None
        gain = gain_ref[which : which + 1, :].astype(f32)
        for t in range(2):
            rows = slice(t * block, (t + 1) * block)
            second = second_ref[rows, :]
            final_ref[rows, :] = low(second + out_acc[rows, :] + bias_ref[which : which + 1, :].astype(f32))
            cot = cots[t][...].astype(f32)
            grad = dh_acc[rows, :]
            found, to_gain = norm_back(second, gain, grad)
            found = cot + found
            g_ref[rows, :] = found
            rounded = low(found)
            e_ref[rows, :] = rounded
            part = jnp.concatenate(
                [
                    rows_of_eight(to_gain),
                    rows_of_eight(grad),
                    rows_of_eight(rounded.astype(f32)),
                    rows_of_eight(cot),
                ]
            )
            sums = part if sums is None else sums + part
        sums_ref[...] = sums


def feed_forward(info, h, cotangent, second, up, down, up_bias, biases, gains, slots):
    rows, depth = h.shape
    block = rows // 2
    up_own, _, up_rest, up_place = up
    down_own, _, down_rest, down_place = down
    hidden = up_own.shape[2]
    tile = min(512, hidden)
    own_tiles = hidden // tile
    total = slots * own_tiles
    rest_tiles = (slots - 1) * own_tiles
    own_at = lambda i: jnp.minimum(i, own_tiles - 1)
    rest_at = lambda i: jnp.maximum(i - own_tiles, 0)
    whole = lambda i, _: (0, 0)
    full = (rows, depth)
    return call(
        functools.partial(feed_kernel, own_tiles=own_tiles),
        info,
        (total,),
        [
            (h, full, whole),
            (cotangent, (None, block, depth), lambda i, _: (0, 0, 0)),
            (cotangent, (None, block, depth), lambda i, _: (0, 1, 0)),
            (second, full, whole),
            (up_own, (None, depth, tile), lambda i, _: (0, 0, own_at(i))),
            (down_own, (None, tile, depth), lambda i, _: (0, own_at(i), 0)),
            (up_rest, (depth, tile), lambda i, _: (0, up_place * rest_tiles + rest_at(i))),
            (down_rest, (depth, tile), lambda i, _: (0, down_place * rest_tiles + rest_at(i))),
            (up_bias, (1, tile), lambda i, _: (0, i)),
            (biases, biases.shape, whole),
            (gains, gains.shape, whole),
        ],
        [
            ((rows, total * tile), bf16, (rows, tile), lambda i, _: (0, i)),
            ((rows, total * tile), bf16, (rows, tile), lambda i, _: (0, i)),
            ((8, total * tile), f32, (8, tile), lambda i, _: (0, i)),
            (full, bf16, full, whole),
            (full, f32, full, whole),
            (full, bf16, full, whole),
            ((32, depth), f32, (32, depth), whole),
        ],
        [pltpu.VMEM(full, f32), pltpu.VMEM(full, f32)],
        micros=32,
    )


def grad_kernel(info, *refs, plan, share, plane, mine):
    acts = refs[: sum(len(pieces) for pieces, _ in plan)]
    refs = refs[len(acts) :]
    grads = refs[: len(plan)]
    refs = refs[len(plan) :]
    got_ref = None
    if mine:
        got_ref, refs = refs[0], refs[1:]
    outs, turned = refs[: plane if mine else 1], refs[-len(plan) :]
    core = info[CORE] if mine else 1 - info[CORE]

    @pl.when(pl.program_id(0) == 0)
    def _():
        at = 0
        for t, (pieces, _) in enumerate(plan):
            start = 0
            for length in pieces:
                for r in range(plane):
                    if share % PAIR == 0:
                        block = 2 * jnp.bitwise_xor(info[PLANE], r) + core
                        cols = acts[at][:, pl.ds(pl.multiple_of(block * share, share), share)]
                    else:
                        cols = acts[at][:, r * share : (r + 1) * share]
                    turned[t][r * share : (r + 1) * share, start : start + length] = cols.T
                start += length
                at += 1

    first = 0
    for t, (_, wide) in enumerate(plan):
        cols = slice(first, first + wide)
        found = nn(turned[t][...], grads[t][...])
        if mine:
            found = low(found + got_ref[:, cols].astype(f32))
            for r in range(plane):
                outs[r][:, cols] = found[r * share : (r + 1) * share, :]
        else:
            outs[0][:, cols] = low(found)
        first += wide


def weight_grads(info, tensors, d, dp_size, slots, got=None):
    depth = tensors[0][0][0][0].shape[2]
    share, plane = depth // dp_size, dp_size // 2
    core = lax.rem(d, 2) if got is not None else 1 - lax.rem(d, 2)
    plan = [(tuple(rows for _, rows, _ in pieces), grad.shape[1] // slots) for pieces, grad in tensors]
    ins = []
    for pieces, _ in tensors:
        for array, rows, place in pieces:
            if share % PAIR == 0:
                ins.append((array, (None, rows, depth), lambda i, info, place=place: place(info) + (0,)))
            else:
                wide = array.reshape(array.shape[:2] + (plane, 2, share))
                wide = lax.dynamic_index_in_dim(wide, core, 3, keepdims=False)
                order = [jnp.bitwise_xor(d // 2, r) for r in range(plane)]
                wide = jnp.concatenate([lax.dynamic_index_in_dim(wide, b, 2) for b in order], axis=2)
                wide = wide.reshape(array.shape[:2] + (depth // 2,))
                ins.append((wide, (None, rows, depth // 2), lambda i, info, place=place: place(info) + (0,)))
    for (_, grad), (_, wide) in zip(tensors, plan):
        ins.append((grad, (grad.shape[0], wide), lambda i, _: (0, i)))
    half = depth // 2
    tile = sum(wide for _, wide in plan)
    if got is not None:
        ins.append((got, (half, tile), lambda i, _: (0, i)))
        outs = [((share, slots * tile), bf16, (share, tile), lambda i, _: (0, i))] * plane
    else:
        outs = [((half, slots * tile), bf16, (half, tile), lambda i, _: (0, i))]
    return call(
        functools.partial(grad_kernel, plan=plan, share=share, plane=plane, mine=got is not None),
        info,
        (slots,),
        ins,
        outs,
        [pltpu.VMEM((half, g.shape[0]), bf16) for _, g in tensors],
        micros=8,
    )


def finish_kernel(info, in_ref, out_ref, *, turn):
    value = in_ref[...].astype(f32)
    out_ref[...] = value.T if turn else value


def finish(info, full, places, wide, turn=False):
    depth = full.shape[0]
    first = places[0]
    if turn:
        tile, cut = min(256, depth), min(512, wide)
        return call(
            functools.partial(finish_kernel, turn=True),
            info,
            (depth // tile, wide // cut),
            [(full, (tile, cut), lambda i, j, _: (i, first * (wide // cut) + j))],
            [((wide, depth), f32, (cut, tile), lambda i, j, _: (j, i))],
            micros=3,
        )[0]
    tile = min(512, depth)
    return call(
        functools.partial(finish_kernel, turn=False),
        info,
        (len(places), depth // tile),
        [(full, (tile, wide), lambda i, j, _: (j, first + i))],
        [((len(places), depth, wide), f32, (None, tile, wide), lambda i, j, _: (i, j, 0))],
        micros=3,
    )[0]


def finish_pair_kernel(info, in_ref, q_ref, kv_ref, o_ref, s_ref, so_ref):
    wide = q_ref.shape[1]

    def cols(t):
        return in_ref[:, t * wide : (t + 1) * wide].astype(f32)

    q_ref[...] = cols(0)
    for t in range(2):
        kv_ref[t] = cols(1 + t)
    o_ref[...] = cols(3).T
    for t in range(3):
        s_ref[t] = cols(4 + t)
    so_ref[...] = cols(7).T


def finish_pair(info, full):
    depth = full.shape[0]
    wide = full.shape[1] // 8
    tile = min(256, depth)
    return call(
        finish_pair_kernel,
        info,
        (depth // tile,),
        [(full, (tile, 8 * wide), lambda i, _: (i, 0))],
        [
            ((depth, wide), f32, (tile, wide), lambda i, _: (i, 0)),
            ((2, depth, wide), f32, (2, tile, wide), lambda i, _: (0, i, 0)),
            ((wide, depth), f32, (wide, tile), lambda i, _: (0, i)),
            ((3, depth, wide), f32, (3, tile, wide), lambda i, _: (0, i, 0)),
            ((wide, depth), f32, (wide, tile), lambda i, _: (0, i)),
        ],
        micros=4,
    )


def build(dp_size, mp_size):
    ring = [(i, (i + 1) % mp_size) for i in range(mp_size)]
    back_ring = [(i, (i - 1) % mp_size) for i in range(mp_size)]
    dp_bits = dp_size.bit_length() - 1
    plane = dp_size // 2

    def flip(axis, size, bits):
        return lambda value: lax.ppermute(value, axis, [(i, i ^ bits) for i in range(size)])

    def shards(
        tokens,
        memory,
        target_lengths,
        source_lengths,
        cotangent,
        norm_gain,
        norm_bias,
        self_in,
        self_in_bias,
        self_out,
        cross_query,
        cross_kv,
        cross_bias,
        cross_out,
        out_bias,
        ffn_up,
        ffn_up_bias,
        ffn_down,
    ):
        rows, length, width = tokens.shape
        source = memory.shape[1]
        d = lax.axis_index("dp")
        z = lax.axis_index("mp")
        group = mp_size // rows
        core = lax.rem(d, 2)
        chips = group // 2
        chip_row = z // chips
        part = (z % chips) * 2 + core
        held = chip_row // rows == core
        row = lax.rem(chip_row, rows)
        block = length // (2 * group)
        share = width // dp_size
        per = width // mp_size
        hid = ffn_up.shape[1]
        swap = flip("dp", dp_size, 1)

        def take_row(values):
            return lax.dynamic_index_in_dim(values, row, 0, keepdims=False)

        def blocks_of(values, p):
            return jnp.concatenate(
                [
                    lax.dynamic_slice_in_dim(values, s * block, block, 0)
                    for s in (p, 2 * group - 1 - p)
                ]
            )

        own_place = lambda i, info: (info[ROW], info[FIRST + i])
        own_h_place = lambda i, info: (0, info[FIRST + i])
        flat_place = lambda i, info: (0, i)
        row_place = lambda i, info: (info[ROW], i)

        def rows_of(weight):
            return lax.dynamic_slice_in_dim(weight, d * share, share, 0)

        def cols_of(weight):
            return lax.dynamic_slice_in_dim(weight, d * share, share, 1).T

        def with_bias(piece, bias):
            extra = jnp.zeros((16, piece.shape[1]), bf16)
            if bias is not None:
                extra = lax.dynamic_update_slice(extra, bias[None], (0, 0))
            return jnp.concatenate([piece, extra])

        def side_by_side(pieces):
            return jnp.concatenate([with_bias(p, b) for p, b in pieces], axis=1)

        def pass_on(value):
            return lax.ppermute(value, "mp", ring)

        def gather_rest(found, wides, *held):
            starts = [0]
            for w in wides:
                starts.append(starts[-1] + w)
            both = jnp.concatenate([s[:, a:b] for a, b in zip(starts[:-1], starts[1:]) for s in found], axis=1)
            ours = both[:share]
            if held:
                ours = after(ours, *held)
            return lax.all_gather(ours, "dp", axis=0, tiled=True), both[share : share + 1].astype(f32)

        def bias_of(own, biases, t, wide):
            far = (mp_size - 1) * wide
            return jnp.concatenate([own.astype(f32)[None], biases[:, t * far : (t + 1) * far]], axis=1)

        def row_of(mine, theirs, cut=lambda values: values):
            return jnp.where(held, cut(take_row(mine)), cut(take_row(theirs)))[None]

        lengths = jnp.stack([target_lengths, source_lengths])
        lengths = jnp.where(held, lengths, swap(lengths))
        lengths = lax.dynamic_index_in_dim(lengths, row, 1, keepdims=False)
        info = jnp.stack(
            [0 * part, part, 2 * group - 1 - part, lengths[0], lengths[1], d // 2, core]
        ).astype(jnp.int32)
        found_a = [
            pass_on(
                side_by_side(
                    [
                        (rows_of(self_in[0]), self_in_bias[0]),
                        (rows_of(self_in[1]), None),
                        (rows_of(self_in[2]), self_in_bias[1]),
                    ]
                )
            )
        ]
        for _ in range(mp_size - 3):
            found_a.append(pass_on(found_a[-1]))
        found_a[-1], tokens_got, info = wall(found_a[-1], swap(tokens), info)
        found_a.append(pass_on(found_a[-1]))
        share_b = side_by_side(
            [
                (cols_of(self_out), None),
                (rows_of(cross_query), cross_bias[0]),
                (rows_of(cross_kv[0]), None),
                (rows_of(cross_kv[1]), cross_bias[1]),
                (cols_of(cross_out), None),
            ]
        )
        share_c = side_by_side(
            [(rows_of(ffn_up), ffn_up_bias), (cols_of(ffn_down), None)]
        )
        found_a[-1], tokens_got, share_b, share_c = wall(found_a[-1], tokens_got, share_b, share_c)
        found_b = [pass_on(share_b)]
        tokens_row = row_of(tokens, tokens_got)
        h1_row = entry_norm(info, tokens_row, norm_gain, norm_bias)
        found_b[0], h1_row = wall(found_b[0], h1_row)
        for _ in range(mp_size - 3):
            found_b.append(pass_on(found_b[-1]))
        found_b[-1], memory_got = wall(found_b[-1], swap(memory))
        found_b.append(pass_on(found_b[-1]))
        memory_row = row_of(memory, memory_got)
        found_b[-1], memory_row = wall(found_b[-1], memory_row)
        rest_a, bias_a = gather_rest(found_a, [per] * 3)
        rest_b, bias_b = gather_rest(found_b, [per] * 5)
        w_q1, w_k1, w_v1 = [(self_in, t, rest_a, t) for t in range(3)]
        w_o1 = (self_out[None], 0, rest_b, 0)
        w_q2 = (cross_query[None], 0, rest_b, 1)
        w_k2, w_v2 = (cross_kv, 0, rest_b, 2), (cross_kv, 1, rest_b, 3)
        w_o2 = (cross_out[None], 0, rest_b, 4)

        found_c = [pass_on(after(share_c, found_b[-1]))]
        for _ in range(mp_size - 3):
            found_c.append(pass_on(found_c[-1]))
        far = min(256, length)
        h1_flat = h1_row[None]
        k1 = project(info, h1_flat, flat_place, (length // far, far), w_k1, None, mp_size)
        found_c[-1], k1, h1_flat = wall(found_c[-1], k1, h1_flat)
        found_c.append(pass_on(found_c[-1]))
        v1 = project(
            info, h1_flat, flat_place, (length // far, far), w_v1, bias_of(self_in_bias[1], bias_a, 2, per), mp_size
        )
        q1 = project(info, h1_flat, own_h_place, (2, block), w_q1, bias_of(self_in_bias[0], bias_a, 0, per), mp_size)
        cot_own = row_of(cotangent, swap(cotangent), lambda values: blocks_of(values, part))
        found_c[-1], v1, q1 = wall(found_c[-1], v1, q1)
        rest_c, bias_c = gather_rest(found_c, [hid, hid])
        w_up, w_down = (ffn_up[None], 0, rest_c, 0), (ffn_down[None], 0, rest_c, 1)
        o1, lse1 = attend_forward(info, q1, k1, v1, True)
        first, h2 = mix(info, o1, w_o1, tokens_row, own_place, out_bias, norm_gain, norm_bias, 0, mp_size)
        q2 = project(info, h2[None], flat_place, (2, block), w_q2, bias_of(cross_bias[0], bias_b, 1, per), mp_size)
        k2 = project(info, memory_row, row_place, (source // far, far), w_k2, None, mp_size)
        v2 = project(
            info, memory_row, row_place, (source // far, far), w_v2, bias_of(cross_bias[1], bias_b, 3, per), mp_size
        )
        o2, lse2 = attend_forward(info, q2, k2, v2, False)
        second, h3 = mix(info, o2, w_o2, first[None], flat_place, out_bias, norm_gain, norm_bias, 1, mp_size)
        hidden, grad_pre, up_sums, final, g2, e2, sums_three = feed_forward(
            info, h3, cot_own, second, w_up, w_down, bias_of(ffn_up_bias, bias_c, 0, hid), out_bias, norm_gain, mp_size
        )

        def to_plane(piece, r):
            return flip("dp", dp_size, 2 * r)(piece)

        def slots_of(total, count=mp_size):
            wide = total[0].shape[1] // count
            slots = []
            for k in range(count):
                cols = slice(k * wide, (k + 1) * wide)
                slots.append(low(sum(t[:, cols].astype(f32) for t in total)))
            return slots

        def to_owners(slots):
            return [
                lax.ppermute(slots[k], "mp", [(i, (i - k) % mp_size) for i in range(mp_size)])
                for k in range(1, mp_size)
            ]

        def add_up(values):
            return low(sum(v.astype(f32) for v in values))

        def gather_grads(total):
            return lax.all_gather(total, "dp", axis=0, tiled=True)

        def gather_rows(mine):
            return lax.all_gather(mine, "mp", axis=0, tiled=True)

        def for_other(found):
            half = found.shape[0] // 2
            return swap(lax.dynamic_slice_in_dim(found, (1 - core) * half, half, 0))

        def own_blocks(array, lead):
            return [
                (array, block, lambda info, t=t: ((info[ROW] if lead else 0), info[FIRST + t])) for t in range(2)
            ]

        def all_rows(array, lead=False):
            return [(array, array.shape[1], lambda info: ((info[ROW] if lead else 0), 0))]

        def core_send(tensors):
            return weight_grads(info, tensors, d, dp_size, mp_size)[0]

        def to_core(sent):
            return flip("dp", dp_size, 1)(sent)

        def core_keep(tensors, got):
            return weight_grads(info, tensors, d, dp_size, mp_size, got)

        row_perm = [(i, (i // chips) * chips + (i % chips - 1) % chips) for i in range(mp_size)]

        def row_sum(piece_of):
            got = [swap(piece_of(2 * c + 1 - core)) for c in range(chips)]
            if chips == 1:
                return got[0], piece_of(part)
            pieces = jnp.stack([add_up([got[c], piece_of(2 * c + core)]) for c in range(chips)])
            place = z % chips
            total = lax.dynamic_index_in_dim(pieces, lax.rem(place + 1, chips), 0, keepdims=False)
            for k in range(chips - 2, -1, -1):
                total = lax.ppermute(total, "mp", row_perm)
                here = lax.dynamic_index_in_dim(pieces, lax.rem(place - k + chips, chips), 0, keepdims=False)
                if k:
                    total = add_up([total, here])
            return total, here

        def all_planes(kept):
            return [kept[0]] + [to_plane(kept[r], r) for r in range(1, plane)]

        output_found = gather_rows(final)
        ffn_tensors = [(all_rows(h3[None]), grad_pre), (all_rows(cot_own), hidden)]
        ffn_sent = core_send(ffn_tensors)
        e2, ffn_sent = wall(e2, ffn_sent)

        ffn_got = to_core(ffn_sent)
        do2 = project(info, e2[None], flat_place, (2, block), w_o2, None, mp_size, flipped=True)
        dq2, dk2, dv2, sum_q2, sum_v2 = attend_backward(info, q2, k2, v2, o2, do2, lse2, False)
        memory_part = back(info, [(dk2, w_k2), (dv2, w_v2)], mp_size)

        def memory_piece(p):
            return lax.dynamic_slice_in_dim(memory_part, p * (source // group), source // group, 0)

        ffn_got, memory_part, dq2 = wall(ffn_got, memory_part, dq2)
        memory_got, memory_here = row_sum(memory_piece)
        ffn_kept = core_keep(ffn_tensors, ffn_got)
        memory_got, dq2, *ffn_kept = wall(memory_got, dq2, *ffn_kept)
        memory_own = add_up([memory_got, memory_here])
        memory_found = gather_rows(memory_own)
        memory_own, dq2 = wall(memory_own, dq2)

        late = plane - 1
        ffn_total = [ffn_kept[0]] + [to_plane(ffn_kept[r], r) for r in range(1, late)]
        g1, e1, sums_two = back_norm(
            info, dq2, w_q2, [], first[None], flat_place, g2, norm_gain, 1, mp_size, True
        )
        cross_tensors = [
            (all_rows(h2[None]), dq2),
            (all_rows(memory_row), dk2),
            (all_rows(memory_row), dv2),
            (all_rows(e2[None]), o2),
        ]
        cross_sent = core_send(cross_tensors)
        cross_got = to_core(cross_sent)
        e1 = after(e1, cross_sent)
        do1 = project(info, e1[None], flat_place, (2, block), w_o1, None, mp_size, flipped=True)
        dq1, dk1, dv1, sum_q1, sum_v1 = attend_backward(info, q1, k1, v1, o1, do1, lse1, True)
        kv_part = back(info, [(dk1, w_k1), (dv1, w_v1)], mp_size)
        wide = ffn_kept[late].shape[1] // 2
        last_one, last_two = ffn_kept[late][:, :wide], ffn_kept[late][:, wide:]
        kv_part, cross_got, last_one, last_two, *ffn_total = wall(kv_part, cross_got, last_one, last_two, *ffn_total)

        def causal_piece(p):
            return blocks_of(kv_part, p)

        last_two = to_plane(last_two, late)
        got, here = row_sum(causal_piece)
        cross_kept = core_keep(cross_tensors, cross_got)
        self_tensors = [
            (own_blocks(h1_flat, False), dq1),
            (all_rows(h1_flat), dk1),
            (all_rows(h1_flat), dv1),
            (all_rows(e1[None]), o1),
        ]
        self_sent = core_send(self_tensors)
        output_got = for_other(output_found)
        got, self_sent, output_got, last_one, last_two, *cross_kept = wall(
            got, self_sent, output_got, last_one, last_two, *cross_kept
        )
        last_one = to_plane(last_one, late)
        cross_total = all_planes(cross_kept)
        self_got = to_core(self_sent)
        tokens_own, sums_one = back_norm(
            info, dq1, w_q1, [got, here], tokens_row, own_place, g1, norm_gain, 0, mp_size, False
        )
        tokens_found = gather_rows(tokens_own)

        def by_slot(sums):
            return jnp.sum(sums, axis=0).reshape(mp_size, -1)

        slot_sums = jnp.concatenate([by_slot(s) for s in (sum_q1, sum_v1, sum_q2, sum_v2, up_sums)], axis=1)
        flipped = slot_sums[::-1]
        twice = jnp.concatenate([flipped, flipped])
        in_order = lax.dynamic_slice_in_dim(twice, mp_size - 1 - z, mp_size, 0)
        whole = [
            jnp.sum(sums.reshape(-1, 8, width), axis=1) for sums in (sums_one, sums_two, sums_three)
        ]
        whole = jnp.concatenate(
            [w[0:1] for w in whole] + [w[1:2] for w in whole] + [whole[1][2:3], whole[2][2:3], whole[2][3:4]]
        )
        small = jnp.concatenate([in_order.reshape(-1, PAIR), whole.reshape(-1, PAIR)])
        small_steps = [("dp", dp_size, 1 << b) for b in range(dp_bits)]
        small_steps += [("mp", mp_size, 1 << b) for b in range(mp_size.bit_length() - 1)]

        self_got, tokens_own = wall(self_got, tokens_own)
        self_kept = core_keep(self_tensors, self_got)
        last_one, *self_kept = wall(last_one, *self_kept)
        self_total = all_planes(self_kept)
        ffn_slots = slots_of([t[:, :wide] for t in ffn_total] + [last_one], mp_size // 2)
        ffn_slots += slots_of([t[:, wide:] for t in ffn_total] + [last_two], mp_size // 2)
        output = order_rows(info, output_found, output_got, rows, group, 2, bf16).reshape(tokens.shape)
        output, small, *ffn_slots = wall(output, small, *ffn_slots)

        def ring_start(slots):
            return lax.ppermute(slots[mp_size - 1], "mp", back_ring)

        def ring_next(slots, k, state):
            return lax.ppermute(add_up([slots[k], state]), "mp", back_ring)

        ffn_state = ring_start(ffn_slots)
        memory_got = for_other(memory_found)
        memory_got, small, ffn_state, *cross_total = wall(memory_got, small, ffn_state, *cross_total)
        for k in range(mp_size - 2, 1, -1):
            ffn_state = ring_next(ffn_slots, k, ffn_state)
        cross_slots = slots_of(cross_total)
        cross_state = ring_start(cross_slots)
        memory_grad = order_rows(info, memory_found, memory_got, rows, group, 1, f32).reshape(memory.shape)
        memory_grad, small, ffn_state, cross_state = wall(memory_grad, small, ffn_state, cross_state)
        ffn_state = ring_next(ffn_slots, 1, ffn_state)
        for k in range(mp_size - 2, 1, -1):
            cross_state = ring_next(cross_slots, k, cross_state)
        ffn_state, small, cross_state, *self_total = wall(ffn_state, small, cross_state, *self_total)
        ffn_full = gather_grads(add_up([ffn_slots[0], ffn_state]))
        cross_state = ring_next(cross_slots, 1, cross_state)
        self_slots = slots_of(self_total)
        self_total = [self_slots[0]] + to_owners(self_slots)
        tokens_got = for_other(tokens_found)
        tokens_grad = order_rows(info, tokens_found, tokens_got, rows, group, 2, f32).reshape(tokens.shape)
        tokens_grad, small, cross_state, *self_total = wall(tokens_grad, small, cross_state, *self_total)
        for step in small_steps:
            small = small + flip(*step)(small)
        joint = jnp.concatenate([add_up([cross_slots[0], cross_state]), add_up(self_total)], axis=1)
        joint_full = gather_grads(joint)
        up_grad, down_grad = finish(info, ffn_full, [0], hid)[0], finish(info, ffn_full, [1], hid, True)
        small = small.reshape(-1)
        slot_part = small[: in_order.size].reshape(in_order.shape)
        mine = lax.dynamic_index_in_dim(slot_part, z, 0, keepdims=False)
        whole = small[in_order.size :].reshape(9, width)
        cross_q, cross_both, cross_o, self_three, self_o = finish_pair(after(info, up_grad, down_grad), joint_full)
        return (
            output,
            tokens_grad,
            memory_grad,
            whole[0:3],
            whole[3:6],
            self_three,
            jnp.stack([mine[:per], mine[per : 2 * per]]),
            self_o,
            cross_q,
            cross_both,
            jnp.stack([mine[2 * per : 3 * per], mine[3 * per : 4 * per]]),
            cross_o,
            whole[6:9],
            up_grad,
            mine[4 * per :],
            down_grad,
        )

    return shards


def solution(mesh):
    placed = (
        P("dp", None, None),
        P("dp", None, None),
        P("dp"),
        P("dp"),
        P("dp", None, None),
        P(),
        P(),
        P(None, None, "mp"),
        P(None, "mp"),
        P("mp", None),
        P(None, "mp"),
        P(None, None, "mp"),
        P(None, "mp"),
        P("mp", None),
        P(),
        P(None, "mp"),
        P("mp"),
        P("mp", None),
    )
    return jax.shard_map(
        build(mesh.shape["dp"], mesh.shape["mp"]),
        mesh=mesh,
        in_specs=placed,
        out_specs=(
            P("dp", None, None),
            P("dp", None, None),
            P("dp", None, None),
            P(),
            P(),
            P(None, None, "mp"),
            P(None, "mp"),
            P("mp", None),
            P(None, "mp"),
            P(None, None, "mp"),
            P(None, "mp"),
            P("mp", None),
            P(),
            P(None, "mp"),
            P("mp"),
            P("mp", None),
        ),
        check_vma=False,
    )
```

```python
import functools

import jax
import jax.numpy as jnp
from jax import lax
from jax.experimental import pallas as pl
from jax.experimental.pallas import tpu as pltpu
from jax.sharding import PartitionSpec as P

neg_fill = -1000000000.0
open_cap = 3e38
eps_norm = 1e-05
PAIR = 128
HALF = 64
QUERY_SCALE = 0.125
ROOT = 0.7978845608028654
CUBE = 0.044715
f32 = jnp.float32
bf16 = jnp.bfloat16
ROW, FIRST, SECOND, TARGET, SOURCE, PLANE, CORE = range(7)


def low(value):
    return value.astype(bf16)


def nn(left, right):
    return lax.dot_general(left, right, (((1,), (0,)), ((), ())), preferred_element_type=f32)


def nt(left, right):
    return lax.dot_general(left, right, (((1,), (1,)), ((), ())), preferred_element_type=f32)


def tn(left, right):
    return lax.dot_general(left, right, (((0,), (0,)), ((), ())), preferred_element_type=f32)


def after(value, *others):
    return lax.optimization_barrier((value,) + others)[0]


def wall(*values):
    return lax.optimization_barrier(values)


def call(kernel, info, grid, ins, outs, scratch=(), micros=1.0):
    return pl.pallas_call(
        kernel,
        out_shape=tuple(jax.ShapeDtypeStruct(s, t) for s, t, _, _ in outs),
        grid_spec=pltpu.PrefetchScalarGridSpec(
            num_scalar_prefetch=1,
            grid=grid,
            in_specs=[pl.BlockSpec(b, m) for _, b, m in ins],
            out_specs=tuple(pl.BlockSpec(b, m) for _, _, b, m in outs),
            scratch_shapes=list(scratch),
        ),
        compiler_params=pltpu.CompilerParams(vmem_limit_bytes=52 << 20),
        cost_estimate=pl.CostEstimate(flops=int(micros * 1e7), bytes_accessed=1 << 10, transcendentals=0),
    )(info, *(a for a, _, _ in ins))


def rows_of_eight(values):
    return jnp.sum(values.reshape(values.shape[0] // 8, 8, values.shape[1]), axis=0)


def norm_stats(values):
    centre = jnp.mean(values, axis=-1, keepdims=True)
    offset = values - centre
    spread = jnp.mean(offset * offset, axis=-1, keepdims=True)
    scale = lax.rsqrt(spread + eps_norm)
    return offset * scale, scale


def norm_back(values, gain, grad):
    hat, scale = norm_stats(values)
    scaled = grad * gain
    mean_one = jnp.mean(scaled, axis=-1, keepdims=True)
    mean_two = jnp.mean(scaled * hat, axis=-1, keepdims=True)
    return scale * (scaled - mean_one - hat * mean_two), grad * hat


def head_halves(both):
    lane = lax.broadcasted_iota(jnp.int32, both.shape, 1)
    zero = jnp.zeros_like(both)
    return jnp.where(lane < HALF, both, zero), jnp.where(lane < HALF, zero, both)


def fill_caps(info, cap_ref, block, causal):
    length = cap_ref.shape[0]
    for t in range(2):
        keys = lax.broadcasted_iota(jnp.int32, (length, block), 0)
        allowed = keys < info[TARGET if causal else SOURCE]
        if causal:
            places = lax.broadcasted_iota(jnp.int32, (length, block), 1) + info[FIRST + t] * block
            allowed = allowed & (keys <= places)
        cap_ref[:, t * block : (t + 1) * block] = jnp.where(allowed, open_cap, neg_fill)


def forward_kernel(info, q_ref, k_ref, v_ref, o_ref, lse_ref, cap_ref, s_ref, *, block, causal, chunk):
    length = k_ref.shape[0]

    @pl.when(pl.program_id(0) == 0)
    def _():
        fill_caps(info, cap_ref, block, causal)

    for t in (1, 0):
        rows = slice(t * block, (t + 1) * block)
        span = length // 2 if (causal and t == 0) else length
        queries = jnp.concatenate(head_halves(q_ref[rows, :] * bf16(QUERY_SCALE)), axis=0)
        most = jnp.full((8, 2 * block), -open_cap, f32)
        for c in range(0, span, chunk):
            keys = slice(c, c + chunk)
            cap = cap_ref[keys, rows]
            scores = jnp.minimum(nt(k_ref[keys, :], queries), jnp.concatenate([cap, cap], axis=1))
            s_ref[t, keys, :] = scores
            most = jnp.maximum(most, jnp.max(scores.reshape(chunk // 8, 8, 2 * block), axis=0))
        most = jnp.max(most, axis=0, keepdims=True)
        total = jnp.zeros((8, 2 * block), f32)
        mixed = jnp.zeros((PAIR, 2 * block), f32)
        for c in range(0, span, chunk):
            keys = slice(c, c + chunk)
            weights = jnp.exp(s_ref[t, keys, :] - most)
            total = total + rows_of_eight(weights)
            mixed = mixed + tn(v_ref[keys, :], low(weights))
        total = jnp.sum(total, axis=0, keepdims=True)
        mixed = mixed / total
        sub = lax.broadcasted_iota(jnp.int32, (PAIR, block), 0)
        o_ref[rows, :] = low(jnp.where(sub < HALF, mixed[:, :block], mixed[:, block:]).T)
        lse = most + jnp.log(total)
        lse_ref[0, 0:1, rows] = lse[:, :block]
        lse_ref[0, 1:2, rows] = lse[:, block:]


def backward_kernel(
    info, q_ref, k_ref, v_ref, o_ref, g_ref, lse_ref, dq_ref, dk_ref, dv_ref, qs_ref, vs_ref, cap_ref, dk_acc, dv_acc,
    *, block, causal, chunk
):
    length = k_ref.shape[0]

    @pl.when(pl.program_id(0) == 0)
    def _():
        fill_caps(info, cap_ref, block, causal)

    q_sums = jnp.zeros((8, PAIR), f32)
    for t in (1, 0):
        rows = slice(t * block, (t + 1) * block)
        span = length // 2 if (causal and t == 0) else length
        grads = g_ref[rows, :]
        prod = (grads.astype(f32) * o_ref[rows, :].astype(f32)).T
        centre = jnp.concatenate(
            [jnp.sum(prod[:HALF], axis=0, keepdims=True), jnp.sum(prod[HALF:], axis=0, keepdims=True)], axis=1
        )
        lse = jnp.concatenate([lse_ref[0, 0:1, rows], lse_ref[0, 1:2, rows]], axis=1)
        queries = jnp.concatenate(head_halves(q_ref[rows, :] * bf16(QUERY_SCALE)), axis=0)
        grads = jnp.concatenate(head_halves(grads), axis=0)
        dq = jnp.zeros((PAIR, 2 * block), f32)
        for c in range(0, span, chunk):
            keys = slice(c, c + chunk)
            k, v = k_ref[keys, :], v_ref[keys, :]
            cap = cap_ref[keys, rows]
            scores = jnp.minimum(nt(k, queries), jnp.concatenate([cap, cap], axis=1))
            probs = jnp.exp(scores - lse)
            grad_scores = low(probs * (nt(v, grads) - centre))
            dv = nn(low(probs), grads)
            dk = nn(grad_scores, queries)
            dq = dq + tn(k, grad_scores)
            if t == 1:
                dk_acc[keys, :] = dk
                dv_acc[keys, :] = dv
            else:
                dk_acc[keys, :] += dk
                dv_acc[keys, :] += dv
        sub = lax.broadcasted_iota(jnp.int32, (PAIR, block), 0)
        dq = jnp.where(sub < HALF, dq[:, :block], dq[:, block:]) * QUERY_SCALE
        dq = low(dq.T)
        dq_ref[rows, :] = dq
        q_sums = q_sums + rows_of_eight(dq.astype(f32))
    dk_ref[...] = low(dk_acc[...])
    dv = low(dv_acc[...])
    dv_ref[...] = dv
    qs_ref[...] = q_sums
    vs_ref[...] = rows_of_eight(dv.astype(f32))


def attend_forward(info, query, keys, values, causal):
    queries, width = query.shape
    length = keys.shape[0]
    here = lambda i, _: (0, i)
    return call(
        functools.partial(forward_kernel, block=queries // 2, causal=causal, chunk=min(256, length // 2)),
        info,
        (width // PAIR,),
        [(query, (queries, PAIR), here), (keys, (length, PAIR), here), (values, (length, PAIR), here)],
        [
            ((queries, width), bf16, (queries, PAIR), here),
            ((width // PAIR, 8, queries), f32, (1, 8, queries), lambda i, _: (i, 0, 0)),
        ],
        [pltpu.VMEM((length, queries), f32), pltpu.VMEM((2, length, queries), f32)],
        micros=16,
    )


def attend_backward(info, query, keys, values, mixed, grad, lse_rows, causal):
    queries, width = query.shape
    length = keys.shape[0]
    here = lambda i, _: (0, i)
    one, key = (queries, PAIR), (length, PAIR)
    return call(
        functools.partial(backward_kernel, block=queries // 2, causal=causal, chunk=min(256, length // 2)),
        info,
        (width // PAIR,),
        [
            (query, one, here),
            (keys, key, here),
            (values, key, here),
            (mixed, one, here),
            (grad, one, here),
            (lse_rows, (1, 8, queries), lambda i, _: (i, 0, 0)),
        ],
        [
            ((queries, width), bf16, one, here),
            ((length, width), bf16, key, here),
            ((length, width), bf16, key, here),
            ((8, width), f32, (8, PAIR), here),
            ((8, width), f32, (8, PAIR), here),
        ],
        [pltpu.VMEM((length, queries), f32), pltpu.VMEM((length, PAIR), f32), pltpu.VMEM((length, PAIR), f32)],
        micros=24,
    )


def order_kernel(info, same_ref, other_ref, out_ref, *, part_of):
    mine = lax.rem(part_of(pl.program_id(0)), 2) == info[CORE]

    @pl.when(mine)
    def _():
        out_ref[...] = same_ref[...].astype(out_ref.dtype)

    @pl.when(jnp.logical_not(mine))
    def _():
        out_ref[...] = other_ref[...].astype(out_ref.dtype)


def order_rows(info, found, got, rows, group, pieces, kind):
    half, width = got.shape
    steps = group * pieces
    block = half // (rows * steps // 2)

    def part_of(i):
        b = lax.rem(i, steps)
        return jnp.where(b >= group, steps - 1 - b, b)

    def source(i):
        late = (lax.rem(i, steps) >= group).astype(jnp.int32)
        return (lax.div(i, steps) * (group // 2) + lax.div(part_of(i), 2)) * pieces + late

    return call(
        functools.partial(order_kernel, part_of=part_of),
        info,
        (rows * steps,),
        [
            (found, (block, width), lambda i, info: (source(i) + info[CORE] * (half // block), 0)),
            (got, (block, width), lambda i, _: (source(i), 0)),
        ],
        [((2 * half, width), kind, (block, width), lambda i, _: (i, 0))],
        micros=4,
    )[0]


def entry_kernel(info, x_ref, gain_ref, shift_ref, h_ref, *, which):
    hat, _ = norm_stats(x_ref[...].astype(f32))
    one = slice(which, which + 1)
    h_ref[...] = low(hat * gain_ref[one, :].astype(f32) + shift_ref[one, :].astype(f32))


def entry_norm(info, tokens, gains, shifts):
    _, length, width = tokens.shape
    tile = min(256, length)
    whole = lambda i, _: (0, 0)
    return call(
        functools.partial(entry_kernel, which=0),
        info,
        (length // tile,),
        [
            (tokens, (None, tile, width), lambda i, info: (info[ROW], i, 0)),
            (gains, gains.shape, whole),
            (shifts, shifts.shape, whole),
        ],
        [((length, width), bf16, (tile, width), lambda i, _: (i, 0))],
        micros=3,
    )[0]


def weight_ins(weight, slots):
    own, lead, rest, place = weight
    depth = rest.shape[0]
    wide = own.shape[1] * own.shape[2] // depth
    return [
        (own, (None,) + own.shape[1:], lambda *_: (lead, 0, 0)),
        (rest, (depth, (slots - 1) * wide), lambda *_: (0, place)),
    ]


def project_kernel(info, x_ref, own_ref, rest_ref, *others, flipped):
    x = x_ref[...]
    mine = nt(x, own_ref[...]) if flipped else nn(x, own_ref[...])
    wide = mine.shape[1]
    rest = nn(x, rest_ref[...])
    out_ref = others[-1]
    if len(others) > 1:
        mine = mine + others[0][:, :wide]
        rest = rest + others[0][:, wide:]
    out_ref[:, :wide] = low(mine)
    out_ref[:, wide:] = low(rest)


def project(info, x, place_of, tiles, weight, bias, slots, flipped=False):
    count, tile = tiles
    depth = x.shape[2]
    ins = [(x, (None, tile, depth), lambda i, info: place_of(i, info) + (0,))] + weight_ins(weight, slots)
    own = weight[0]
    width = slots * (own.shape[1] * own.shape[2] // depth)
    if bias is not None:
        ins.append((bias, bias.shape, lambda i, _: (0, 0)))
    return call(
        functools.partial(project_kernel, flipped=flipped),
        info,
        (count,),
        ins,
        [((count * tile, width), bf16, (tile, width), lambda i, _: (i, 0))],
        micros=2.5 * count * tile / 1024,
    )[0]


def mix_kernel(info, x_ref, own_ref, rest_ref, resid_ref, bias_ref, gain_ref, shift_ref, sum_ref, h_ref, *, which):
    wide = own_ref.shape[0]
    found = nn(x_ref[:, :wide], own_ref[...]) + nt(x_ref[:, wide:], rest_ref[...])
    found = resid_ref[...].astype(f32) + found + bias_ref[which : which + 1, :].astype(f32)
    sum_ref[...] = found
    hat, _ = norm_stats(found)
    one = slice(which + 1, which + 2)
    h_ref[...] = low(hat * gain_ref[one, :].astype(f32) + shift_ref[one, :].astype(f32))


def mix(info, x, weight, resid, resid_place, biases, gains, shifts, which, slots):
    rows, width = x.shape
    block = rows // 2
    whole = lambda i, _: (0, 0)
    here = lambda i, _: (i, 0)
    depth = resid.shape[2]
    return call(
        functools.partial(mix_kernel, which=which),
        info,
        (2,),
        [(x, (block, width), here)]
        + weight_ins(weight, slots)
        + [
            (resid, (None, block, depth), lambda i, info: resid_place(i, info) + (0,)),
            (biases, biases.shape, whole),
            (gains, gains.shape, whole),
            (shifts, shifts.shape, whole),
        ],
        [((rows, depth), f32, (block, depth), here), ((rows, depth), bf16, (block, depth), here)],
        micros=4,
    )


def back_dots(pairs):
    total = None
    for x_ref, own_ref, rest_ref in pairs:
        wide = own_ref.shape[1]
        found = nt(x_ref[:, :wide], own_ref[...]) + nt(x_ref[:, wide:], rest_ref[...])
        total = found if total is None else total + found
    return total


def back_kernel(info, *refs, count):
    pairs = [refs[3 * j : 3 * j + 3] for j in range(count)]
    refs[-1][...] = low(back_dots(pairs))


def back(info, terms, slots):
    rows, width = terms[0][0].shape
    depth = terms[0][1][2].shape[0]
    tile = min(256, rows)
    ins = []
    for x, weight in terms:
        ins += [(x, (tile, width), lambda i, _: (i, 0))] + weight_ins(weight, slots)
    return call(
        functools.partial(back_kernel, count=len(terms)),
        info,
        (rows // tile,),
        ins,
        [((rows, depth), bf16, (tile, depth), lambda i, _: (i, 0))],
        micros=5,
    )[0]


def back_norm_kernel(info, *refs, extras, which, keep):
    x_ref, own_ref, rest_ref = refs[:3]
    extra = refs[3 : 3 + extras]
    v_ref, add_ref, gain_ref = refs[3 + extras : 6 + extras]
    outs = refs[6 + extras :]
    grad = back_dots([(x_ref, own_ref, rest_ref)])
    for e in extra:
        grad = grad + e[...].astype(f32)
    found, to_gain = norm_back(v_ref[...].astype(f32), gain_ref[which : which + 1, :].astype(f32), grad)
    found = add_ref[...] + found
    low_found = low(found)
    if keep:
        outs[0][...] = found
    outs[-2][...] = low_found
    sums = jnp.concatenate([rows_of_eight(to_gain), rows_of_eight(grad), rows_of_eight(low_found.astype(f32))])

    @pl.when(pl.program_id(0) == 0)
    def _():
        outs[-1][...] = sums

    @pl.when(pl.program_id(0) > 0)
    def _():
        outs[-1][...] += sums


def back_norm(info, x, weight, extras, values, values_place, add, gains, which, slots, keep):
    rows, width = x.shape
    block = rows // 2
    depth = add.shape[1]
    here = lambda i, _: (i, 0)
    whole = lambda i, _: (0, 0)
    one = (block, depth)
    outs = [((rows, depth), bf16, one, here), ((24, depth), f32, (24, depth), whole)]
    if keep:
        outs = [((rows, depth), f32, one, here)] + outs
    return call(
        functools.partial(back_norm_kernel, extras=len(extras), which=which, keep=keep),
        info,
        (2,),
        [(x, (block, width), here)]
        + weight_ins(weight, slots)
        + [(e, one, here) for e in extras]
        + [
            (values, (None, block, depth), lambda i, info: values_place(i, info) + (0,)),
            (add, one, here),
            (gains, gains.shape, whole),
        ],
        outs,
        micros=4,
    )


def feed_kernel(
    info, h_ref, c0_ref, c1_ref, second_ref, upo_ref, downo_ref, upr_ref, downr_ref, ub_ref, bias_ref, gain_ref,
    a_ref, du_ref, us_ref, final_ref, g_ref, e_ref, sums_ref, out_acc, dh_acc, *, own_tiles
):
    i = pl.program_id(0)
    block = c0_ref.shape[0]
    cots = (c0_ref, c1_ref)
    which = 2

    def tile(own):
        sums = None
        for t in range(2):
            rows = slice(t * block, (t + 1) * block)
            up = upo_ref[...] if own else upr_ref[...]
            pre = nn(h_ref[rows, :], up) + ub_ref[...]
            square = pre * pre
            curve = jnp.tanh(ROOT * (pre + CUBE * square * pre))
            act = low(0.5 * pre * (1.0 + curve))
            slope = 0.5 * (1.0 + curve) + 0.5 * pre * (1.0 - curve * curve) * (ROOT * (1.0 + 3.0 * CUBE * square))
            a_ref[rows, :] = act
            if own:
                grad = nt(cots[t][...], downo_ref[...])
                out = nn(act, downo_ref[...])
            else:
                grad = nn(cots[t][...], downr_ref[...])
                out = nt(act, downr_ref[...])
            du = low(slope * grad)
            du_ref[rows, :] = du
            part = rows_of_eight(du.astype(f32))
            sums = part if sums is None else sums + part
            dh = nt(du, up)
            first = i == 0
            if own:

                @pl.when(first)
                def _():
                    out_acc[rows, :] = out
                    dh_acc[rows, :] = dh

                @pl.when(jnp.logical_not(first))
                def _():
                    out_acc[rows, :] += out
                    dh_acc[rows, :] += dh
            else:
                out_acc[rows, :] += out
                dh_acc[rows, :] += dh
        us_ref[...] = sums

    @pl.when(i < own_tiles)
    def _():
        tile(True)

    @pl.when(i >= own_tiles)
    def _():
        tile(False)

    @pl.when(i == pl.num_programs(0) - 1)
    def _():
        sums = None
        gain = gain_ref[which : which + 1, :].astype(f32)
        for t in range(2):
            rows = slice(t * block, (t + 1) * block)
            second = second_ref[rows, :]
            final_ref[rows, :] = low(second + out_acc[rows, :] + bias_ref[which : which + 1, :].astype(f32))
            cot = cots[t][...].astype(f32)
            grad = dh_acc[rows, :]
            found, to_gain = norm_back(second, gain, grad)
            found = cot + found
            g_ref[rows, :] = found
            rounded = low(found)
            e_ref[rows, :] = rounded
            part = jnp.concatenate(
                [
                    rows_of_eight(to_gain),
                    rows_of_eight(grad),
                    rows_of_eight(rounded.astype(f32)),
                    rows_of_eight(cot),
                ]
            )
            sums = part if sums is None else sums + part
        sums_ref[...] = sums


def feed_forward(info, h, cotangent, second, up, down, up_bias, biases, gains, slots):
    rows, depth = h.shape
    block = rows // 2
    up_own, _, up_rest, up_place = up
    down_own, _, down_rest, down_place = down
    hidden = up_own.shape[2]
    tile = min(512, hidden)
    own_tiles = hidden // tile
    total = slots * own_tiles
    rest_tiles = (slots - 1) * own_tiles
    own_at = lambda i: jnp.minimum(i, own_tiles - 1)
    rest_at = lambda i: jnp.maximum(i - own_tiles, 0)
    whole = lambda i, _: (0, 0)
    full = (rows, depth)
    return call(
        functools.partial(feed_kernel, own_tiles=own_tiles),
        info,
        (total,),
        [
            (h, full, whole),
            (cotangent, (None, block, depth), lambda i, _: (0, 0, 0)),
            (cotangent, (None, block, depth), lambda i, _: (0, 1, 0)),
            (second, full, whole),
            (up_own, (None, depth, tile), lambda i, _: (0, 0, own_at(i))),
            (down_own, (None, tile, depth), lambda i, _: (0, own_at(i), 0)),
            (up_rest, (depth, tile), lambda i, _: (0, up_place * rest_tiles + rest_at(i))),
            (down_rest, (depth, tile), lambda i, _: (0, down_place * rest_tiles + rest_at(i))),
            (up_bias, (1, tile), lambda i, _: (0, i)),
            (biases, biases.shape, whole),
            (gains, gains.shape, whole),
        ],
        [
            ((rows, total * tile), bf16, (rows, tile), lambda i, _: (0, i)),
            ((rows, total * tile), bf16, (rows, tile), lambda i, _: (0, i)),
            ((8, total * tile), f32, (8, tile), lambda i, _: (0, i)),
            (full, bf16, full, whole),
            (full, f32, full, whole),
            (full, bf16, full, whole),
            ((32, depth), f32, (32, depth), whole),
        ],
        [pltpu.VMEM(full, f32), pltpu.VMEM(full, f32)],
        micros=32,
    )


def grad_kernel(info, *refs, plan, share, plane, mine):
    acts = refs[: sum(len(pieces) for pieces, _ in plan)]
    refs = refs[len(acts) :]
    grads = refs[: len(plan)]
    refs = refs[len(plan) :]
    got_ref = None
    if mine:
        got_ref, refs = refs[0], refs[1:]
    outs, turned = refs[: plane if mine else 1], refs[-len(plan) :]
    core = info[CORE] if mine else 1 - info[CORE]

    @pl.when(pl.program_id(0) == 0)
    def _():
        at = 0
        for t, (pieces, _) in enumerate(plan):
            start = 0
            for length in pieces:
                for r in range(plane):
                    if share % PAIR == 0:
                        block = 2 * jnp.bitwise_xor(info[PLANE], r) + core
                        cols = acts[at][:, pl.ds(pl.multiple_of(block * share, share), share)]
                    else:
                        cols = acts[at][:, r * share : (r + 1) * share]
                    turned[t][r * share : (r + 1) * share, start : start + length] = cols.T
                start += length
                at += 1

    first = 0
    for t, (_, wide) in enumerate(plan):
        cols = slice(first, first + wide)
        found = nn(turned[t][...], grads[t][...])
        if mine:
            found = low(found + got_ref[:, cols].astype(f32))
            for r in range(plane):
                outs[r][:, cols] = found[r * share : (r + 1) * share, :]
        else:
            outs[0][:, cols] = low(found)
        first += wide


def weight_grads(info, tensors, d, dp_size, slots, got=None):
    depth = tensors[0][0][0][0].shape[2]
    share, plane = depth // dp_size, dp_size // 2
    core = lax.rem(d, 2) if got is not None else 1 - lax.rem(d, 2)
    plan = [(tuple(rows for _, rows, _ in pieces), grad.shape[1] // slots) for pieces, grad in tensors]
    ins = []
    for pieces, _ in tensors:
        for array, rows, place in pieces:
            if share % PAIR == 0:
                ins.append((array, (None, rows, depth), lambda i, info, place=place: place(info) + (0,)))
            else:
                wide = array.reshape(array.shape[:2] + (plane, 2, share))
                wide = lax.dynamic_index_in_dim(wide, core, 3, keepdims=False)
                order = [jnp.bitwise_xor(d // 2, r) for r in range(plane)]
                wide = jnp.concatenate([lax.dynamic_index_in_dim(wide, b, 2) for b in order], axis=2)
                wide = wide.reshape(array.shape[:2] + (depth // 2,))
                ins.append((wide, (None, rows, depth // 2), lambda i, info, place=place: place(info) + (0,)))
    for (_, grad), (_, wide) in zip(tensors, plan):
        ins.append((grad, (grad.shape[0], wide), lambda i, _: (0, i)))
    half = depth // 2
    tile = sum(wide for _, wide in plan)
    if got is not None:
        ins.append((got, (half, tile), lambda i, _: (0, i)))
        outs = [((share, slots * tile), bf16, (share, tile), lambda i, _: (0, i))] * plane
    else:
        outs = [((half, slots * tile), bf16, (half, tile), lambda i, _: (0, i))]
    return call(
        functools.partial(grad_kernel, plan=plan, share=share, plane=plane, mine=got is not None),
        info,
        (slots,),
        ins,
        outs,
        [pltpu.VMEM((half, g.shape[0]), bf16) for _, g in tensors],
        micros=8,
    )


def finish_kernel(info, in_ref, out_ref, *, turn):
    value = in_ref[...].astype(f32)
    out_ref[...] = value.T if turn else value


def finish(info, full, places, wide, turn=False):
    depth = full.shape[0]
    first = places[0]
    if turn:
        tile, cut = min(256, depth), min(512, wide)
        return call(
            functools.partial(finish_kernel, turn=True),
            info,
            (depth // tile, wide // cut),
            [(full, (tile, cut), lambda i, j, _: (i, first * (wide // cut) + j))],
            [((wide, depth), f32, (cut, tile), lambda i, j, _: (j, i))],
            micros=3,
        )[0]
    tile = min(512, depth)
    return call(
        functools.partial(finish_kernel, turn=False),
        info,
        (len(places), depth // tile),
        [(full, (tile, wide), lambda i, j, _: (j, first + i))],
        [((len(places), depth, wide), f32, (None, tile, wide), lambda i, j, _: (i, j, 0))],
        micros=3,
    )[0]


def finish_pair_kernel(info, in_ref, q_ref, kv_ref, o_ref, s_ref, so_ref):
    wide = q_ref.shape[1]

    def cols(t):
        return in_ref[:, t * wide : (t + 1) * wide].astype(f32)

    q_ref[...] = cols(0)
    for t in range(2):
        kv_ref[t] = cols(1 + t)
    o_ref[...] = cols(3).T
    for t in range(3):
        s_ref[t] = cols(4 + t)
    so_ref[...] = cols(7).T


def finish_pair(info, full):
    depth = full.shape[0]
    wide = full.shape[1] // 8
    tile = min(256, depth)
    return call(
        finish_pair_kernel,
        info,
        (depth // tile,),
        [(full, (tile, 8 * wide), lambda i, _: (i, 0))],
        [
            ((depth, wide), f32, (tile, wide), lambda i, _: (i, 0)),
            ((2, depth, wide), f32, (2, tile, wide), lambda i, _: (0, i, 0)),
            ((wide, depth), f32, (wide, tile), lambda i, _: (0, i)),
            ((3, depth, wide), f32, (3, tile, wide), lambda i, _: (0, i, 0)),
            ((wide, depth), f32, (wide, tile), lambda i, _: (0, i)),
        ],
        micros=4,
    )


def build(dp_size, mp_size):
    ring = [(i, (i + 1) % mp_size) for i in range(mp_size)]
    back_ring = [(i, (i - 1) % mp_size) for i in range(mp_size)]
    dp_bits = dp_size.bit_length() - 1
    plane = dp_size // 2

    def flip(axis, size, bits):
        return lambda value: lax.ppermute(value, axis, [(i, i ^ bits) for i in range(size)])

    def shards(
        tokens,
        memory,
        target_lengths,
        source_lengths,
        cotangent,
        norm_gain,
        norm_bias,
        self_in,
        self_in_bias,
        self_out,
        cross_query,
        cross_kv,
        cross_bias,
        cross_out,
        out_bias,
        ffn_up,
        ffn_up_bias,
        ffn_down,
    ):
        rows, length, width = tokens.shape
        source = memory.shape[1]
        d = lax.axis_index("dp")
        z = lax.axis_index("mp")
        group = mp_size // rows
        core = lax.rem(d, 2)
        chips = group // 2
        chip_row = z // chips
        part = (z % chips) * 2 + core
        held = chip_row // rows == core
        row = lax.rem(chip_row, rows)
        block = length // (2 * group)
        share = width // dp_size
        per = width // mp_size
        hid = ffn_up.shape[1]
        swap = flip("dp", dp_size, 1)

        def take_row(values):
            return lax.dynamic_index_in_dim(values, row, 0, keepdims=False)

        def blocks_of(values, p):
            return jnp.concatenate(
                [
                    lax.dynamic_slice_in_dim(values, s * block, block, 0)
                    for s in (p, 2 * group - 1 - p)
                ]
            )

        own_place = lambda i, info: (info[ROW], info[FIRST + i])
        own_h_place = lambda i, info: (0, info[FIRST + i])
        flat_place = lambda i, info: (0, i)
        row_place = lambda i, info: (info[ROW], i)

        def rows_of(weight):
            return lax.dynamic_slice_in_dim(weight, d * share, share, 0)

        def cols_of(weight):
            return lax.dynamic_slice_in_dim(weight, d * share, share, 1).T

        def with_bias(piece, bias):
            extra = jnp.zeros((16, piece.shape[1]), bf16)
            if bias is not None:
                extra = lax.dynamic_update_slice(extra, bias[None], (0, 0))
            return jnp.concatenate([piece, extra])

        def side_by_side(pieces):
            return jnp.concatenate([with_bias(p, b) for p, b in pieces], axis=1)

        def pass_on(value):
            return lax.ppermute(value, "mp", ring)

        def gather_rest(found, wides, *held):
            starts = [0]
            for w in wides:
                starts.append(starts[-1] + w)
            both = jnp.concatenate([s[:, a:b] for a, b in zip(starts[:-1], starts[1:]) for s in found], axis=1)
            ours = both[:share]
            if held:
                ours = after(ours, *held)
            return lax.all_gather(ours, "dp", axis=0, tiled=True), both[share : share + 1].astype(f32)

        def bias_of(own, biases, t, wide):
            far = (mp_size - 1) * wide
            return jnp.concatenate([own.astype(f32)[None], biases[:, t * far : (t + 1) * far]], axis=1)

        def row_of(mine, theirs, cut=lambda values: values):
            return jnp.where(held, cut(take_row(mine)), cut(take_row(theirs)))[None]

        lengths = jnp.stack([target_lengths, source_lengths])
        lengths = jnp.where(held, lengths, swap(lengths))
        lengths = lax.dynamic_index_in_dim(lengths, row, 1, keepdims=False)
        info = jnp.stack(
            [0 * part, part, 2 * group - 1 - part, lengths[0], lengths[1], d // 2, core]
        ).astype(jnp.int32)
        found_a = [
            pass_on(
                side_by_side(
                    [
                        (rows_of(self_in[0]), self_in_bias[0]),
                        (rows_of(self_in[1]), None),
                        (rows_of(self_in[2]), self_in_bias[1]),
                    ]
                )
            )
        ]
        for _ in range(mp_size - 3):
            found_a.append(pass_on(found_a[-1]))
        found_a[-1], tokens_got, info = wall(found_a[-1], swap(tokens), info)
        found_a.append(pass_on(found_a[-1]))
        share_b = side_by_side(
            [
                (cols_of(self_out), None),
                (rows_of(cross_query), cross_bias[0]),
                (rows_of(cross_kv[0]), None),
                (rows_of(cross_kv[1]), cross_bias[1]),
                (cols_of(cross_out), None),
            ]
        )
        share_c = side_by_side(
            [(rows_of(ffn_up), ffn_up_bias), (cols_of(ffn_down), None)]
        )
        found_a[-1], tokens_got, share_b, share_c = wall(found_a[-1], tokens_got, share_b, share_c)
        found_b = [pass_on(share_b)]
        tokens_row = row_of(tokens, tokens_got)
        h1_row = entry_norm(info, tokens_row, norm_gain, norm_bias)
        found_b[0], h1_row = wall(found_b[0], h1_row)
        for _ in range(mp_size - 3):
            found_b.append(pass_on(found_b[-1]))
        found_b[-1], memory_got = wall(found_b[-1], swap(memory))
        found_b.append(pass_on(found_b[-1]))
        memory_row = row_of(memory, memory_got)
        found_b[-1], memory_row = wall(found_b[-1], memory_row)
        rest_a, bias_a = gather_rest(found_a, [per] * 3)
        rest_b, bias_b = gather_rest(found_b, [per] * 5)
        w_q1, w_k1, w_v1 = [(self_in, t, rest_a, t) for t in range(3)]
        w_o1 = (self_out[None], 0, rest_b, 0)
        w_q2 = (cross_query[None], 0, rest_b, 1)
        w_k2, w_v2 = (cross_kv, 0, rest_b, 2), (cross_kv, 1, rest_b, 3)
        w_o2 = (cross_out[None], 0, rest_b, 4)

        found_c = [pass_on(after(share_c, found_b[-1]))]
        for _ in range(mp_size - 3):
            found_c.append(pass_on(found_c[-1]))
        far = min(256, length)
        h1_flat = h1_row[None]
        k1 = project(info, h1_flat, flat_place, (length // far, far), w_k1, None, mp_size)
        found_c[-1], k1, h1_flat = wall(found_c[-1], k1, h1_flat)
        found_c.append(pass_on(found_c[-1]))
        v1 = project(
            info, h1_flat, flat_place, (length // far, far), w_v1, bias_of(self_in_bias[1], bias_a, 2, per), mp_size
        )
        q1 = project(info, h1_flat, own_h_place, (2, block), w_q1, bias_of(self_in_bias[0], bias_a, 0, per), mp_size)
        cot_own = row_of(cotangent, swap(cotangent), lambda values: blocks_of(values, part))
        found_c[-1], v1, q1 = wall(found_c[-1], v1, q1)
        rest_c, bias_c = gather_rest(found_c, [hid, hid])
        w_up, w_down = (ffn_up[None], 0, rest_c, 0), (ffn_down[None], 0, rest_c, 1)
        o1, lse1 = attend_forward(info, q1, k1, v1, True)
        first, h2 = mix(info, o1, w_o1, tokens_row, own_place, out_bias, norm_gain, norm_bias, 0, mp_size)
        q2 = project(info, h2[None], flat_place, (2, block), w_q2, bias_of(cross_bias[0], bias_b, 1, per), mp_size)
        k2 = project(info, memory_row, row_place, (source // far, far), w_k2, None, mp_size)
        v2 = project(
            info, memory_row, row_place, (source // far, far), w_v2, bias_of(cross_bias[1], bias_b, 3, per), mp_size
        )
        o2, lse2 = attend_forward(info, q2, k2, v2, False)
        second, h3 = mix(info, o2, w_o2, first[None], flat_place, out_bias, norm_gain, norm_bias, 1, mp_size)
        hidden, grad_pre, up_sums, final, g2, e2, sums_three = feed_forward(
            info, h3, cot_own, second, w_up, w_down, bias_of(ffn_up_bias, bias_c, 0, hid), out_bias, norm_gain, mp_size
        )

        def to_plane(piece, r):
            return flip("dp", dp_size, 2 * r)(piece)

        def slots_of(total, count=mp_size):
            wide = total[0].shape[1] // count
            slots = []
            for k in range(count):
                cols = slice(k * wide, (k + 1) * wide)
                slots.append(low(sum(t[:, cols].astype(f32) for t in total)))
            return slots

        def to_owners(slots):
            return [
                lax.ppermute(slots[k], "mp", [(i, (i - k) % mp_size) for i in range(mp_size)])
                for k in range(1, mp_size)
            ]

        def add_up(values):
            return low(sum(v.astype(f32) for v in values))

        def gather_grads(total):
            return lax.all_gather(total, "dp", axis=0, tiled=True)

        def gather_rows(mine):
            return lax.all_gather(mine, "mp", axis=0, tiled=True)

        def for_other(found):
            half = found.shape[0] // 2
            return swap(lax.dynamic_slice_in_dim(found, (1 - core) * half, half, 0))

        def own_blocks(array, lead):
            return [
                (array, block, lambda info, t=t: ((info[ROW] if lead else 0), info[FIRST + t])) for t in range(2)
            ]

        def all_rows(array, lead=False):
            return [(array, array.shape[1], lambda info: ((info[ROW] if lead else 0), 0))]

        def core_send(tensors):
            return weight_grads(info, tensors, d, dp_size, mp_size)[0]

        def to_core(sent):
            return flip("dp", dp_size, 1)(sent)

        def core_keep(tensors, got):
            return weight_grads(info, tensors, d, dp_size, mp_size, got)

        row_perm = [(i, (i // chips) * chips + (i % chips - 1) % chips) for i in range(mp_size)]

        def row_sum(piece_of):
            got = [swap(piece_of(2 * c + 1 - core)) for c in range(chips)]
            if chips == 1:
                return got[0], piece_of(part)
            pieces = jnp.stack([add_up([got[c], piece_of(2 * c + core)]) for c in range(chips)])
            place = z % chips
            total = lax.dynamic_index_in_dim(pieces, lax.rem(place + 1, chips), 0, keepdims=False)
            for k in range(chips - 2, -1, -1):
                total = lax.ppermute(total, "mp", row_perm)
                here = lax.dynamic_index_in_dim(pieces, lax.rem(place - k + chips, chips), 0, keepdims=False)
                if k:
                    total = add_up([total, here])
            return total, here

        def all_planes(kept):
            return [kept[0]] + [to_plane(kept[r], r) for r in range(1, plane)]

        output_found = gather_rows(final)
        ffn_tensors = [(all_rows(h3[None]), grad_pre), (all_rows(cot_own), hidden)]
        ffn_sent = core_send(ffn_tensors)
        e2, ffn_sent = wall(e2, ffn_sent)

        ffn_got = to_core(ffn_sent)
        do2 = project(info, e2[None], flat_place, (2, block), w_o2, None, mp_size, flipped=True)
        dq2, dk2, dv2, sum_q2, sum_v2 = attend_backward(info, q2, k2, v2, o2, do2, lse2, False)
        memory_part = back(info, [(dk2, w_k2), (dv2, w_v2)], mp_size)

        def memory_piece(p):
            return lax.dynamic_slice_in_dim(memory_part, p * (source // group), source // group, 0)

        ffn_got, memory_part, dq2 = wall(ffn_got, memory_part, dq2)
        memory_got, memory_here = row_sum(memory_piece)
        ffn_kept = core_keep(ffn_tensors, ffn_got)
        memory_got, dq2, *ffn_kept = wall(memory_got, dq2, *ffn_kept)
        memory_own = add_up([memory_got, memory_here])
        memory_found = gather_rows(memory_own)
        memory_own, dq2 = wall(memory_own, dq2)

        late = plane - 1
        ffn_total = [ffn_kept[0]] + [to_plane(ffn_kept[r], r) for r in range(1, late)]
        g1, e1, sums_two = back_norm(
            info, dq2, w_q2, [], first[None], flat_place, g2, norm_gain, 1, mp_size, True
        )
        cross_tensors = [
            (all_rows(h2[None]), dq2),
            (all_rows(memory_row), dk2),
            (all_rows(memory_row), dv2),
            (all_rows(e2[None]), o2),
        ]
        cross_sent = core_send(cross_tensors)
        cross_got = to_core(cross_sent)
        e1 = after(e1, cross_sent)
        do1 = project(info, e1[None], flat_place, (2, block), w_o1, None, mp_size, flipped=True)
        dq1, dk1, dv1, sum_q1, sum_v1 = attend_backward(info, q1, k1, v1, o1, do1, lse1, True)
        kv_part = back(info, [(dk1, w_k1), (dv1, w_v1)], mp_size)
        wide = ffn_kept[late].shape[1] // 2
        last_one, last_two = ffn_kept[late][:, :wide], ffn_kept[late][:, wide:]
        kv_part, cross_got, last_one, last_two, *ffn_total = wall(kv_part, cross_got, last_one, last_two, *ffn_total)

        def causal_piece(p):
            return blocks_of(kv_part, p)

        last_two = to_plane(last_two, late)
        got, here = row_sum(causal_piece)
        cross_kept = core_keep(cross_tensors, cross_got)
        self_tensors = [
            (own_blocks(h1_flat, False), dq1),
            (all_rows(h1_flat), dk1),
            (all_rows(h1_flat), dv1),
            (all_rows(e1[None]), o1),
        ]
        self_sent = core_send(self_tensors)
        output_got = for_other(output_found)
        got, self_sent, output_got, last_one, last_two, *cross_kept = wall(
            got, self_sent, output_got, last_one, last_two, *cross_kept
        )
        last_one = to_plane(last_one, late)
        cross_total = all_planes(cross_kept)
        self_got = to_core(self_sent)
        tokens_own, sums_one = back_norm(
            info, dq1, w_q1, [got, here], tokens_row, own_place, g1, norm_gain, 0, mp_size, False
        )
        tokens_found = gather_rows(tokens_own)

        def by_slot(sums):
            return jnp.sum(sums, axis=0).reshape(mp_size, -1)

        slot_sums = jnp.concatenate([by_slot(s) for s in (sum_q1, sum_v1, sum_q2, sum_v2, up_sums)], axis=1)
        flipped = slot_sums[::-1]
        twice = jnp.concatenate([flipped, flipped])
        in_order = lax.dynamic_slice_in_dim(twice, mp_size - 1 - z, mp_size, 0)
        whole = [
            jnp.sum(sums.reshape(-1, 8, width), axis=1) for sums in (sums_one, sums_two, sums_three)
        ]
        whole = jnp.concatenate(
            [w[0:1] for w in whole] + [w[1:2] for w in whole] + [whole[1][2:3], whole[2][2:3], whole[2][3:4]]
        )
        small = jnp.concatenate([in_order.reshape(-1, PAIR), whole.reshape(-1, PAIR)])
        small_steps = [("dp", dp_size, 1 << b) for b in range(dp_bits)]
        small_steps += [("mp", mp_size, 1 << b) for b in range(mp_size.bit_length() - 1)]

        self_got, tokens_own = wall(self_got, tokens_own)
        self_kept = core_keep(self_tensors, self_got)
        last_one, *self_kept = wall(last_one, *self_kept)
        self_total = all_planes(self_kept)
        ffn_slots = slots_of([t[:, :wide] for t in ffn_total] + [last_one], mp_size // 2)
        ffn_slots += slots_of([t[:, wide:] for t in ffn_total] + [last_two], mp_size // 2)
        output = order_rows(info, output_found, output_got, rows, group, 2, bf16).reshape(tokens.shape)
        output, small, *ffn_slots = wall(output, small, *ffn_slots)

        def ring_start(slots):
            return lax.ppermute(slots[mp_size - 1], "mp", back_ring)

        def ring_next(slots, k, state):
            return lax.ppermute(add_up([slots[k], state]), "mp", back_ring)

        ffn_state = ring_start(ffn_slots)
        memory_got = for_other(memory_found)
        memory_got, small, ffn_state, *cross_total = wall(memory_got, small, ffn_state, *cross_total)
        for k in range(mp_size - 2, 0, -1):
            ffn_state = ring_next(ffn_slots, k, ffn_state)
        cross_slots = slots_of(cross_total)
        cross_state = ring_start(cross_slots)
        memory_grad = order_rows(info, memory_found, memory_got, rows, group, 1, f32).reshape(memory.shape)
        memory_grad, small, ffn_state, cross_state = wall(memory_grad, small, ffn_state, cross_state)
        for k in range(mp_size - 2, 1, -1):
            cross_state = ring_next(cross_slots, k, cross_state)
        ffn_state, small, cross_state, *self_total = wall(ffn_state, small, cross_state, *self_total)
        ffn_full = gather_grads(add_up([ffn_slots[0], ffn_state]))
        cross_state = ring_next(cross_slots, 1, cross_state)
        self_slots = slots_of(self_total)
        self_total = [self_slots[0]] + to_owners(self_slots)
        tokens_got = for_other(tokens_found)
        tokens_grad = order_rows(info, tokens_found, tokens_got, rows, group, 2, f32).reshape(tokens.shape)
        tokens_grad, small, cross_state, *self_total = wall(tokens_grad, small, cross_state, *self_total)
        for step in small_steps:
            small = small + flip(*step)(small)
        joint = jnp.concatenate([add_up([cross_slots[0], cross_state]), add_up(self_total)], axis=1)
        joint_full = gather_grads(joint)
        up_grad, down_grad = finish(info, ffn_full, [0], hid)[0], finish(info, ffn_full, [1], hid, True)
        small = small.reshape(-1)
        slot_part = small[: in_order.size].reshape(in_order.shape)
        mine = lax.dynamic_index_in_dim(slot_part, z, 0, keepdims=False)
        whole = small[in_order.size :].reshape(9, width)
        cross_q, cross_both, cross_o, self_three, self_o = finish_pair(after(info, up_grad, down_grad), joint_full)
        return (
            output,
            tokens_grad,
            memory_grad,
            whole[0:3],
            whole[3:6],
            self_three,
            jnp.stack([mine[:per], mine[per : 2 * per]]),
            self_o,
            cross_q,
            cross_both,
            jnp.stack([mine[2 * per : 3 * per], mine[3 * per : 4 * per]]),
            cross_o,
            whole[6:9],
            up_grad,
            mine[4 * per :],
            down_grad,
        )

    return shards


def solution(mesh):
    placed = (
        P("dp", None, None),
        P("dp", None, None),
        P("dp"),
        P("dp"),
        P("dp", None, None),
        P(),
        P(),
        P(None, None, "mp"),
        P(None, "mp"),
        P("mp", None),
        P(None, "mp"),
        P(None, None, "mp"),
        P(None, "mp"),
        P("mp", None),
        P(),
        P(None, "mp"),
        P("mp"),
        P("mp", None),
    )
    return jax.shard_map(
        build(mesh.shape["dp"], mesh.shape["mp"]),
        mesh=mesh,
        in_specs=placed,
        out_specs=(
            P("dp", None, None),
            P("dp", None, None),
            P("dp", None, None),
            P(),
            P(),
            P(None, None, "mp"),
            P(None, "mp"),
            P("mp", None),
            P(None, "mp"),
            P(None, None, "mp"),
            P(None, "mp"),
            P("mp", None),
            P(),
            P(None, "mp"),
            P("mp"),
            P("mp", None),
        ),
        check_vma=False,
    )
```
